32 devices in a mesh: dp: 8 (over y, x, core), section: 4 (over z).
Axes of the slice: x: 2, y: 2, z: 4, core: 2. Of those that a mesh axis runs over, the one named last changes fastest.
Arguments:
- features: bfloat16 [8192, 1024], P('dp'), may hold values from -6 to 6
- cotangent: bfloat16 [8192, 1024], P('dp'), may hold values from -8 to 8
- row_counts: int32 [8, 8], P('dp'), may hold values from 1 to 512, 1024 in all within a row
- key_valid: int32 [8192], P('dp'), may hold values 0 or 1
- attend_gain: float32 [1024], replicated, may hold values from 0.25 to 1.75
- attend_qkv: bfloat16 [1024, 3072], replicated, may hold values from -0.1875 to 0.1875
- attend_out: bfloat16 [1024, 1024], replicated, may hold values from -1.5 to 1.5
- mixer_gain: float32 [1024], replicated, may hold values from 0.25 to 1.75
- mixer_up: bfloat16 [1024, 4096], replicated, may hold values from -0.1875 to 0.1875
- mixer_down: bfloat16 [4096, 1024], replicated, may hold values from -0.09375 to 0.09375
- column_gain: float32 [64], replicated, may hold values from 0.25 to 1.75
- column_qkv: bfloat16 [64, 192], replicated, may hold values from -0.75 to 0.75
- column_out: bfloat16 [64, 64], replicated, may hold values from -2 to 2
- column_mix_gain: float32 [64], replicated, may hold values from 0.25 to 1.75
- column_up: bfloat16 [64, 256], replicated, may hold values from -0.75 to 0.75
- column_down: bfloat16 [256, 64], replicated, may hold values from -0.375 to 0.375
Outputs:
- result: bfloat16 [8192, 1024], P('dp', 'section')
- input_grad: float32 [8192, 1024], P('dp', 'section')
- attend_gain_grad: float32 [1024], P(('dp', 'section'))
- attend_qkv_grad: float32 [1024, 3072], P(('dp', 'section'))
- attend_out_grad: float32 [1024, 1024], P(('dp', 'section'))
- mixer_gain_grad: float32 [1024], P(('dp', 'section'))
- mixer_up_grad: float32 [1024, 4096], P(('dp', 'section'))
- mixer_down_grad: float32 [4096, 1024], P(('dp', 'section'))
- column_gain_grad: float32 [64], replicated
- column_qkv_grad: float32 [64, 192], replicated
- column_out_grad: float32 [64, 64], replicated
- column_mix_gain_grad: float32 [64], replicated
- column_up_grad: float32 [64, 256], replicated
- column_down_grad: float32 [256, 64], replicated
The draws below stay inside these ranges and needn't reach their ends.
Inputs may be any that keep to these rules, and one draw needn't show every extreme that they name: `row_counts`: each group's 8 counts sum to 1024, and the largest of each group is exactly 512.
All inputs are finite; a program needn't handle non-finite values. No bound on the sum of `key_valid` on one device may be relied on, other than what follows from the above.
Results may differ from the reference program's by a relative error of at most 0.023.
Values may be sent and summed in bfloat16 or wider, within the bound.
No kernel may reach another device: no remote copies, remote signals or barrier semaphores. Data moves between devices by JAX's collectives and lax.ppermute only.
A program may use at most 384 MiB of HBM per device.

```python
import math
import jax
import jax.numpy as jnp
import numpy as np
from jax import lax

ROWS = 1024
DATASETS = 8
ATTR = 16
EMBED = 64
HEADS = 8
HEADS_ATTR = 8
FF = 4096
FF_ATTR = 256
D = 1024
TOTAL = 8192
N_DP = 8


def draw_cotangent(key, part):
    key = jax.random.fold_in(key, 11)
    rows_key, base_key = jax.random.split(key, 2)
    group_at = (jnp.arange(TOTAL) // ROWS).astype(jnp.float32)
    group_scale = jnp.exp(jnp.log(3.0) * group_at / max(N_DP - 1, 1))
    row_scale = jnp.exp(jax.random.uniform(rows_key, (TOTAL,), jnp.float32, -0.7, 0.7))
    base = jax.random.normal(base_key, (TOTAL, D), jnp.float32)
    values = base * (group_scale * row_scale)[:, None] * 0.6
    return jnp.clip(values, -8.0, 8.0).astype(jnp.bfloat16)


def touch_ends(values, key, low, top_value):
    longest = values.shape.index(max(values.shape))
    spots = []
    for shift in (0, 1):
        where = [jax.random.randint(jax.random.fold_in(key, axis), (), 0, length) for axis, length in enumerate(values.shape)]
        where[longest] = (where[longest] + shift) % values.shape[longest]
        spots.append(tuple(where))
    return values.at[spots[0]].set(low).at[spots[1]].set(top_value)


def level_of(rng, dims, cuts, low, top_value):
    gain = 1.0
    for dim, blocks in cuts:
        heights = jax.random.uniform(jax.random.fold_in(jax.random.fold_in(rng, 6), dim), (blocks,), jnp.float32, low / len(cuts), top_value / len(cuts))
        gain = gain * jnp.repeat(jnp.exp(heights), dims[dim] // blocks).reshape((-1,) + (1,) * (len(dims) - 1 - dim))
    return gain


def length_profile(count, total, limit, slope):
    weights = [(1 << 20) // math.isqrt(rank ** slope) + 1 for rank in range(2, count + 1)]
    surplus, given = total - limit - (count - 1), [1] * (count - 1)
    while surplus > 0:
        movable = [i for i in range(count - 1) if given[i] < limit]
        mass, left = sum([weights[i] for i in movable]), surplus
        for i in movable:
            more = min(limit - given[i], max(1, left * weights[i] // mass), surplus)
            given[i] = given[i] + more
            surplus = surplus - more
    return np.array([limit] + given)


def uneven_parts(own_key, amount, total, most, lean):
    if amount == 2:
        one = jax.random.randint(own_key, (), max(1, total - most), min(most, total - 1) + 1)
        return jnp.stack([one, total - one])
    lengths = jnp.asarray(length_profile(amount, total, most, lean), jnp.int32)
    pairs = (amount - 1) // 2
    giver, sink = lengths[1:1 + 2 * pairs:2], lengths[2:2 + 2 * pairs:2]
    slack = jnp.minimum(giver - 1, most - sink)
    passed = jax.random.randint(jax.random.fold_in(own_key, 1), (pairs,), 0, 1 << 20) % (slack + 1)
    lengths = lengths.at[1:1 + 2 * pairs:2].set(giver - passed).at[2:2 + 2 * pairs:2].set(sink + passed)
    return lengths[jax.random.permutation(jax.random.fold_in(own_key, 2), amount)]


def scatter_about(own_key, dims, scale, bound, shards=(), held_as=jnp.bfloat16):
    array = jax.random.normal(own_key, dims, jnp.float32) * scale
    if len(shards) > 0:
        array = level_of(own_key, dims, shards, -0.22, 0.18) * array
    return jnp.clip(array, min=-bound, max=bound).astype(held_as)


def setup_inputs(seed: int = 0) -> dict:
    streams_of = jax.random.split(jax.random.key(seed), 17)
    return {
        "features": scatter_about(streams_of[0], (TOTAL, D), 1.0, 6.0, ((0, 8),)),
        "cotangent": draw_cotangent(jax.random.fold_in(streams_of[16], 71), 0),
        "row_counts": jax.vmap(lambda own: uneven_parts(own, DATASETS, ROWS, ROWS // 2, 2))(jax.random.split(streams_of[2], N_DP)).reshape((N_DP, DATASETS)).astype(jnp.int32),
        "key_valid": touch_ends((jax.random.randint(streams_of[3], (TOTAL,), 0, 8) < 7).astype(jnp.int32), jax.random.fold_in(streams_of[3], 1), 0, 1),
        "attend_gain": jnp.clip(1.0 + 0.15 * jax.random.normal(streams_of[4], (D,), jnp.float32), 0.25, 1.75),
        "attend_qkv": scatter_about(streams_of[5], (D, 3 * D), D ** -0.5, 0.1875),
        "attend_out": scatter_about(streams_of[6], (D, D), (D // 64) ** -0.5, 1.5),
        "mixer_gain": jnp.clip(1.0 + 0.15 * jax.random.normal(streams_of[7], (D,), jnp.float32), 0.25, 1.75),
        "mixer_up": scatter_about(streams_of[8], (D, FF), D ** -0.5, 0.1875),
        "mixer_down": scatter_about(streams_of[9], (FF, D), FF ** -0.5, 0.09375),
        "column_gain": jnp.clip(1.0 + 0.15 * jax.random.normal(streams_of[10], (EMBED,), jnp.float32), 0.25, 1.75),
        "column_qkv": scatter_about(streams_of[11], (EMBED, 3 * EMBED), EMBED ** -0.5, 0.75),
        "column_out": scatter_about(streams_of[12], (EMBED, EMBED), (EMBED // 8) ** -0.5, 2.0),
        "column_mix_gain": jnp.clip(1.0 + 0.15 * jax.random.normal(streams_of[13], (EMBED,), jnp.float32), 0.25, 1.75),
        "column_up": scatter_about(streams_of[14], (EMBED, FF_ATTR), EMBED ** -0.5, 0.75),
        "column_down": scatter_about(streams_of[15], (FF_ATTR, EMBED), FF_ATTR ** -0.5, 0.375),
    }


@jax.custom_vjp
def low(v):
    return lax.optimization_barrier(v.astype(jnp.bfloat16)).astype(jnp.float32)

@jax.custom_vjp
def low_back(v):
    return v

def low_keep(v):
    return (low(v), None)

def low_pass(kept, grad):
    return (grad,)

def back_keep(v):
    return (v, None)

def back_low(kept, grad):
    return (low(grad),)
low.defvjp(low_keep, low_pass)
low_back.defvjp(back_keep, back_low)
EPSILON = 1e-05
MASKED = -1e+30
GELU_SCALE = 0.7978845608028654
HIGH = lax.Precision.HIGHEST

def normalize(vector, gain_vec):
    centred = vector - lax.optimization_barrier(jnp.mean(vector, axis=-1, keepdims=True))
    second = lax.optimization_barrier(jnp.mean(centred * centred, axis=-1, keepdims=True))
    return centred * lax.rsqrt(second + EPSILON) * gain_vec

def smooth(inputs):
    return 0.5 * inputs * (1.0 + jnp.tanh(GELU_SCALE * (inputs + 0.044715 * inputs * inputs * inputs)))

def softmax_rows(scores):
    row_peak = lax.optimization_barrier(jnp.max(scores, axis=-1, keepdims=True))
    lifted = jnp.exp(scores - row_peak)
    return lifted / lax.optimization_barrier(jnp.sum(lifted, axis=-1, keepdims=True))

def matmul(left, right):
    return jnp.dot(left, right, precision=HIGH, preferred_element_type=jnp.float32)

def group_forward(params, block, counts, valid):
    attend_gain, attend_qkv, attend_out, mixer_gain, mixer_up, mixer_down, column_gain, column_qkv, column_out, column_mix_gain, column_up, column_down = params
    row_count, model_width = block.shape
    head_dim = model_width // HEADS
    places = lax.iota(jnp.int32, row_count)
    bounds = jnp.cumsum(counts).astype(jnp.int32)
    segment = lax.optimization_barrier(jnp.sum((places[:, None] >= bounds[None, :]).astype(jnp.int32), axis=1))
    allowed = (segment[:, None] == segment[None, :]) & ((valid[None, :] == 1) | (places[:, None] == places[None, :]))
    normed = low(normalize(block, attend_gain))
    projected = low(low_back(matmul(normed, attend_qkv))).reshape(row_count, 3, HEADS, head_dim)
    scores = low_back(jnp.einsum('qhd,khd->hqk', projected[:, 0], projected[:, 1], precision=HIGH) * head_dim ** (-0.5))
    scores = jnp.where(allowed[None], scores, MASKED)
    shares = low(softmax_rows(scores))
    mixed = jnp.einsum('hqk,khd->qhd', shares, projected[:, 2], precision=HIGH).reshape(row_count, model_width)
    mixed = low(low_back(mixed))
    section_one = low(low_back(block + matmul(mixed, attend_out)))
    normed = low(normalize(section_one, mixer_gain))
    hidden = low(smooth(low_back(matmul(normed, mixer_up))))
    section_two = low(low_back(section_one + matmul(hidden, mixer_down)))
    cells = section_two.reshape(row_count * ATTR, -1)
    embed_width = cells.shape[1]
    small_dim = embed_width // HEADS_ATTR
    normed = low(normalize(cells, column_gain))
    projected = low(low_back(matmul(normed, column_qkv))).reshape(row_count, ATTR, 3, HEADS_ATTR, small_dim)
    scores = low_back(jnp.einsum('rahd,rbhd->rhab', projected[:, :, 0], projected[:, :, 1], precision=HIGH) * small_dim ** (-0.5))
    shares = low(softmax_rows(scores))
    mixed = jnp.einsum('rhab,rbhd->rahd', shares, projected[:, :, 2], precision=HIGH).reshape(row_count * ATTR, embed_width)
    mixed = low(low_back(mixed))
    section_three = low(low_back(cells + matmul(mixed, column_out)))
    normed = low(normalize(section_three, column_mix_gain))
    hidden = low(smooth(low_back(matmul(normed, column_up))))
    finished = low(section_three + matmul(hidden, column_down))
    return finished.reshape(row_count, model_width)

def reference(features, cotangent, row_counts, key_valid, attend_gain, attend_qkv, attend_out, mixer_gain, mixer_up, mixer_down, column_gain, column_qkv, column_out, column_mix_gain, column_up, column_down):
    params = tuple((weight.astype(jnp.float32) for weight in (attend_gain, attend_qkv, attend_out, mixer_gain, mixer_up, mixer_down, column_gain, column_qkv, column_out, column_mix_gain, column_up, column_down)))
    widened = features.astype(jnp.float32).reshape(N_DP, ROWS, -1)
    valid_groups = key_valid.reshape(N_DP, ROWS)

    def forward(inputs, weights):

        def one_group(carried, group):
            block, counts, valid = group
            return (carried, group_forward(weights, block, counts, valid))
        _, outputs = lax.scan(jax.checkpoint(one_group), None, (inputs, row_counts, valid_groups))
        return outputs
    outputs, pullback = jax.vjp(forward, widened, params)
    input_grad, grads_all = pullback(cotangent.astype(jnp.float32).reshape(outputs.shape))
    return (outputs.reshape(TOTAL, -1).astype(jnp.bfloat16), input_grad.reshape(TOTAL, -1), grads_all[0], grads_all[1], grads_all[2], grads_all[3], grads_all[4], grads_all[5], grads_all[6], grads_all[7], grads_all[8], grads_all[9], grads_all[10], grads_all[11])
```

```python
import functools

import jax
import jax.numpy as jnp
from jax import lax
from jax.experimental import pallas as pl
from jax.experimental.pallas import tpu as pltpu
from jax.sharding import PartitionSpec as P

ATTR = 16
HEADS = 8
HEADS_ATTR = 8

EPSILON = 1e-05
MASKED = -1e30
GELU_SCALE = 0.7978845608028654
GELU_CUBE = 0.044715
BF16 = jnp.bfloat16
F32 = jnp.float32


def exchanged(value, axis, mask):
    count = lax.axis_size(axis)
    return lax.ppermute(value, axis, [(at, at ^ mask) for at in range(count)])


def normal_parts(vector, axis=-1):
    centred = vector - jnp.mean(vector, axis=axis, keepdims=True)
    rate = lax.rsqrt(jnp.mean(centred * centred, axis=axis, keepdims=True) + EPSILON)
    return centred * rate, rate


def normal_back(normed, rate, scaled, axis=-1):
    middle = jnp.mean(scaled, axis=axis, keepdims=True)
    along = jnp.mean(scaled * normed, axis=axis, keepdims=True)
    return rate * (scaled - middle - normed * along)


def smooth(inputs):
    inner = GELU_SCALE * (inputs + GELU_CUBE * inputs * inputs * inputs)
    return 0.5 * inputs * (1.0 + jnp.tanh(inner))


def smooth_pair(inputs):
    square = inputs * inputs
    bent = jnp.tanh(GELU_SCALE * inputs * (1.0 + GELU_CUBE * square))
    half = 0.5 * (1.0 + bent)
    slope = half + (0.5 * GELU_SCALE) * inputs * (1.0 - bent * bent) * (
        1.0 + (3.0 * GELU_CUBE) * square
    )
    return inputs * half, slope


def dot(left, right):
    return jnp.dot(left, right, preferred_element_type=F32)


def dot_rows(left, right):
    return lax.dot_general(left, right, (((0,), (0,)), ((), ())), preferred_element_type=F32)


def dot_last(left, right):
    return lax.dot_general(left, right, (((1,), (1,)), ((), ())), preferred_element_type=F32)


def attend_forward_kernel(q_ref, k_ref, v_ref, mask_ref, out_ref, *, scale):
    scores = jnp.where(mask_ref[...] > 0, dot_last(q_ref[...], k_ref[...]) * scale, MASKED)
    lifted = jnp.exp(scores - jnp.max(scores, axis=-1, keepdims=True))
    shares = (lifted / jnp.sum(lifted, axis=-1, keepdims=True)).astype(BF16)
    out_ref[...] = dot(shares, v_ref[...]).astype(BF16)


def attend_forward(projected, mask, own_rows):
    rows, wide = projected.shape
    width = wide // 3
    head_dim = width // HEADS
    return pl.pallas_call(
        functools.partial(attend_forward_kernel, scale=head_dim**-0.5),
        grid=(HEADS,),
        in_specs=[
            pl.BlockSpec((own_rows, head_dim), lambda h: (0, h)),
            pl.BlockSpec((rows, head_dim), lambda h: (0, HEADS + h)),
            pl.BlockSpec((rows, head_dim), lambda h: (0, 2 * HEADS + h)),
            pl.BlockSpec((own_rows, rows), lambda h: (0, 0)),
        ],
        out_specs=pl.BlockSpec((own_rows, head_dim), lambda h: (0, h)),
        out_shape=jax.ShapeDtypeStruct((own_rows, width), BF16),
        compiler_params=pltpu.CompilerParams(vmem_limit_bytes=48 * 2**20),
        name="attend_forward",
    )(projected, projected, projected, mask)


def attend_backward_kernel(
    first_ref, q_ref, k_ref, v_ref, up_ref, mask_ref, mixed_ref, dq_ref, dk_ref, dv_ref, *, scale
):
    queries, keys, values, upstream = q_ref[...], k_ref[...], v_ref[...], up_ref[...]
    scores = jnp.where(mask_ref[...] > 0, dot_last(queries, keys) * scale, MASKED)
    lifted = jnp.exp(scores - jnp.max(scores, axis=-1, keepdims=True))
    shares = lifted / jnp.sum(lifted, axis=-1, keepdims=True)
    shares_low = shares.astype(BF16)
    mixed_ref[...] = dot(shares_low, values).astype(BF16)
    share_grad = dot_last(upstream, values)
    centre = jnp.sum(share_grad * shares, axis=-1, keepdims=True)
    score_grad = (shares * (share_grad - centre)).astype(BF16)
    dq_ref[...] = (dot(score_grad, keys) * scale).astype(BF16)
    dk_ref[...] = (dot_rows(score_grad, queries) * scale).astype(BF16)
    dv_ref[...] = dot_rows(shares_low, upstream).astype(BF16)


def attend_backward(projected, pulled, mask, first_head):
    rows, wide = projected.shape
    head_dim = wide // 3 // HEADS
    count = pulled.shape[1] // head_dim
    block = (rows, head_dim)
    like = jax.ShapeDtypeStruct(pulled.shape, BF16)
    return pl.pallas_call(
        functools.partial(attend_backward_kernel, scale=head_dim**-0.5),
        grid_spec=pltpu.PrefetchScalarGridSpec(
            num_scalar_prefetch=1,
            grid=(count,),
            in_specs=[
                pl.BlockSpec(block, lambda h, f: (0, f[0] + h)),
                pl.BlockSpec(block, lambda h, f: (0, HEADS + f[0] + h)),
                pl.BlockSpec(block, lambda h, f: (0, 2 * HEADS + f[0] + h)),
                pl.BlockSpec(block, lambda h, f: (0, h)),
                pl.BlockSpec((rows, rows), lambda h, f: (0, 0)),
            ],
            out_specs=[pl.BlockSpec(block, lambda h, f: (0, h))] * 4,
        ),
        out_shape=[like] * 4,
        compiler_params=pltpu.CompilerParams(vmem_limit_bytes=48 * 2**20),
        name="attend_backward",
    )(first_head, projected, projected, projected, pulled, mask)


def column_kernel(
    cells_ref,
    upstream_ref,
    gain_ref,
    qkv_ref,
    qkv_t_ref,
    out_ref,
    out_t_ref,
    mix_gain_ref,
    up_ref,
    up_t_ref,
    down_ref,
    down_t_ref,
    result_ref,
    cells_grad_ref,
    gain_grad_ref,
    qkv_grad_ref,
    out_grad_ref,
    mix_gain_grad_ref,
    up_grad_ref,
    down_grad_ref,
    projected,
    normed_low,
    shares_kept,
    score_grads,
    mixed,
    mixed_grad,
    sum_grad,
    *,
    width,
    small,
):
    lanes = cells_ref.shape[1]
    heads = HEADS_ATTR
    scale = small**-0.5
    lane_blocks = lanes // 128
    gain = gain_ref[...]
    mix_gain = mix_gain_ref[...]

    for ref in (gain_grad_ref, qkv_grad_ref, out_grad_ref, mix_gain_grad_ref, up_grad_ref, down_grad_ref):
        ref[...] = jnp.zeros_like(ref)

    def at_rows(a):
        return pl.ds(pl.multiple_of(a * width, width), width)

    @pl.loop(0, ATTR)
    def _(a):
        normed, _ = normal_parts(cells_ref[at_rows(a), :].astype(F32), 0)
        low = (normed * gain).astype(BF16)
        normed_low[at_rows(a), :] = low
        projected[a] = dot(qkv_t_ref[...], low).astype(BF16).astype(F32).reshape(
            3, small, heads, lanes
        )

    for block in range(lane_blocks):
        here = slice(block * 128, block * 128 + 128)

        @pl.loop(0, ATTR)
        def _(a):
            query = projected[a, 0, :, :, here]
            scores = [
                jnp.sum(query * projected[b, 1, :, :, here], axis=0) * scale for b in range(ATTR)
            ]
            peak = functools.reduce(jnp.maximum, scores)
            lifted = [jnp.exp(score - peak) for score in scores]
            rate = 1.0 / functools.reduce(jnp.add, lifted)
            total = jnp.zeros((small, heads, 128), F32)
            for b in range(ATTR):
                share = lifted[b] * rate
                shares_kept[a, b, :, here] = share
                total += share.astype(BF16).astype(F32)[None] * projected[b, 2, :, :, here]
            mixed[at_rows(a), here] = total.reshape(width, 128).astype(BF16)

    @pl.loop(0, ATTR)
    def _(a):
        rows = at_rows(a)
        cells = cells_ref[rows, :].astype(F32)
        mixed_low = mixed[rows, :]
        third = (cells + dot(out_t_ref[...], mixed_low)).astype(BF16).astype(F32)
        normed, rate = normal_parts(third, 0)
        low = (normed * mix_gain).astype(BF16)
        hidden, slope = smooth_pair(dot(up_t_ref[...], low))
        hidden = hidden.astype(BF16)
        result_ref[rows, :] = (third + dot(down_t_ref[...], hidden)).astype(BF16)
        upstream = upstream_ref[rows, :]
        down_grad_ref[...] += dot_last(upstream, hidden)
        lifted_grad = (slope * dot(down_ref[...], upstream)).astype(BF16)
        up_grad_ref[...] += dot_last(low, lifted_grad)
        normed_grad = dot(up_ref[...], lifted_grad)
        mix_gain_grad_ref[...] += normed_grad * normed
        third_grad = (
            upstream.astype(F32) + normal_back(normed, rate, normed_grad * mix_gain, 0)
        ).astype(BF16)
        sum_grad[rows, :] = third_grad
        out_grad_ref[...] += dot_last(mixed_low, third_grad)
        mixed_grad[a] = dot(out_ref[...], third_grad).astype(BF16).astype(F32).reshape(
            small, heads, lanes
        )

    for block in range(lane_blocks):
        here = slice(block * 128, block * 128 + 128)

        @pl.loop(0, ATTR)
        def _(a):
            pulled = mixed_grad[a, :, :, here]
            share_grads = [
                jnp.sum(pulled * projected[b, 2, :, :, here], axis=0) for b in range(ATTR)
            ]
            shares = [shares_kept[a, b, :, here] for b in range(ATTR)]
            centre = functools.reduce(jnp.add, [s * g for s, g in zip(shares, share_grads)])
            total = jnp.zeros((small, heads, 128), F32)
            for b in range(ATTR):
                grad = (shares[b] * (share_grads[b] - centre)).astype(BF16).astype(F32)
                score_grads[a, b, :, here] = grad
                shares_kept[a, b, :, here] = shares[b].astype(BF16).astype(F32)
                total += grad[None] * projected[b, 1, :, :, here]
            mixed[at_rows(a), here] = (total * scale).reshape(width, 128).astype(BF16)

        @pl.loop(0, ATTR)
        def _(b):
            key_grad = jnp.zeros((small, heads, 128), F32)
            value_grad = jnp.zeros((small, heads, 128), F32)
            for a in range(ATTR):
                key_grad += score_grads[a, b, :, here][None] * projected[a, 0, :, :, here]
                value_grad += shares_kept[a, b, :, here][None] * mixed_grad[a, :, :, here]
            projected[b, 1, :, :, here] = key_grad * scale
            projected[b, 2, :, :, here] = value_grad

    @pl.loop(0, ATTR)
    def _(a):
        rows = at_rows(a)
        key_value = projected[a, 1:3].reshape(2 * width, lanes).astype(BF16)
        grads = jnp.concatenate([mixed[rows, :], key_value], axis=0)
        qkv_grad_ref[...] += dot_last(normed_low[rows, :], grads)
        normed_grad = dot(qkv_ref[...], grads)
        normed, rate = normal_parts(cells_ref[rows, :].astype(F32), 0)
        gain_grad_ref[...] += normed_grad * normed
        back = normal_back(normed, rate, normed_grad * gain, 0)
        cells_grad_ref[rows, :] = (sum_grad[rows, :].astype(F32) + back).astype(BF16)


def column_layers(cells, upstream, gain, qkv, out, mix_gain, up, down):
    depth, lanes = cells.shape
    width = depth // ATTR
    small = width // HEADS_ATTR
    hidden = up.shape[1]
    qkv_heads = qkv.reshape(width, 3, HEADS_ATTR, small).transpose(0, 1, 3, 2)
    qkv_heads = qkv_heads.reshape(width, 3 * width)
    out_heads = out.reshape(HEADS_ATTR, small, width).transpose(1, 0, 2).reshape(width, width)
    spread = functools.partial(jnp.broadcast_to, shape=(width, lanes))
    like = jax.ShapeDtypeStruct
    results = pl.pallas_call(
        functools.partial(column_kernel, width=width, small=small),
        out_shape=[
            like((depth, lanes), BF16),
            like((depth, lanes), BF16),
            like((width, lanes), F32),
            like((width, 3 * width), F32),
            like((width, width), F32),
            like((width, lanes), F32),
            like((width, hidden), F32),
            like((width, hidden), F32),
        ],
        scratch_shapes=[
            pltpu.VMEM((ATTR, 3, small, HEADS_ATTR, lanes), F32),
            pltpu.VMEM((depth, lanes), BF16),
            pltpu.VMEM((ATTR, ATTR, HEADS_ATTR, lanes), F32),
            pltpu.VMEM((ATTR, ATTR, HEADS_ATTR, lanes), F32),
            pltpu.VMEM((depth, lanes), BF16),
            pltpu.VMEM((ATTR, small, HEADS_ATTR, lanes), F32),
            pltpu.VMEM((depth, lanes), BF16),
        ],
        compiler_params=pltpu.CompilerParams(vmem_limit_bytes=48 * 2**20),
        name="column_layers",
    )(
        cells,
        upstream,
        spread(gain[:, None]),
        qkv_heads,
        qkv_heads.T,
        out_heads,
        out_heads.T,
        spread(mix_gain[:, None]),
        up,
        up.T,
        down,
        down.T,
    )
    result, cells_grad, gain_grad, qkv_grad, out_grad, mix_gain_grad, up_grad, down_grad = results
    qkv_grad = qkv_grad.reshape(width, 3, small, HEADS_ATTR).transpose(0, 1, 3, 2)
    out_grad = out_grad.reshape(small, HEADS_ATTR, width).transpose(1, 0, 2)
    return (
        result,
        cells_grad,
        jnp.sum(gain_grad, axis=1),
        qkv_grad.reshape(width, 3 * width),
        out_grad.reshape(width, width),
        jnp.sum(mix_gain_grad, axis=1),
        up_grad,
        down_grad.T,
    )


def one_bit(value, dim, bit):
    return lax.dynamic_index_in_dim(value, bit, dim, keepdims=False)


def halved(value, dim, own_bit, axis, mask):
    arrived = exchanged(one_bit(value, dim, 1 - own_bit).astype(BF16), axis, mask)
    return one_bit(value, dim, own_bit).astype(F32) + arrived.astype(F32)


def body(
    features,
    cotangent,
    row_counts,
    key_valid,
    attend_gain,
    attend_qkv,
    attend_out,
    mixer_gain,
    mixer_up,
    mixer_down,
    column_gain,
    column_qkv,
    column_out,
    column_mix_gain,
    column_up,
    column_down,
):
    dp_count = lax.axis_size("dp")
    section_count = lax.axis_size("section")
    dp_at, section_at = lax.axis_index("dp"), lax.axis_index("section")
    core, near, far = dp_at & 1, section_at & 1, section_at >> 1
    chip_bits = (dp_count // 2).bit_length() - 1
    group_rows, width = features.shape
    half_rows = group_rows // 2
    own = half_rows // 2
    head_dim = width // HEADS
    hidden = mixer_up.shape[1]

    counts = row_counts[0]
    bounds = jnp.cumsum(counts)
    largest = jnp.argmax(counts)
    start = bounds[largest] - counts[largest]
    half_start = start + half_rows * far
    own_start = half_start + own * near
    near_start = half_start + own * (1 - near)
    segment = jnp.sum(
        (lax.iota(jnp.int32, group_rows)[:, None] >= bounds[None, :]).astype(jnp.int32), axis=1
    )

    def turned(array):
        return jnp.concatenate([array, array[:half_rows]], axis=0)

    def cut(array, begin):
        return lax.dynamic_slice_in_dim(array, begin, own, 0)

    def both(array):
        longer = turned(array)
        return jnp.concatenate([cut(longer, own_start), cut(longer, near_start)], axis=0)

    half_x = both(features)
    half_segment, half_valid = both(segment), both(key_valid)
    upstream = cut(turned(cotangent), own_start)
    mask = (
        (half_segment[:, None] == half_segment[None, :])
        & ((half_valid == 1)[None, :] | jnp.eye(half_rows, dtype=bool))
    ).astype(F32)

    half_n, half_rate = normal_parts(half_x.astype(F32))
    half_normed = (half_n * attend_gain).astype(BF16)
    projected = dot(half_normed, attend_qkv).astype(BF16)
    attended = attend_forward(projected, mask, own)
    first = (half_x[:own].astype(F32) + dot(attended, attend_out)).astype(BF16)

    def across_cores(array):
        return jnp.concatenate([array, exchanged(array, "dp", 1)], axis=0)

    def across_near(array):
        return jnp.concatenate([array, exchanged(array, "section", 1)], axis=0)

    first_wide = first.astype(F32)
    second_n, second_rate = normal_parts(first_wide)
    second_normed = (second_n * mixer_gain).astype(BF16)
    hidden_own, slope_own = smooth_pair(dot(second_normed, mixer_up))
    second = (first_wide + dot(hidden_own.astype(BF16), mixer_down)).astype(BF16)

    part = hidden // (dp_count * section_count)

    def own_part(weight, dim):
        shape = weight.shape[:dim] + (dp_count // 2, 2, 2, 2, part) + weight.shape[dim + 1 :]
        taken = one_bit(one_bit(weight.reshape(shape), dim + 3, near), dim + 1, core)
        return taken.reshape(weight.shape[:dim] + (hidden // 4,) + weight.shape[dim + 1 :])

    up_part, down_part = own_part(mixer_up, 1), own_part(mixer_down, 0)
    pool_normed = across_cores(across_near(second_normed))
    pool_hidden, pool_slope = smooth_pair(dot(pool_normed, up_part))
    pool_hidden = pool_hidden.astype(BF16)

    columns = column_layers(
        second.T,
        upstream.T,
        column_gain,
        column_qkv,
        column_out,
        column_mix_gain,
        column_up,
        column_down,
    )
    result_own = columns[0].T
    second_grad = columns[1].T

    def to_columns(rows_own):
        quarter = width // section_count
        pieces = rows_own.reshape(own, section_count, quarter)
        kept = [one_bit(pieces, 1, section_at)]
        for mask_at in range(1, section_count):
            kept.append(exchanged(one_bit(pieces, 1, section_at ^ mask_at), "section", mask_at))
        stacked = jnp.stack(kept)
        ordered = jnp.take(stacked, jnp.arange(section_count) ^ section_at, axis=0)
        ordered = ordered.reshape(group_rows, quarter)
        doubled = jnp.concatenate([ordered, ordered], axis=0)
        return lax.dynamic_slice_in_dim(doubled, group_rows - start, group_rows, 0)

    result = to_columns(result_own)

    def summed(flat):
        for mask_at in [1 << bit for bit in range(chip_bits + 1)]:
            flat = flat + exchanged(flat, "dp", mask_at)
        for mask_at in (1, 2):
            flat = flat + exchanged(flat, "section", mask_at)
        return flat

    small_grads = columns[2:]
    small_sum = summed(jnp.concatenate([grad.reshape(-1) for grad in small_grads]))

    lifted_grad = (slope_own * dot_last(second_grad, mixer_down)).astype(BF16)
    second_normed_grad = dot_last(lifted_grad, mixer_up)
    mixer_gain_grad = jnp.sum(second_normed_grad * second_n, axis=0)
    back = normal_back(second_n, second_rate, second_normed_grad * mixer_gain)
    first_grad = (second_grad.astype(F32) + back).astype(BF16)

    pool_grad = across_cores(across_near(second_grad))
    down_grad = dot_rows(pool_hidden, pool_grad)
    pool_lifted = (pool_slope * dot_last(pool_grad, down_part)).astype(BF16)
    up_grad = dot_rows(pool_normed, pool_lifted)

    def scattered(grad):
        bits = (2,) * (chip_bits + 1)
        rest, columns_all = grad.shape[0] >> (chip_bits + 1), grad.shape[1]
        shaped = grad.reshape(bits + (rest, columns_all))
        done = []
        for piece, order in (
            (shaped[..., : columns_all // 2], range(chip_bits)),
            (shaped[..., columns_all // 2 :], range(chip_bits - 1, -1, -1)),
        ):
            left = list(range(chip_bits))
            for bit in order:
                dim = left.index(chip_bits - 1 - bit)
                left.pop(dim)
                piece = halved(piece, dim, (dp_at >> (bit + 1)) & 1, "dp", 2 << bit)
            done.append(halved(piece, 0, far, "section", 2))
        return jnp.concatenate(done, axis=-1)

    def quad_columns(block):
        low = block.astype(BF16).reshape((2, 2) + block.shape[1:])
        rows_near = one_bit(low, 1, near)
        other = exchanged(one_bit(low, 1, 1 - near), "section", 1)
        pair = jnp.where(near == 0, jnp.stack([rows_near, other]), jnp.stack([other, rows_near]))
        rows_core = one_bit(pair, 1, core)
        other = exchanged(one_bit(pair, 1, 1 - core), "dp", 1)
        quad = jnp.where(core == 0, jnp.stack([rows_core, other]), jnp.stack([other, rows_core]))
        return quad.transpose(2, 0, 1, 3).astype(F32)

    mixer_down_grad = scattered(down_grad)

    def rows_first(grad):
        rows, cols = grad.shape
        rest = rows // (dp_count * section_count)
        shaped = grad.reshape(dp_count // 2, 2, 2, 2, rest, cols).transpose(0, 2, 1, 3, 4, 5)
        return shaped.reshape(rows, cols), rest

    ordered, rest = rows_first(up_grad)
    up_block = quad_columns(scattered(ordered).reshape(4, rest, hidden // 4))
    mixer_up_grad = (
        up_block.reshape(rest, 2, 2, dp_count // 2, 2, part)
        .transpose(0, 3, 1, 4, 2, 5)
        .reshape(rest, hidden)
    )

    own_heads = HEADS // 2
    own_width = own_heads * head_dim
    first_head = (near * own_heads).astype(jnp.int32)
    half_grad = across_near(first_grad)
    own_out = lax.dynamic_slice_in_dim(attend_out, near * own_width, own_width, 0)
    half_pulled = dot_last(half_grad, own_out).astype(BF16)
    half_mixed, dq, dk, dv = attend_backward(projected, half_pulled, mask, first_head[None])
    half_dqkv = jnp.stack([dq, dk, dv], axis=1)
    own_qkv = lax.dynamic_slice_in_dim(
        attend_qkv.reshape(width, 3, width), near * own_width, own_width, 2
    )
    qkv_in_grad = dot_last(
        half_dqkv.reshape(half_rows, 3 * own_width), own_qkv.reshape(width, 3 * own_width)
    )
    arrived = exchanged(qkv_in_grad[own:].astype(BF16), "section", 1)
    normed_grad = qkv_in_grad[:own] + arrived.astype(F32)
    own_n, own_rate = half_n[:own], half_rate[:own]
    attend_gain_grad = jnp.sum(normed_grad * own_n, axis=0)
    back = normal_back(own_n, own_rate, normed_grad * attend_gain)
    input_own = (first_grad.astype(F32) + back).astype(BF16)
    input_grad = to_columns(input_own).astype(F32)

    def core_heads(array):
        shaped = array.reshape(array.shape[:-1] + (2, own_width // 2))
        dim = shaped.ndim - 2
        arrived = exchanged(one_bit(shaped, dim, 1 - core), "dp", 1)
        return jnp.concatenate([one_bit(shaped, dim, core), arrived], axis=0)

    pool_dqkv = core_heads(half_dqkv).reshape(group_rows, 3 * own_width // 2)
    pool_first = across_cores(half_normed)
    qkv_grad = dot_rows(pool_first, pool_dqkv)
    ordered, rest = rows_first(qkv_grad)
    qkv_block = quad_columns(scattered(ordered).reshape(4, rest, 3 * own_width // 2))
    attend_qkv_grad = (
        qkv_block.reshape(rest, 2, 2, 3, own_width // 2)
        .transpose(0, 3, 2, 1, 4)
        .reshape(rest, 3 * width)
    )

    pool_mixed = core_heads(half_mixed)
    pool_first_grad = across_cores(half_grad)
    out_grad = dot_rows(pool_mixed, pool_first_grad)
    out_block = scattered(out_grad)
    moves = []
    blocks = dp_count * section_count
    per_quad = blocks // 4
    for dp_from in range(dp_count):
        for section_from in range(section_count):
            place = (dp_from >> 1) * 2 + (section_from >> 1)
            holds = ((section_from & 1) * 2 + (dp_from & 1)) * per_quad + place
            moves.append((dp_from * section_count + section_from, holds))
    attend_out_grad = lax.ppermute(out_block.astype(BF16), ("dp", "section"), moves).astype(F32)

    gains = summed(jnp.stack([attend_gain_grad, mixer_gain_grad]))
    share = width // (dp_count * section_count)
    gains = lax.dynamic_slice_in_dim(gains, (dp_at * section_count + section_at) * share, share, 1)

    small_out, at = [], 0
    for grad in small_grads:
        small_out.append(small_sum[at : at + grad.size].reshape(grad.shape))
        at += grad.size
    return (
        result,
        input_grad,
        gains[0],
        attend_qkv_grad,
        attend_out_grad,
        gains[1],
        mixer_up_grad,
        mixer_down_grad,
        *small_out,
    )


def solution(mesh):
    split = P(("dp", "section"))
    return jax.shard_map(
        body,
        mesh=mesh,
        in_specs=(P("dp", None), P("dp", None), P("dp", None), P("dp")) + (P(),) * 12,
        out_specs=(P("dp", "section"),) * 2 + (split,) * 6 + (P(),) * 6,
        check_vma=False,
    )
```

```python
import functools

import jax
import jax.numpy as jnp
from jax import lax
from jax.experimental import pallas as pl
from jax.experimental.pallas import tpu as pltpu
from jax.sharding import PartitionSpec as P

ATTR = 16
HEADS = 8
HEADS_ATTR = 8

EPSILON = 1e-05
MASKED = -1e30
GELU_SCALE = 0.7978845608028654
GELU_CUBE = 0.044715
BF16 = jnp.bfloat16
F32 = jnp.float32

FLOPS, BYTES = 1.10e+09, 3.60e+06

CORE, NEAR, FAR, CHIP, SECTION, COUNTS = range(6)


def exchanged(value, axis, mask):
    count = lax.axis_size(axis)
    return lax.ppermute(value, axis, [(at, at ^ mask) for at in range(count)])


def normal_parts(vector, axis=-1):
    centred = vector - jnp.mean(vector, axis=axis, keepdims=True)
    rate = lax.rsqrt(jnp.mean(centred * centred, axis=axis, keepdims=True) + EPSILON)
    return centred * rate, rate


def normal_back(normed, rate, scaled, axis=-1):
    middle = jnp.mean(scaled, axis=axis, keepdims=True)
    along = jnp.mean(scaled * normed, axis=axis, keepdims=True)
    return rate * (scaled - middle - normed * along)


def smooth_pair(inputs):
    square = inputs * inputs
    bent = jnp.tanh(GELU_SCALE * inputs * (1.0 + GELU_CUBE * square))
    half = 0.5 * (1.0 + bent)
    slope = half + (0.5 * GELU_SCALE) * inputs * (1.0 - bent * bent) * (
        1.0 + (3.0 * GELU_CUBE) * square
    )
    return inputs * half, slope


def dot(left, right):
    return jnp.dot(left, right, preferred_element_type=F32)


def dot_rows(left, right):
    return lax.dot_general(left, right, (((0,), (0,)), ((), ())), preferred_element_type=F32)


def dot_last(left, right):
    return lax.dot_general(left, right, (((1,), (1,)), ((), ())), preferred_element_type=F32)


def shape_of(dims, dtype):
    return jax.ShapeDtypeStruct(dims, dtype)


class Joined:
    def __init__(self, *pieces, far=()):
        self.pieces, self.far = pieces, far
        self.shape = (sum(rows for _, _, rows in pieces), *pieces[0][0].shape[1:])
        self.dtype = pieces[0][0].dtype


class Arriving:
    def __init__(self, pieces, ref, sems):
        self.ref, self.shape, self.dtype = ref, ref.shape, ref.dtype
        self.copies, at = [], 0
        for k, (source, first, rows) in enumerate(pieces):
            target = ref
            if len(pieces) > 1:
                source, target = source.at[pl.ds(first, rows)], ref.at[pl.ds(at, rows)]
            self.copies.append(pltpu.make_async_copy(source, target, sems[k]))
            at += rows
        for copy in self.copies:
            copy.start()

    def wait(self):
        for copy in self.copies:
            copy.wait()
        self.copies = []

    def __getitem__(self, at):
        self.wait()
        return self.ref[at]


class Leaving:
    def __init__(self, target, ref, sem):
        self.ref, self.shape, self.dtype = ref, ref.shape, ref.dtype
        self.copy, self.started = pltpu.make_async_copy(ref, target, sem), False

    def __getitem__(self, at):
        return self.ref[at]

    def __setitem__(self, at, value):
        self.ref[at] = value

    def send(self):
        if not self.started:
            self.copy.start()
            self.started = True


def call(
    body, name, info, arrays, out_shape, scratch=(), vmem=16, raw=(), far_in=(), far_out=(), near_in=(),
    near_out=(), plain=False, micros=0,
):
    options = dict(
        compiler_params=pltpu.CompilerParams(vmem_limit_bytes=vmem * 2**20),
        cost_estimate=pl.CostEstimate(
            flops=int(micros * FLOPS), bytes_accessed=int(micros * BYTES), transcendentals=0
        ),
        name=name,
    )
    if plain:

        def whole(array):
            return pl.BlockSpec(array.shape, lambda *_: (0,) * len(array.shape))

        spec = pltpu.PrefetchScalarGridSpec(
            num_scalar_prefetch=1,
            grid=(1,),
            in_specs=[whole(array) for array in arrays],
            out_specs=[whole(shape) for shape in out_shape],
            scratch_shapes=scratch,
        )
        return pl.pallas_call(body, grid_spec=spec, out_shape=out_shape, **options)(info, *arrays)
    copied = [k for k in range(len(arrays)) if k not in raw and k not in near_in]
    flat, places, in_specs = [], [], []
    for k, array in enumerate(arrays):
        pieces = array.pieces if isinstance(array, Joined) else [(array, 0, array.shape[0])]
        places.append([(len(flat) + n, first, rows) for n, (_, first, rows) in enumerate(pieces)])
        for n, (piece, _, _) in enumerate(pieces):
            if k in raw or k in far_in or n in getattr(array, "far", ()):
                piece = pltpu.with_memory_space_constraint(piece, pltpu.HBM)
            if k in near_in:
                piece = pltpu.with_memory_space_constraint(piece, pltpu.VMEM)
            flat.append(piece)
            in_specs.append(
                pl.BlockSpec(memory_space=pltpu.VMEM if k in near_in else pl.ANY)
            )
    count, outs = len(flat), len(out_shape)
    leaving = [k for k in range(outs) if k not in near_out]

    def run(info_ref, *refs):
        given, made, rest = refs[:count], refs[count : count + outs], refs[count + outs :]
        held, rest = rest[: len(copied)], rest[len(copied) :]
        out_held, rest = rest[: len(leaving)], rest[len(leaving) :]
        in_sems, out_sems, *rest = rest
        inputs = []
        for k in range(len(arrays)):
            if k in raw or k in near_in:
                inputs.append(given[places[k][0][0]])
                continue
            pieces = [
                (given[at], first, rows)
                for at, first, rows in places[k]
            ]
            sems = [in_sems.at[at] for at, _, _ in places[k]]
            inputs.append(Arriving(pieces, held[copied.index(k)], sems))
        outputs = [
            Leaving(made[k], out_held[leaving.index(k)], out_sems.at[k]) if k in leaving else made[k]
            for k in range(outs)
        ]
        body(info_ref, *inputs, *outputs, *rest)
        outputs = [outputs[k] for k in leaving]
        for one in inputs:
            if isinstance(one, Arriving):
                one.wait()
        for one in outputs:
            one.send()
        for one in outputs:
            one.copy.wait()

    def in_vmem(array):
        return pltpu.VMEM(array.shape, array.dtype)

    plain_out = out_shape
    out_shape = list(out_shape)
    for k, shape in enumerate(plain_out):
        if k in far_out or k in near_out:
            space = pltpu.HBM if k in far_out else pltpu.VMEM
            out_shape[k] = space(shape.shape, shape.dtype)
    spec = pltpu.PrefetchScalarGridSpec(
        num_scalar_prefetch=1,
        grid=(),
        in_specs=in_specs,
        out_specs=[
            pl.BlockSpec(memory_space=pltpu.VMEM if k in near_out else pl.ANY) for k in range(outs)
        ],
        scratch_shapes=[in_vmem(arrays[k]) for k in copied]
        + [in_vmem(plain_out[k]) for k in leaving]
        + [pltpu.SemaphoreType.DMA((count,)), pltpu.SemaphoreType.DMA((outs,))]
        + list(scratch),
    )
    return pl.pallas_call(run, grid_spec=spec, out_shape=out_shape, **options)(info, *flat)


def picked(source, columns):
    at = lax.broadcasted_iota(jnp.int32, (source.shape[0], columns), 1)
    return jnp.where(at == source, 1.0, 0.0).astype(BF16)


def bounds_of(info_ref):
    bounds, bound = [], jnp.int32(0)
    for k in range(COUNTS, info_ref.shape[0]):
        bound = bound + info_ref[k]
        bounds.append(bound)
    return bounds


def group_row(info_ref, far, near, at, rows):
    start = jnp.int32(0)
    for k, bound in enumerate(bounds_of(info_ref)):
        start = jnp.where(info_ref[COUNTS + k] == rows // 2, bound - rows // 2, start)
    source = at + (start + far * (rows // 2) + near * (rows // 4))
    return jnp.where(source >= rows, source - rows, source)


def softmax_parts(queries, keys, allowed, scale):
    scores = jnp.where(allowed, dot_last(queries, keys) * scale, MASKED)
    lifted = jnp.exp(scores - jnp.max(scores, axis=-1, keepdims=True))
    return lifted * (1.0 / jnp.sum(lifted, axis=-1, keepdims=True))


def attend_kernel(
    info_ref, features, valid_ref, gain_ref, qkv_hbm, out_hbm, next_gain_ref, up_hbm, down_hbm,
    own_ref, normed_ref, projected_ref, mask_ref, shared_ref, first_ref, slope_ref,
    turned_ref, weights, out, ups, downs, sems, *, head_dim,
):
    rows, width = features.shape
    half, own = rows // 2, rows // 4
    pair = 2 * head_dim

    def copy(source, target, at):
        return pltpu.make_async_copy(source, target, sems.at[at])

    to_weights = copy(qkv_hbm, weights, 0)
    to_out = copy(out_hbm, out, 1)
    to_mixer = [copy(up_hbm, ups, 2), copy(down_hbm, downs, 3)]
    to_weights.start()

    near, far = info_ref[NEAR], info_ref[FAR]

    def source_of(at):
        side = jnp.where(at < own, near, 1 - near)
        return group_row(info_ref, far, side, jnp.where(at < own, at, at - own), rows)

    row_source = source_of(lax.broadcasted_iota(jnp.int32, (half, 1), 0))
    lane_source = source_of(lax.broadcasted_iota(jnp.int32, (1, half), 1))
    pick = picked(row_source, rows)
    row_segment = jnp.zeros((half, 1), jnp.int32)
    lane_segment = jnp.zeros((1, half), jnp.int32)
    for bound in bounds_of(info_ref):
        row_segment += (row_source >= bound).astype(jnp.int32)
        lane_segment += (lane_source >= bound).astype(jnp.int32)
    valid = valid_ref[...].astype(F32).astype(BF16)
    usable = dot_last(jnp.broadcast_to(valid, (8, rows)), pick)[:1]
    same = lax.broadcasted_iota(jnp.int32, (half, half), 0) == lax.broadcasted_iota(
        jnp.int32, (half, half), 1
    )
    allowed = (row_segment == lane_segment) & ((usable > 0.5) | same)
    mask_ref[...] = jnp.where(allowed, 1.0, 0.0)
    features.wait()
    to_out.start()
    taken = dot(pick, features[...])
    own_ref[...] = taken[:own].astype(BF16)
    normed, _ = normal_parts(taken)
    normed_ref[...] = (normed * gain_ref[...]).astype(BF16)

    to_weights.wait()
    projected_ref[...] = dot(normed_ref[...], weights[...]).astype(BF16)
    projected_ref.send()
    normed_ref.send()
    mask_ref.send()
    own_ref.send()
    for one in to_mixer:
        one.start()

    @pl.loop(0, width // pair)
    def _(step):
        def columns(first):
            return pl.ds(pl.multiple_of(first + step * pair, pair), pair)

        queries = projected_ref[:own, columns(0)]
        keys = projected_ref[:, columns(width)]
        values = projected_ref[:, columns(2 * width)]
        open_ = mask_ref[:own, :] > 0
        mixed = []
        for head in range(2):
            here = slice(head * head_dim, (head + 1) * head_dim)
            shares = softmax_parts(queries[:, here], keys[:, here], open_, head_dim**-0.5)
            mixed.append(dot(shares.astype(BF16), values[:, here]).astype(BF16))
        shared_ref[own:, columns(0)] = jnp.concatenate(mixed, axis=1)

    to_out.wait()
    first = own_ref[...].astype(F32) + dot(shared_ref[own:, :], out[...])
    first_ref[...] = first.astype(BF16)
    total = first_ref[...].astype(F32)
    normed, _ = normal_parts(total)
    shared_ref[:own, :] = (normed * next_gain_ref[...]).astype(BF16)
    shared_ref.send()
    first_ref.send()

    for one in to_mixer:
        one.wait()
    hidden, slope = smooth_pair(dot(shared_ref[:own, :], ups[...]))
    slope_ref[...] = slope.astype(BF16)
    slope_ref.send()
    turned_ref[...] = (total + dot(hidden.astype(BF16), downs[...])).T.astype(BF16)


def attend(info, features, valid, gain, qkv, out, next_gain, up, down):
    rows, width = features.shape
    half, own = rows // 2, rows // 4
    wide, hidden = qkv.shape[1], up.shape[1]
    return call(
        functools.partial(attend_kernel, head_dim=width // HEADS),
        "attend",
        info,
        (features, valid, gain, qkv, out, next_gain, up, down),
        [
            shape_of((own, width), BF16),
            shape_of((half, width), BF16),
            shape_of((half, wide), BF16),
            shape_of((half, half), F32),
            shape_of((half, width), BF16),
            shape_of((own, width), BF16),
            shape_of((own, hidden), BF16),
            shape_of((width, own), BF16),
        ],
        raw=(3, 4, 6, 7),
        far_in=(0, 1, 2, 5),
        far_out=(0, 1, 2, 3, 5, 6, 7),
        scratch=[
            pltpu.VMEM((width, wide), BF16),
            pltpu.VMEM((width, width), BF16),
            pltpu.VMEM((width, hidden), BF16),
            pltpu.VMEM((hidden, width), BF16),
            pltpu.SemaphoreType.DMA((4,)),
        ],
        vmem=56,
        micros=20,
    )


def attend_back_kernel(
    info_ref, grad, projected, mask, out_hbm, qkv_hbm,
    kept_ref, sent_ref, e_own_ref, e_sent_ref, out, weights, grads, sems, *, head_dim,
):
    rows, width = grad.shape
    own, quarter = rows // 2, width // 4
    heads = HEADS // 2
    wide = heads * head_dim
    scale = head_dim**-0.5
    near = info_ref[NEAR]
    first = pl.multiple_of(near * wide, wide)
    to_out = pltpu.make_async_copy(out_hbm.at[pl.ds(first, wide), :], out, sems.at[0])
    to_weights = [
        pltpu.make_async_copy(
            qkv_hbm.at[:, pl.ds(pl.multiple_of(first + k * width, wide), wide)],
            weights.at[:, pl.ds(k * wide, wide)],
            sems.at[1 + k],
        )
        for k in range(3)
    ]
    to_out.start()
    for one in to_weights:
        one.start()

    projected.wait()
    mask.wait()
    to_out.wait()
    pulled = dot_last(grad[...], out[...]).astype(BF16)
    allowed = mask[...] > 0

    def columns(which):
        return projected.ref[:, pl.ds(pl.multiple_of(first + which * width, wide), wide)]

    all_queries, all_keys, all_values = columns(0), columns(1), columns(2)
    for head in range(heads):
        at = slice(head * head_dim, (head + 1) * head_dim)
        queries, keys, values = all_queries[:, at], all_keys[:, at], all_values[:, at]
        shares = softmax_parts(queries, keys, allowed, scale)
        share_grad = dot_last(pulled[:, at], values)
        centre = jnp.sum(share_grad * shares, axis=-1, keepdims=True)
        score_grad = (shares * (share_grad - centre)).astype(BF16)
        grads[:, at] = (dot(score_grad, keys) * scale).astype(BF16)
        at = slice(wide + head * head_dim, wide + (head + 1) * head_dim)
        grads[:, at] = (dot_rows(score_grad, queries) * scale).astype(BF16)
        at = slice(2 * wide + head * head_dim, 2 * wide + (head + 1) * head_dim)
        grads[:, at] = dot_rows(shares.astype(BF16), pulled[:, head * head_dim : (head + 1) * head_dim]).astype(BF16)
    core = info_ref[CORE]
    for target, side in ((sent_ref, 1 - core), (kept_ref, core)):
        for k in range(3):
            place = pl.multiple_of(k * wide + side * (wide // 2), wide // 2)
            target[:, k * quarter : (k + 1) * quarter] = grads[:, pl.ds(place, wide // 2)]
        place = pl.multiple_of((side * 2 + near) * quarter, quarter)
        target[:, 3 * quarter :] = grad.ref[:, pl.ds(place, quarter)]
        target.send()
    for one in to_weights:
        one.wait()
    summed = dot_last(grads[...], weights[...])
    e_own_ref[...] = summed[:own]
    e_sent_ref[...] = summed[own:].astype(BF16)


def attend_back(info, projected, mask, own_grad, near_grad, out, qkv):
    own, width = own_grad.shape
    rows = 2 * own
    wide = width // 2
    return call(
        functools.partial(attend_back_kernel, head_dim=width // HEADS),
        "attend_back",
        info,
        (Joined((own_grad, 0, own), (near_grad, 0, own)), projected, mask, out, qkv),
        [
            shape_of((rows, width), BF16),
            shape_of((rows, width), BF16),
            shape_of((own, width), F32),
            shape_of((own, width), BF16),
        ],
        raw=(3, 4),
        far_in=(1, 2),
        scratch=[
            pltpu.VMEM((wide, width), BF16),
            pltpu.VMEM((width, 3 * wide), BF16),
            pltpu.VMEM((rows, 3 * wide), BF16),
            pltpu.SemaphoreType.DMA((4,)),
        ],
        vmem=24,
        micros=11,
        far_out=(0,),
    )


def last_kernel(info_ref, e_own_ref, e_near_ref, grad_ref, x_ref, gain_ref, *refs):
    pieces, held = refs[:-1], refs[-1]
    upstream = e_own_ref[...] + e_near_ref[...].astype(F32)
    normed, rate = normal_parts(x_ref[...].astype(F32))
    back = normal_back(normed, rate, upstream * gain_ref[...])
    held[...] = grad_ref[...].astype(F32) + back
    own, quarter = held.shape[0], pieces[0].shape[1]
    for mask in range(4):
        at = pl.multiple_of((info_ref[SECTION] ^ mask) * quarter, quarter)
        value = held[:, pl.ds(at, quarter)].astype(BF16)
        pieces[min(mask, 2)][(mask // 3) * own : (mask // 3 + 1) * own, :] = value


def last_norm(info, e_own, e_near, grad, x, gain, sections):
    own, width = x.shape
    return call(
        last_kernel,
        "last_norm",
        info,
        (e_own, e_near, grad, x, gain),
        [
            shape_of((own, width // sections), BF16),
            shape_of((own, width // sections), BF16),
            shape_of((2 * own, width // sections), BF16),
        ],
        scratch=[pltpu.VMEM((own, width), F32)],
        plain=True,
        micros=20,
        vmem=8,
    )


def place_kernel(info_ref, *refs, turned):
    pieces, out_ref = refs[:-1], refs[-1]
    rows = out_ref.shape[0]
    own = rows // 4
    at = lax.broadcasted_iota(jnp.int32, (own, 1), 0)
    total = None
    for mask, piece in enumerate(pieces):
        section = info_ref[SECTION] ^ mask
        pick = picked(group_row(info_ref, section >> 1, section & 1, at, rows), rows)
        if turned:
            part = lax.dot_general(
                pick, piece[...], (((0,), (1,)), ((), ())), preferred_element_type=F32
            )
        else:
            part = dot_rows(pick, piece[...])
        total = part if total is None else total + part
    out_ref[...] = total.astype(out_ref.dtype)


def placed(info, pieces, dtype, turned, micros=0):
    own = pieces[0].shape[1 if turned else 0]
    quarter = pieces[0].shape[0 if turned else 1]
    rows = own * len(pieces)
    return call(
        functools.partial(place_kernel, turned=turned),
        "placed",
        info,
        pieces,
        [shape_of((rows, quarter), dtype)],
        plain=True,
        micros=micros,
        vmem=8,
    )[0]


def part_copies(info_ref, weight_hbm, held, sems, part, axis):
    quarter = held.shape[axis]
    copies = []
    width = part if part % 128 == 0 else quarter
    for k in range(quarter // width):
        first = hidden_block(k, info_ref) * part if width == part else 0
        source, target = pl.ds(pl.multiple_of(first, width), width), pl.ds(k * width, width)
        if axis == 1:
            pair = weight_hbm.at[:, source], held.at[:, target]
        else:
            pair = weight_hbm.at[source, :], held.at[target, :]
        copies.append(pltpu.make_async_copy(*pair, sems.at[k]))
    for copy in copies:
        copy.start()
    return copies, width


def mixer_back_kernel(info_ref, grad, slope, first, gain, ups, downs, out_ref):
    pulled = dot_last(grad[...], downs[...])
    lifted = (slope[...].astype(F32) * pulled).astype(BF16)
    total = dot_last(lifted, ups[...])
    normed, rate = normal_parts(first[...].astype(F32))
    back = normal_back(normed, rate, total * gain[...])
    out_ref[...] = (grad[...].astype(F32) + back).astype(BF16)


def mixer_back(info, grad, slope, first, gain, up, down):
    return call(
        mixer_back_kernel,
        "mixer_back",
        info,
        (grad, slope, first, gain, up, down),
        [shape_of(grad.shape, BF16)],
        vmem=24,
        far_in=(1, 2, 3),
        near_in=(4, 5),
        micros=60,
    )[0]


def pool_kernel(info_ref, pool, up_hbm, hidden_ref, slope_ref, held, sems, *, part):
    copies, _ = part_copies(info_ref, up_hbm, held, sems, part, 1)
    for copy in copies:
        copy.wait()
    hidden, slope = smooth_pair(dot(pool[...], held[...]))
    hidden_ref[...] = hidden.astype(BF16)
    hidden_ref.send()
    slope_ref[...] = slope.astype(BF16)


def pool_forward(info, shared, up, blocks):
    own, width = shared[0].shape[0] // 2, shared[0].shape[1]
    hidden = up.shape[1]
    quarter, part = hidden // 4, hidden // blocks
    pool = Joined(*[(array, 0, own) for array in shared])
    return call(
        functools.partial(pool_kernel, part=part),
        "pool_forward",
        info,
        (pool, own_quarter(info, up, blocks, 1)),
        [shape_of((pool.shape[0], quarter), BF16)] * 2,
        scratch=[pltpu.VMEM((width, quarter), BF16), pltpu.SemaphoreType.DMA((blocks // 4,))],
        vmem=24,
        raw=(1,),
        far_out=(0, 1),
        micros=60,
    )


def hidden_block(at, info):
    return (((at // 2) * 2 + info[CORE]) * 2 + at % 2) * 2 + info[NEAR]


def own_quarter(info, weight, blocks, axis):
    part = weight.shape[axis] // blocks
    if part % 128 == 0:
        return weight
    order = hidden_block(jnp.arange(blocks // 4), info)
    shape = weight.shape[:axis] + (blocks, part) + weight.shape[axis + 1 :]
    taken = jnp.take(weight.reshape(shape), order, axis=axis)
    return taken.reshape(weight.shape[:axis] + (-1,) + weight.shape[axis + 1 :])


def split_place(position, bit):
    chip, far = position >> 1, position & 1
    low = chip & ((1 << bit) - 1)
    rest = ((chip >> (bit + 1)) << bit) | low
    return (chip >> bit) & 1, rest * 2 + far


def halves_like(positions, rows, columns):
    return [shape_of((positions, rows, columns // 2), BF16)] * 2


def down_kernel(info_ref, grad, hidden, *refs, part, bits):
    outs, held = refs[:-1], refs[-1]
    grad.wait()
    held[...] = dot_rows(hidden[...], grad[...])
    store_positions(info_ref, outs, held, bits, (part, 1))


def down_gradient(info, hidden, grads, blocks, bits):
    pool, quarter = hidden.shape
    own, width = grads[0].shape
    part = quarter * 4 // blocks
    like = halves_like(blocks // 4, part, width)
    return call(
        functools.partial(down_kernel, part=part, bits=bits),
        "down_gradient",
        info,
        (Joined(*[(array, 0, own) for array in grads]), hidden),
        like,
        scratch=[pltpu.VMEM((quarter, width), F32)],
        vmem=20,
        micros=20,
        far_in=(1,),
    )


def store_positions(info_ref, outs, held, bits, layout):
    rest, quads = layout
    positions = held.shape[0] // (rest * quads)
    columns = held.shape[1] // 2
    own_place = info_ref[CHIP] * 2 + info_ref[FAR]
    for position in range(positions):
        source = position ^ own_place
        for quad in range(quads):
            if quads == 1:
                block = source
            else:
                block = (((source >> 1) * 2 + quad // 2) * 2 + (source & 1)) * 2 + quad % 2
            rows = pl.ds(pl.multiple_of(block * rest, rest), rest)
            for side, bit in enumerate((0, bits - 1)):
                goes, place = split_place(position, bit)
                place += side * positions // 2
                value = held[rows, side * columns : (side + 1) * columns]
                outs[goes][place, quad * rest : (quad + 1) * rest, :] = value.astype(BF16)


def up_kernel(info_ref, grad, slope, normed, down_hbm, *refs, part, bits):
    outs, (weight, lifted, total, sems) = refs[:2], refs[2:]
    copies, _ = part_copies(info_ref, down_hbm, weight, sems, part, 0)
    for copy in copies:
        copy.wait()
    pulled = dot_last(grad[...], weight[...])
    lifted[...] = (slope[...].astype(F32) * pulled).astype(BF16)
    total[...] = dot_rows(normed[...], lifted[...])
    store_positions(info_ref, outs, total, bits, (outs[0].shape[1] // 4, 4))


def up_gradient(info, slope, shared, grads, down, blocks, bits):
    pool, quarter = slope.shape
    hidden, width = down.shape
    own = grads[0].shape[0]
    like = halves_like(blocks // 4, width * 4 // blocks, quarter)
    return call(
        functools.partial(up_kernel, part=hidden // blocks, bits=bits),
        "up_gradient",
        info,
        (
            Joined(*[(array, 0, own) for array in grads]),
            slope,
            Joined(*[(array, 0, own) for array in shared]),
            own_quarter(info, down, blocks, 0),
        ),
        like,
        raw=(3,),
        scratch=[
            pltpu.VMEM((quarter, width), BF16),
            pltpu.VMEM((pool, quarter), BF16),
            pltpu.VMEM((width, quarter), F32),
            pltpu.SemaphoreType.DMA((blocks // 4,)),
        ],
        vmem=28,
        micros=8,
        far_in=(1, 2),
    )


def attend_grad_kernel(info_ref, normed, mixed, packs, *refs, bits):
    outs, total = refs[:-1], refs[-1]
    edge = total.shape[1] * 3 // 4
    total[:, :edge] = dot_rows(normed[...], packs[:, :edge])
    total[:, edge:] = dot_rows(mixed[...], packs[:, edge:])
    store_positions(info_ref, outs, total, bits, (outs[0].shape[1] // 4, 4))


def attend_gradient(info, normed, shared, packs, blocks, bits):
    half, width = normed[0].shape
    columns = packs[0].shape[1]
    own = half // 2
    like = halves_like(blocks // 4, width * 4 // blocks, columns)
    return call(
        functools.partial(attend_grad_kernel, bits=bits),
        "attend_gradient",
        info,
        (
            Joined(*[(array, 0, half) for array in normed]),
            Joined(*[(array, own, own) for array in shared]),
            Joined(*[(array, 0, half) for array in packs], far=(0,)),
        ),
        like,
        scratch=[pltpu.VMEM((width, columns), F32)],
        vmem=20,
        micros=0,
        far_in=(0, 1),
    )


def by_quad(info_ref, pieces):
    near, core = info_ref[NEAR] == 0, info_ref[CORE] == 0
    low = [jnp.where(near, pieces[k], pieces[k ^ 1]) for k in range(4)]
    return [jnp.where(core, low[k], low[k ^ 2]) for k in range(4)]


def gain_row(weight, grad, gain):
    total = jnp.sum(weight.astype(F32) * grad, axis=1, keepdims=True)
    eye = lax.broadcasted_iota(jnp.int32, (total.shape[0],) * 2, 0) == lax.broadcasted_iota(
        jnp.int32, (total.shape[0],) * 2, 1
    )
    return jnp.sum(jnp.where(eye, total, 0.0), axis=0, keepdims=True) / gain


def finish_kernel(info_ref, *refs, part, small, came):
    small_ref, came_ref, up_weight, qkv_weight, up_gain, qkv_gain = refs[4:10]
    up_ref, up_gain_ref, qkv_ref, out_ref, qkv_gain_ref = refs[10:15]
    pieces = by_quad(info_ref, [ref[...].astype(F32) for ref in refs[:4]])
    hidden = up_ref.shape[1] // 4
    quarter = out_ref.shape[1] // 4
    blocks = []
    for chip in range(hidden // (2 * part)):
        for core in range(2):
            for far in range(2):
                for near in range(2):
                    at = (chip * 2 + far) * part
                    blocks.append(pieces[core * 2 + near][:, at : at + part])
    up_ref[...] = jnp.concatenate(blocks, axis=1)
    for which in range(3):
        for near in range(2):
            for core in range(2):
                at = ((which * 2 + near) * 2 + core) * quarter
                source = hidden + which * quarter
                qkv_ref[:, at : at + quarter] = pieces[core * 2 + near][:, source : source + quarter]
    for k, piece in enumerate(pieces):
        out_ref[:, k * quarter : (k + 1) * quarter] = piece[:, hidden + 3 * quarter :]
    up_gain_ref[...] = gain_row(up_weight[...], up_ref[...], up_gain[...])
    qkv_gain_ref[...] = gain_row(qkv_weight[...], qkv_ref[...], qkv_gain[...])
    blocks = []
    for k in range(small[1]):
        blocks.append(small_ref[small[0] + k] + came_ref[came + k].astype(F32))
    column_finish(jnp.concatenate(blocks, axis=0), refs[15:])


def finish(info, pieces, sums, up, qkv, up_gain, qkv_gain, part, width, column_hidden):
    rest, hidden = up.shape
    wide = qkv.shape[1]
    shapes = [(rest, hidden), (1, rest), (rest, wide), (rest, wide // 3), (1, rest)]
    shapes += [(1, width), (width, 3 * width), (width, width), (1, width)]
    shapes += [(width, column_hidden)] * 2
    (small, small_at), count = sums.small
    handle, came_at = sums.small_sent
    results = call(
        functools.partial(finish_kernel, part=part, small=(small_at, count), came=came_at),
        "finish",
        info,
        (*pieces, small, sums.messages[handle], up, qkv, up_gain[None], qkv_gain[None]),
        [shape_of(dims, F32) for dims in shapes],
        plain=True,
        vmem=12,
    )
    up_grad, up_gain_grad, qkv_grad, out_grad, qkv_gain_grad, *columns = results
    columns[0], columns[3], columns[5] = columns[0][0], columns[3][0], columns[5].T
    return up_grad, up_gain_grad[0], qkv_grad, out_grad, qkv_gain_grad[0], columns


def ordered(arrays, *before):
    count = len(arrays)
    return lax.optimization_barrier((*arrays, *before))[:count]


def step_kernel(info_ref, *refs, inputs, adds, copies, ends, small):
    ins, outs = refs[:inputs], refs[inputs:]

    def value(kept, came, k):
        total = ins[kept[0]][kept[1] + k].astype(F32)
        if came is None:
            return total
        return total + ins[came[0]][came[1] + k].astype(F32)

    for kept, came, count, place, keep, sent in adds:
        for k in range(count):
            total = value(kept, came, k)
            to = ((k >> (place + 1)) << place) | (k & ((1 << place) - 1))
            if (k >> place) & 1:
                outs[sent[0]][sent[1] + to] = total.astype(BF16)
            else:
                outs[keep[0]][keep[1] + to] = total
    for source, count, target in copies:
        for k in range(count):
            outs[target[0]][target[1] + k] = ins[source[0]][source[1] + k]
    for end, sides in ends:
        columns = outs[end].shape[1] // 2
        for side, (kept, came) in enumerate(sides):
            outs[end][:, side * columns : (side + 1) * columns] = value(kept, came, 0)
    for kept, came, count, keep, sent in small:
        for k in range(count):
            if came is not None and len(came) == 4:
                far, first, half, size = came
                at = [pl.ds(first + side * half + k * size, size) for side in range(2)]
                other = jnp.concatenate([ins[far][rows, :] for rows in at], axis=1)
                total = ins[kept[0]][k * size : (k + 1) * size, :] + other.astype(F32)
            else:
                total = value(kept, came, k)
            outs[keep[0]][keep[1] + k] = total
            if sent is not None:
                outs[sent[0]][sent[1] + k] = total.astype(BF16)


class Sums:
    def __init__(self, info, bits, block):
        self.info, self.bits, self.block = info, bits, block
        self.gradients, self.messages, self.held = {}, [], {}
        self.small, self.small_sent, self.small_route = None, None, [*range(bits), "near", "core"]
        self.fresh = None

    def step(
        self, *advance, new=None, far_at=None, small=False, hold=(), before=(), micros=0
    ):
        with_small = small
        arrays, outs, adds, copies, ends = [], [], [], [], []
        sends, kept_count, kept_by, finished, small = {}, 0, [], [], []

        def given(array):
            for k, other in enumerate(arrays):
                if other is array:
                    return k
            arrays.append(array)
            return len(arrays) - 1

        def made(shape):
            outs.append(shape)
            return len(outs) - 1

        def to_send(key, count):
            at = sends.get(key, 0)
            sends[key] = at + count
            return key, at

        def to_keep(count):
            nonlocal kept_count
            kept_count += count
            return kept_count - count

        def there(kept):
            return given(kept[0]), kept[1]

        moving = [self.gradients[name] for name in advance]
        needed = {side["sent"][0] for one in moving for side in one}
        if with_small and self.small_sent is not None:
            needed.add(self.small_sent[0])
        needed = sorted(needed)
        came = ordered([self.messages[at] for at in needed], *before) if needed else ()
        came_at = {at: given(array) for at, array in zip(needed, came)}

        def arrived(sent):
            return None if sent is None else (came_at[sent[0]], sent[1])

        block = self.block
        for name, one in zip(advance, moving):
            if not one[0]["route"]:
                end = made(shape_of((block[0], 2 * block[1]), F32))
                ends.append((end, [(there(s["kept"]), arrived(s["sent"])) for s in one]))
                del self.gradients[name]
                continue
            for side in one:
                key = side["route"].pop(0)
                if key == "far":
                    place, side["below"] = 0, 0
                else:
                    place = len(side["left"]) - 1 - side["left"].index(key) + side["below"]
                    side["left"].remove(key)
                entry = [there(side["kept"]), arrived(side["sent"]), side["count"], place]
                side["count"] //= 2
                side["sent"] = to_send(key, side["count"])
                kept_by.append((side, entry, to_keep(side["count"])))
        sent_sides = [side for side, _, _ in kept_by]
        if new is not None:
            name, (kept, sent) = new
            one, count = [], kept.shape[0] // 2
            for number in range(2):
                order = tuple(range(self.bits))
                order = order if number == 0 else order[::-1]
                route = list(order[1:])
                route.insert(self.bits if far_at is None else far_at - 1, "far")
                side = {
                    "route": route,
                    "below": 1,
                    "left": [bit for bit in range(self.bits - 1, -1, -1) if bit != order[0]],
                    "kept": (kept, number * count),
                    "count": count,
                    "sent": to_send(order[0], count),
                }
                copies.append(((given(sent), number * count), count, side["sent"]))
                one.append(side)
            self.gradients[name] = one
            sent_sides += one
        if with_small:
            kept, count = self.small
            entry = [there(kept), arrived(self.small_sent), count, to_keep(count)]
            if self.fresh is not None:
                far, first = self.fresh
                entry[1] = (given(far), first, kept[0].shape[0], block[0])
                self.fresh = None
            self.small_sent = None
            if self.small_route:
                self.small_sent = to_send(self.small_route.pop(0), count)
            small.append((*entry, self.small_sent))
        keys = sorted(sends, key=str)
        sent_out = {key: made(shape_of((sends[key], *block), BF16)) for key in keys}
        if kept_count:
            kept_out = made(shape_of((kept_count, *block), F32))

        def target(sent):
            return None if sent is None else (sent_out[sent[0]], sent[1])

        adds = [(*entry, (kept_out, at), target(side["sent"])) for side, entry, at in kept_by]
        copies = [(source, count, target(sent)) for source, count, sent in copies]
        small = [(*entry[:3], (kept_out, entry[3]), target(entry[4])) for entry in small]
        results = call(
            functools.partial(
                step_kernel, inputs=len(arrays), adds=adds, copies=copies, ends=ends, small=small
            ),
            "sums_step",
            self.info,
            tuple(arrays),
            outs,
            vmem=12,
            plain=True,
            micros=micros,
        )
        for side, _, at in kept_by:
            side["kept"] = (results[kept_out], at)
        handles = {}
        for key in keys:
            handles[key] = len(self.messages)
            self.messages.append(None)
            self.held[handles[key]] = (key, results[sent_out[key]])
            if key not in hold:
                self.release(handles[key])
        for side in sent_sides:
            side["sent"] = (handles[side["sent"][0]], side["sent"][1])
        if with_small:
            self.small = ((results[kept_out], small[0][3][1]), self.small[1])
            if self.small_sent is not None:
                self.small_sent = (handles[self.small_sent[0]], self.small_sent[1])
        self.sent = [results[sent_out[key]] for key in keys]
        self.handles = handles
        return [results[end] for end, _ in ends]

    def release(self, handle, *before):
        key, array = self.held.pop(handle)
        (array,) = ordered((array,), *before)
        places = {"far": ("section", 2), "near": ("section", 1), "core": ("dp", 1)}
        axis, mask = places[key] if key in places else ("dp", 2 << key)
        self.messages[handle] = exchanged(array, axis, mask)


def quad_kernel(info_ref, *refs, inputs, sides, rest):
    ins, pieces, held = refs[:inputs], refs[inputs:-1], refs[-1]
    columns = held.shape[1] // len(sides)
    for k, (kept, came) in enumerate(sides):
        total = ins[kept[0]][kept[1]] + ins[came[0]][came[1]].astype(F32)
        held[:, k * columns : (k + 1) * columns] = total
    own = info_ref[CORE] * 2 + info_ref[NEAR]
    for mask, piece in enumerate(pieces):
        rows = pl.ds(pl.multiple_of((own ^ mask) * rest, rest), rest)
        piece[...] = held[rows, :].astype(BF16)


def quad_pieces(info, sums, names, rest):
    arrays = []

    def there(place):
        for k, other in enumerate(arrays):
            if other is place[0]:
                return k, place[1]
        arrays.append(place[0])
        return len(arrays) - 1, place[1]

    sides = [
        (there(side["kept"]), there((sums.messages[side["sent"][0]], side["sent"][1])))
        for name in names
        for side in sums.gradients[name]
    ]
    block, columns = sums.block
    return call(
        functools.partial(quad_kernel, inputs=len(arrays), sides=sides, rest=rest),
        "quad_pieces",
        info,
        tuple(arrays),
        [shape_of((rest, columns * len(sides)), BF16)] * 4,
        scratch=[pltpu.VMEM((block, columns * len(sides)), F32)],
        plain=True,
        vmem=8,
    )


TOGETHER = 4


def one_hot(rows, columns, row_of_column):
    row = lax.broadcasted_iota(jnp.int32, (rows, columns), 0)
    column = lax.broadcasted_iota(jnp.int32, (rows, columns), 1)
    return jnp.where(row == row_of_column(column), 1.0, 0.0).astype(BF16)


def head_order(count, small):
    heads, width = HEADS_ATTR, HEADS_ATTR * small

    def row_of(column):
        inside = column % width
        return column - inside + (inside % small) * heads + inside // small

    return one_hot(count, count, row_of)


def column_kernel(
    info_ref,
    cells_ref,
    cotangent,
    gain_ref,
    qkv_ref,
    out_ref,
    mix_gain_ref,
    up_ref,
    down_t_ref,
    mixer_up_hbm,
    mixer_down_hbm,
    *refs,
    width,
    small,
    sections,
):
    results = refs[:3]
    cells_grad_ref, sums_ref, mixer_up_ref, mixer_down_ref = refs[3:7]
    (
        projected,
        normed_low,
        shares_kept,
        score_grads,
        mixed,
        mixed_grad,
        sum_grad,
        turned_grad,
        upstream_all,
        gain_sum,
        mix_gain_sum,
        gain_wide,
        mix_gain_wide,
        qkv_group,
        out_group,
        out_group_t,
        up_group_t,
        down_group,
        qkv_heads,
        mixer_sems,
    ) = refs[7:]
    to_mixer = [
        pltpu.make_async_copy(mixer_up_hbm, mixer_up_ref, mixer_sems.at[0]),
        pltpu.make_async_copy(mixer_down_hbm, mixer_down_ref, mixer_sems.at[1]),
    ]
    lanes = cells_ref.shape[1]
    hidden_width = up_ref.shape[1]
    heads = HEADS_ATTR
    scale = small**-0.5
    lane_blocks = lanes // 128
    group = ATTR // sections
    wide = group * width
    up_at = (slice(0, width), slice(0, hidden_width))
    down_at = (slice(0, width), slice(hidden_width, 2 * hidden_width))
    qkv_at = (slice(width, 2 * width), slice(0, 3 * width))
    out_at = (slice(width, 2 * width), slice(3 * width, 4 * width))
    gain_at = (slice(width, 2 * width), slice(4 * width, 4 * width + 128))

    spread = one_hot(width, wide, lambda column: column % width)

    def diagonal(lanes_tiled):
        tiled = jnp.concatenate([lanes_tiled] * group, axis=0)
        row = lax.broadcasted_iota(jnp.int32, tiled.shape, 0) // lanes_tiled.shape[0]
        column = lax.broadcasted_iota(jnp.int32, tiled.shape, 1) // width
        return jnp.where(row == column, tiled, 0.0)

    triple = head_order(3 * width, small)
    qkv_heads[...] = dot_last(qkv_ref[...], triple).astype(BF16)
    qkv_group[...] = diagonal(dot(dot_last(triple, qkv_ref[...]).astype(BF16), spread)).astype(BF16)
    out_heads = dot(head_order(width, small), out_ref[...]).astype(BF16)
    out_wide = diagonal(dot(out_heads, spread))
    out_group[...] = out_wide.astype(BF16)
    out_group_t[...] = out_wide.T.astype(BF16)
    up_group_t[...] = diagonal(dot_rows(up_ref[...], spread)).astype(BF16)
    down_group[...] = diagonal(dot_rows(down_t_ref[...], spread)).astype(BF16)
    eye = lax.broadcasted_iota(jnp.int32, (width, width), 0) == lax.broadcasted_iota(
        jnp.int32, (width, width), 1
    )
    for ref, kept in ((gain_ref, gain_wide), (mix_gain_ref, mix_gain_wide)):
        column = jnp.sum(jnp.where(eye, ref[...], 0.0), axis=1, keepdims=True)
        kept[...] = jnp.broadcast_to(column, (width, lanes))

    sums_ref[...] = jnp.zeros(sums_ref.shape, F32)
    gain_sum[...] = jnp.zeros_like(gain_sum)
    mix_gain_sum[...] = jnp.zeros_like(mix_gain_sum)

    def at_group(g):
        if isinstance(g, int):
            return slice(g * wide, (g + 1) * wide)
        return pl.ds(pl.multiple_of(g * wide, wide), wide)

    def at_rows(a):
        return pl.ds(pl.multiple_of(a * width, width), width)

    def apart(value):
        return value.reshape(group, width, lanes)

    def each(value):
        size = value.shape[0] // group
        return [value[k * size : (k + 1) * size] for k in range(group)]

    def along(value):
        return jnp.concatenate(each(value), axis=1)

    cells_ref.wait()

    for g in range(sections):
        normed, _ = normal_parts(apart(cells_ref[at_group(g), :].astype(F32)), 1)
        low = (normed * gain_wide[...][None]).astype(BF16).reshape(wide, lanes)
        normed_low[at_group(g), :] = low
        part = dot(qkv_group[...], low).astype(BF16).astype(F32)
        projected[pl.ds(g * group, group)] = part.reshape(group, 3, small, heads, lanes)

    for block in range(lane_blocks):
        here = slice(block * 128, block * 128 + 128)

        @pl.loop(0, ATTR, step=TOGETHER)
        def _(first):
            several = range(TOGETHER)
            queries = [projected[first + k, 0, :, :, here] for k in several]
            scores = [[] for _ in several]
            for b in range(ATTR):
                key = projected[b, 1, :, :, here]
                for k in several:
                    scores[k].append(jnp.sum(queries[k] * key, axis=0) * scale)
            shares = []
            for k in several:
                peak = functools.reduce(jnp.maximum, scores[k])
                lifted = [jnp.exp(score - peak) for score in scores[k]]
                rate = 1.0 / functools.reduce(jnp.add, lifted)
                shares.append([each_one * rate for each_one in lifted])
                for b in range(ATTR):
                    shares_kept[first + k, b, :, here] = shares[k][b]
            totals = [None for _ in several]
            for b in range(ATTR):
                value = projected[b, 2, :, :, here]
                for k in several:
                    term = shares[k][b].astype(BF16).astype(F32)[None] * value
                    totals[k] = term if totals[k] is None else totals[k] + term
            for k in several:
                mixed[at_rows(first + k), here] = totals[k].reshape(width, 128).astype(BF16)

    cotangent.wait()
    for one in to_mixer:
        one.start()

    rows = cotangent.shape[0]
    source = group_row(
        info_ref,
        info_ref[FAR],
        info_ref[NEAR],
        lax.broadcasted_iota(jnp.int32, (1, lanes), 1),
        rows,
    )
    at = lax.broadcasted_iota(jnp.int32, (rows, lanes), 0)
    pick = jnp.where(at == source, 1.0, 0.0).astype(BF16)
    upstream_all[...] = dot_rows(cotangent[...], pick).astype(BF16)

    for piece in range(sections):
        g = info_ref[SECTION] ^ piece
        here = at_group(g)
        mixed_low = mixed[here, :]
        third = cells_ref[here, :].astype(F32) + dot(out_group_t[...], mixed_low)
        third = third.astype(BF16).astype(F32)
        normed, rate = normal_parts(apart(third), 1)
        low = (normed * mix_gain_wide[...][None]).astype(BF16).reshape(wide, lanes)
        hidden, slope = smooth_pair(dot(up_group_t[...], low))
        hidden = hidden.astype(BF16)
        change = jnp.concatenate([dot(down_t_ref[...], each_one) for each_one in each(hidden)], axis=0)
        result = (third + change).astype(BF16)
        results[min(piece, 2)][(piece // 3) * wide : (piece // 3 + 1) * wide, :] = result
        upstream = upstream_all[here, :]
        sums_ref[down_at] += dot_last(along(upstream), along(hidden))
        lifted_grad = (slope * dot(down_group[...], upstream)).astype(BF16)
        sums_ref[up_at] += dot_last(along(low), along(lifted_grad))
        normed_grad = apart(
            jnp.concatenate([dot(up_ref[...], each_one) for each_one in each(lifted_grad)], axis=0)
        )
        mix_gain_sum[...] += jnp.sum(normed_grad * normed, axis=0)
        back = normal_back(normed, rate, normed_grad * mix_gain_wide[...][None], 1)
        third_grad = (upstream.astype(F32) + back.reshape(wide, lanes)).astype(BF16)
        sum_grad[here, :] = third_grad
        sums_ref[out_at] += dot_last(along(third_grad), along(mixed_low))
        part = dot(out_group[...], third_grad).astype(BF16).astype(F32)
        mixed_grad[pl.ds(g * group, group)] = part.reshape(group, small, heads, lanes)

    for block in range(lane_blocks):
        here = slice(block * 128, block * 128 + 128)

        @pl.loop(0, ATTR, step=TOGETHER)
        def _(first):
            several = range(TOGETHER)
            pulled = [mixed_grad[first + k, :, :, here] for k in several]
            share_grads = [[] for _ in several]
            for b in range(ATTR):
                value = projected[b, 2, :, :, here]
                for k in several:
                    share_grads[k].append(jnp.sum(pulled[k] * value, axis=0))
            grads = []
            for k in several:
                shares = [shares_kept[first + k, b, :, here] for b in range(ATTR)]
                products = [s * g for s, g in zip(shares, share_grads[k])]
                centre = functools.reduce(jnp.add, products)
                grads.append([])
                for b in range(ATTR):
                    grad = (products[b] - shares[b] * centre).astype(BF16).astype(F32)
                    score_grads[first + k, b, :, here] = grad
                    shares_kept[first + k, b, :, here] = shares[b].astype(BF16).astype(F32)
                    grads[k].append(grad)
            totals = [None for _ in several]
            for b in range(ATTR):
                key = projected[b, 1, :, :, here]
                for k in several:
                    term = grads[k][b][None] * key
                    totals[k] = term if totals[k] is None else totals[k] + term
            for k in several:
                total = (totals[k] * scale).reshape(width, 128)
                mixed[at_rows(first + k), here] = total.astype(BF16)

        @pl.loop(0, ATTR, step=TOGETHER)
        def _(first):
            several = range(TOGETHER)
            key_grads = [None for _ in several]
            value_grads = [None for _ in several]
            for a in range(ATTR):
                query, pulled = projected[a, 0, :, :, here], mixed_grad[a, :, :, here]
                for k in several:
                    term = score_grads[a, first + k, :, here][None] * query
                    key_grads[k] = term if a == 0 else key_grads[k] + term
                    term = shares_kept[a, first + k, :, here][None] * pulled
                    value_grads[k] = term if a == 0 else value_grads[k] + term
            for k in several:
                projected[first + k, 1, :, :, here] = key_grads[k] * scale
                projected[first + k, 2, :, :, here] = value_grads[k]

    for g in range(sections):
        here = at_group(g)
        query_grads = each(mixed[here, :])
        grads = []
        for k in range(group):
            key_value = projected[g * group + k, 1:3].reshape(2 * width, lanes).astype(BF16)
            grads.append(jnp.concatenate([query_grads[k], key_value], axis=0))
        sums_ref[qkv_at] += dot_last(
            along(normed_low[here, :]), jnp.concatenate(grads, axis=1)
        )
        normed_grad = jnp.concatenate([dot(qkv_heads[...], grad) for grad in grads], axis=0)
        normed_grad = apart(normed_grad)
        normed, rate = normal_parts(apart(cells_ref[here, :].astype(F32)), 1)
        gain_sum[...] += jnp.sum(normed_grad * normed, axis=0)
        back = normal_back(normed, rate, normed_grad * gain_wide[...][None], 1)
        turned_grad[here, :] = sum_grad[here, :].astype(F32) + back.reshape(wide, lanes)

    cells_grad_ref[...] = turned_grad[...].T.astype(BF16)
    lane = lax.broadcasted_iota(jnp.int32, (width, 128), 1)
    first = jnp.sum(gain_sum[...], axis=1, keepdims=True)
    second = jnp.sum(mix_gain_sum[...], axis=1, keepdims=True)
    sums_ref[gain_at] = jnp.where(
        lane == 0, first, jnp.where(lane == 1, second, 0.0)
    )
    rows = sums_ref.shape[0]
    for half in range(2):
        at = 2 * wide + half * rows
        part = sums_ref[:, half * hidden_width : (half + 1) * hidden_width]
        results[2][at : at + rows, :] = part.astype(BF16)
    for one in to_mixer:
        one.wait()


def column_layers(
    info, cells, cotangent, gain, qkv, out, mix_gain, up, down, mixer_up, mixer_down, sections
):
    depth, lanes = cells.shape
    width = depth // ATTR
    small = width // HEADS_ATTR
    hidden = up.shape[1]
    wide = width * (ATTR // sections)
    piece = depth // sections
    out_shape = [
        shape_of((piece, lanes), BF16),
        shape_of((piece, lanes), BF16),
        shape_of((2 * piece + 4 * width, lanes), BF16),
        shape_of((lanes, depth), BF16),
        shape_of((2 * width, 2 * hidden), F32),
        shape_of(mixer_up.shape, BF16),
        shape_of(mixer_down.shape, BF16),
    ]
    arrays = (
        cells, cotangent, gain[None], qkv, out, mix_gain[None], up, down.T, mixer_up, mixer_down
    )
    results = call(
        functools.partial(column_kernel, width=width, small=small, sections=sections),
        "column_layers",
        info,
        arrays,
        out_shape,
        scratch=[
            pltpu.VMEM((ATTR, 3, small, HEADS_ATTR, lanes), F32),
            pltpu.VMEM((depth, lanes), BF16),
            pltpu.VMEM((ATTR, ATTR, HEADS_ATTR, lanes), F32),
            pltpu.VMEM((ATTR, ATTR, HEADS_ATTR, lanes), F32),
            pltpu.VMEM((depth, lanes), BF16),
            pltpu.VMEM((ATTR, small, HEADS_ATTR, lanes), F32),
            pltpu.VMEM((depth, lanes), BF16),
            pltpu.VMEM((depth, lanes), F32),
            pltpu.VMEM((depth, lanes), BF16),
            pltpu.VMEM((width, lanes), F32),
            pltpu.VMEM((width, lanes), F32),
            pltpu.VMEM((width, lanes), F32),
            pltpu.VMEM((width, lanes), F32),
            pltpu.VMEM((3 * wide, wide), BF16),
            pltpu.VMEM((wide, wide), BF16),
            pltpu.VMEM((wide, wide), BF16),
            pltpu.VMEM((hidden * wide // width, wide), BF16),
            pltpu.VMEM((hidden * wide // width, wide), BF16),
            pltpu.VMEM((width, 3 * width), BF16),
            pltpu.SemaphoreType.DMA((2,)),
        ],
        vmem=26,
        raw=(8, 9),
        near_out=(5, 6),
        far_in=(0, 1),
        micros=24,
    )
    return results[:3], *results[3:]


def column_finish(sums, refs):
    gain_ref, qkv_ref, out_ref, mix_gain_ref, up_ref, down_t_ref = refs
    width, hidden = up_ref.shape
    small = width // HEADS_ATTR
    up_ref[...] = sums[:width, :hidden]
    down_t_ref[...] = sums[:width, hidden : 2 * hidden]
    low = sums[width : 2 * width]
    qkv_ref[...] = jnp.dot(
        low[:, : 3 * width],
        head_order(3 * width, small).astype(F32),
        precision=lax.Precision.HIGHEST,
        preferred_element_type=F32,
    )
    out_ref[...] = lax.dot_general(
        head_order(width, small).astype(F32),
        low[:, 3 * width : 4 * width],
        (((0,), (1,)), ((), ())),
        precision=lax.Precision.HIGHEST,
        preferred_element_type=F32,
    )
    eye = lax.broadcasted_iota(jnp.int32, (width, width), 0) == lax.broadcasted_iota(
        jnp.int32, (width, width), 1
    )
    for k, ref in enumerate((gain_ref, mix_gain_ref)):
        at = 4 * width + k
        ref[...] = jnp.sum(jnp.where(eye, low[:, at : at + 1], 0.0), axis=0, keepdims=True)


def body(
    features,
    cotangent,
    row_counts,
    key_valid,
    attend_gain,
    attend_qkv,
    attend_out,
    mixer_gain,
    mixer_up,
    mixer_down,
    column_gain,
    column_qkv,
    column_out,
    column_mix_gain,
    column_up,
    column_down,
):
    dp_count, sections = lax.axis_size("dp"), lax.axis_size("section")
    dp_at, section_at = lax.axis_index("dp"), lax.axis_index("section")
    core, near, far = dp_at & 1, section_at & 1, section_at >> 1
    bits = (dp_count // 2).bit_length() - 1
    blocks = dp_count * sections
    group_rows, width = features.shape
    hidden = mixer_up.shape[1]
    entries = (core, near, far, dp_at >> 1, section_at)
    lane = lax.iota(jnp.int32, COUNTS)
    place = sum(jnp.where(lane == k, entry.astype(jnp.int32), 0) for k, entry in enumerate(entries))
    info = jnp.concatenate([place, row_counts[0]])

    def near_of(array):
        return exchanged(array, "section", 1)

    def core_of(array):
        return exchanged(array, "dp", 1)

    own_x, half_normed, projected, mask, shared, first, slope, second_t = attend(
        info, features, key_valid[None], attend_gain[None], attend_qkv, attend_out,
        mixer_gain[None], mixer_up, mixer_down,
    )
    shared_near, shared_core = near_of(shared), core_of(shared)
    half_core = core_of(half_normed)

    result_pieces, second_grad, column_sums, near_up, near_down = column_layers(
        info, second_t, cotangent, column_gain, column_qkv, column_out, column_mix_gain,
        column_up, column_down, mixer_up, mixer_down, sections,
    )
    shared_near, shared_core, half_core = ordered(
        (shared_near, shared_core, half_core), second_grad
    )
    grad_near, grad_core = near_of(second_grad), core_of(second_grad)
    shared_both = core_of(shared_near)

    first_grad = mixer_back(
        info, second_grad, slope, first, mixer_gain[None], near_up, near_down
    )
    first_near = near_of(first_grad)

    pool = ordered((shared, shared_near, shared_core, shared_both), first_grad)
    pool_hidden, pool_slope = pool_forward(info, pool, mixer_up, blocks)
    (grad_core,) = ordered((grad_core,), pool_hidden)
    (grad_near,) = ordered((grad_near,), pool_hidden)
    second_pool = (second_grad, grad_near, grad_core, core_of(grad_near))
    down_parts = down_gradient(info, pool_hidden, second_pool, blocks, bits)
    result_far = exchanged(result_pieces[2], "section", 2)
    sums = Sums(info, bits, down_parts[0].shape[1:])
    sums.step(new=("down", down_parts), far_at=1)
    (slope_later,) = ordered((pool_slope,), *sums.sent)
    up_parts = up_gradient(info, slope_later, pool, second_pool, mixer_down, blocks, bits)
    quarter = width // sections
    sums.small = (column_sums, 0), column_sums.shape[0] // sums.block[0]
    sums.fresh = result_far, 2 * quarter

    sums.step("down", new=("up", up_parts), small=True, hold=("far",))
    down_far = sums.handles["far"]
    first_near, own_grad = ordered((first_near, first_grad), *sums.sent)
    near_pieces = ordered((result_pieces[1], result_far[quarter : 2 * quarter]), *sums.sent)
    result_near = near_of(jnp.concatenate(near_pieces, axis=0))
    kept, sent, e_own, e_sent = attend_back(
        info, projected, mask, own_grad, first_near, attend_out, attend_qkv
    )
    sent_came = core_of(sent)
    sums.release(down_far, kept)
    sums.step("up", small=True, before=(result_near,), micros=40)
    settled = sums.sent
    (sent_came,) = ordered((sent_came,), *settled)
    attend_parts = attend_gradient(
        info, (half_normed, half_core), pool, (kept, sent_came), blocks, bits
    )
    (e_sent,) = ordered((e_sent,), *settled)
    e_near = near_of(e_sent)
    sums.step(new=("attend", attend_parts))
    for _ in range(bits - 1):
        sums.step("up", small=True, before=sums.sent)
    (e_near,) = ordered((e_near,), sums.messages[down_far], *sums.sent)
    input_pieces = last_norm(
        info, e_own, e_near, first_grad, own_x, attend_gain[None], sections
    )
    far_came = exchanged(input_pieces[2], "section", 2)
    for _ in range(bits - 1):
        sums.step("down", "attend", before=input_pieces[:1])
    up_far = sums.messages[sums.gradients["up"][0]["sent"][0]]
    (result_near,) = ordered((result_near,), *sums.sent)
    pieces = [result_pieces[0], result_near[:quarter], result_far[:quarter], result_near[quarter:]]
    result = placed(info, pieces, features.dtype, True, 20)
    (mixer_down_grad,) = sums.step("down", "attend", small=True, before=(result, up_far))
    (far_came,) = ordered((far_came,), *sums.sent)
    own = far_came.shape[0] // 2
    near_came = near_of(jnp.concatenate([input_pieces[1], far_came[own:]], axis=0))

    rest = width // blocks
    pieces = quad_pieces(info, sums, ("up", "attend"), rest)
    (near_came,) = ordered((near_came,), pieces[0])
    input_grad = placed(
        info,
        [input_pieces[0], near_came[:own], far_came[:own], near_came[own:]],
        F32,
        False,
        20,
    )
    moves = [(at, at ^ (sections + 1)) for at in range(blocks)]
    pieces = (
        pieces[0],
        exchanged(pieces[1], "section", 1),
        exchanged(pieces[2], "dp", 1),
        lax.ppermute(pieces[3], ("dp", "section"), moves),
    )

    own_block = dp_at * sections + section_at
    (own_block,) = ordered((own_block,), *sums.sent)

    def own_rows(array):
        return lax.dynamic_slice_in_dim(array, own_block * rest, rest, 0)

    (
        mixer_up_grad, mixer_gain_grad, attend_qkv_grad, attend_out_grad, attend_gain_grad,
        column_grads,
    ) = finish(
        info,
        pieces,
        sums,
        own_rows(mixer_up),
        own_rows(attend_qkv),
        own_rows(mixer_gain),
        own_rows(attend_gain),
        hidden // blocks,
        column_gain.shape[0],
        column_up.shape[1],
    )

    return (
        result,
        input_grad,
        attend_gain_grad,
        attend_qkv_grad,
        attend_out_grad,
        mixer_gain_grad,
        mixer_up_grad,
        mixer_down_grad,
        *column_grads,
    )


def solution(mesh):
    split = P(("dp", "section"))
    return jax.shard_map(
        body,
        mesh=mesh,
        in_specs=(P("dp", None), P("dp", None), P("dp", None), P("dp")) + (P(),) * 12,
        out_specs=(P("dp", "section"),) * 2 + (split,) * 6 + (P(),) * 6,
        check_vma=False,
    )
```

```python
import functools

import jax
import jax.numpy as jnp
from jax import lax
from jax.experimental import pallas as pl
from jax.experimental.pallas import tpu as pltpu
from jax.sharding import PartitionSpec as P

ATTR = 16
HEADS = 8
HEADS_ATTR = 8

EPSILON = 1e-05
MASKED = -1e30
GELU_SCALE = 0.7978845608028654
GELU_CUBE = 0.044715
BF16 = jnp.bfloat16
F32 = jnp.float32

FLOPS, BYTES = 1.10e+09, 3.60e+06

CORE, NEAR, FAR, CHIP, SECTION, COUNTS = range(6)


def exchanged(value, axis, mask):
    count = lax.axis_size(axis)
    return lax.ppermute(value, axis, [(at, at ^ mask) for at in range(count)])


def normal_parts(vector, axis=-1):
    centred = vector - jnp.mean(vector, axis=axis, keepdims=True)
    rate = lax.rsqrt(jnp.mean(centred * centred, axis=axis, keepdims=True) + EPSILON)
    return centred * rate, rate


def normal_back(normed, rate, scaled, axis=-1):
    middle = jnp.mean(scaled, axis=axis, keepdims=True)
    along = jnp.mean(scaled * normed, axis=axis, keepdims=True)
    return rate * (scaled - middle - normed * along)


def smooth_pair(inputs):
    square = inputs * inputs
    bent = jnp.tanh(GELU_SCALE * inputs * (1.0 + GELU_CUBE * square))
    half = 0.5 * (1.0 + bent)
    slope = half + (0.5 * GELU_SCALE) * inputs * (1.0 - bent * bent) * (
        1.0 + (3.0 * GELU_CUBE) * square
    )
    return inputs * half, slope


def dot(left, right):
    return jnp.dot(left, right, preferred_element_type=F32)


def dot_rows(left, right):
    return lax.dot_general(left, right, (((0,), (0,)), ((), ())), preferred_element_type=F32)


def dot_last(left, right):
    return lax.dot_general(left, right, (((1,), (1,)), ((), ())), preferred_element_type=F32)


def shape_of(dims, dtype):
    return jax.ShapeDtypeStruct(dims, dtype)


class Joined:
    def __init__(self, *pieces, far=()):
        self.pieces, self.far = pieces, far
        self.shape = (sum(rows for _, _, rows in pieces), *pieces[0][0].shape[1:])
        self.dtype = pieces[0][0].dtype


class Arriving:
    def __init__(self, pieces, ref, sems):
        self.ref, self.shape, self.dtype = ref, ref.shape, ref.dtype
        self.copies, at = [], 0
        for k, (source, first, rows) in enumerate(pieces):
            target = ref
            if len(pieces) > 1:
                source, target = source.at[pl.ds(first, rows)], ref.at[pl.ds(at, rows)]
            self.copies.append(pltpu.make_async_copy(source, target, sems[k]))
            at += rows
        for copy in self.copies:
            copy.start()

    def wait(self):
        for copy in self.copies:
            copy.wait()
        self.copies = []

    def __getitem__(self, at):
        self.wait()
        return self.ref[at]


class Leaving:
    def __init__(self, target, ref, sem):
        self.ref, self.shape, self.dtype = ref, ref.shape, ref.dtype
        self.copy, self.started = pltpu.make_async_copy(ref, target, sem), False

    def __getitem__(self, at):
        return self.ref[at]

    def __setitem__(self, at, value):
        self.ref[at] = value

    def send(self):
        if not self.started:
            self.copy.start()
            self.started = True


def call(
    body, name, info, arrays, out_shape, scratch=(), vmem=16, raw=(), far_in=(), far_out=(), near_in=(),
    near_out=(), plain=False, micros=0,
    blocks=None,
):
    options = dict(
        compiler_params=pltpu.CompilerParams(vmem_limit_bytes=vmem * 2**20),
        cost_estimate=pl.CostEstimate(
            flops=int(micros * FLOPS), bytes_accessed=int(micros * BYTES), transcendentals=0
        ),
        name=name,
    )
    if plain:

        def whole(array, at=None):
            if blocks is not None and at in blocks:
                return pl.BlockSpec(*blocks[at])
            return pl.BlockSpec(array.shape, lambda *_: (0,) * len(array.shape))

        spec = pltpu.PrefetchScalarGridSpec(
            num_scalar_prefetch=1,
            grid=(1,),
            in_specs=[whole(array, at) for at, array in enumerate(arrays)],
            out_specs=[whole(shape) for shape in out_shape],
            scratch_shapes=scratch,
        )
        return pl.pallas_call(body, grid_spec=spec, out_shape=out_shape, **options)(info, *arrays)
    copied = [k for k in range(len(arrays)) if k not in raw and k not in near_in]
    flat, places, in_specs = [], [], []
    for k, array in enumerate(arrays):
        pieces = array.pieces if isinstance(array, Joined) else [(array, 0, array.shape[0])]
        places.append([(len(flat) + n, first, rows) for n, (_, first, rows) in enumerate(pieces)])
        for n, (piece, _, _) in enumerate(pieces):
            if k in raw or k in far_in or n in getattr(array, "far", ()):
                piece = pltpu.with_memory_space_constraint(piece, pltpu.HBM)
            if k in near_in:
                piece = pltpu.with_memory_space_constraint(piece, pltpu.VMEM)
            flat.append(piece)
            in_specs.append(
                pl.BlockSpec(memory_space=pltpu.VMEM if k in near_in else pl.ANY)
            )
    count, outs = len(flat), len(out_shape)
    leaving = [k for k in range(outs) if k not in near_out]

    def run(info_ref, *refs):
        given, made, rest = refs[:count], refs[count : count + outs], refs[count + outs :]
        held, rest = rest[: len(copied)], rest[len(copied) :]
        out_held, rest = rest[: len(leaving)], rest[len(leaving) :]
        in_sems, out_sems, *rest = rest
        inputs = []
        for k in range(len(arrays)):
            if k in raw or k in near_in:
                inputs.append(given[places[k][0][0]])
                continue
            pieces = [
                (given[at], first, rows)
                for at, first, rows in places[k]
            ]
            sems = [in_sems.at[at] for at, _, _ in places[k]]
            inputs.append(Arriving(pieces, held[copied.index(k)], sems))
        outputs = [
            Leaving(made[k], out_held[leaving.index(k)], out_sems.at[k]) if k in leaving else made[k]
            for k in range(outs)
        ]
        body(info_ref, *inputs, *outputs, *rest)
        outputs = [outputs[k] for k in leaving]
        for one in inputs:
            if isinstance(one, Arriving):
                one.wait()
        for one in outputs:
            one.send()
        for one in outputs:
            one.copy.wait()

    def in_vmem(array):
        return pltpu.VMEM(array.shape, array.dtype)

    plain_out = out_shape
    out_shape = list(out_shape)
    for k, shape in enumerate(plain_out):
        if k in far_out or k in near_out:
            space = pltpu.HBM if k in far_out else pltpu.VMEM
            out_shape[k] = space(shape.shape, shape.dtype)
    spec = pltpu.PrefetchScalarGridSpec(
        num_scalar_prefetch=1,
        grid=(),
        in_specs=in_specs,
        out_specs=[
            pl.BlockSpec(memory_space=pltpu.VMEM if k in near_out else pl.ANY) for k in range(outs)
        ],
        scratch_shapes=[in_vmem(arrays[k]) for k in copied]
        + [in_vmem(plain_out[k]) for k in leaving]
        + [pltpu.SemaphoreType.DMA((count,)), pltpu.SemaphoreType.DMA((outs,))]
        + list(scratch),
    )
    return pl.pallas_call(run, grid_spec=spec, out_shape=out_shape, **options)(info, *flat)


def picked(source, columns):
    at = lax.broadcasted_iota(jnp.int32, (source.shape[0], columns), 1)
    return jnp.where(at == source, 1.0, 0.0).astype(BF16)


def bounds_of(info_ref):
    bounds, bound = [], jnp.int32(0)
    for k in range(COUNTS, info_ref.shape[0]):
        bound = bound + info_ref[k]
        bounds.append(bound)
    return bounds


def group_row(info_ref, far, near, at, rows):
    start = jnp.int32(0)
    for k, bound in enumerate(bounds_of(info_ref)):
        start = jnp.where(info_ref[COUNTS + k] == rows // 2, bound - rows // 2, start)
    source = at + (start + far * (rows // 2) + near * (rows // 4))
    return jnp.where(source >= rows, source - rows, source)


def softmax_parts(queries, keys, allowed, scale):
    scores = jnp.where(allowed, dot_last(queries, keys) * scale, MASKED)
    lifted = jnp.exp(scores - jnp.max(scores, axis=-1, keepdims=True))
    return lifted * (1.0 / jnp.sum(lifted, axis=-1, keepdims=True))


def attend_kernel(
    info_ref, features, valid_ref, gain_ref, qkv_hbm, out_hbm, next_gain_ref, up_hbm, down_hbm,
    own_ref, normed_ref, projected_ref, mask_ref, shared_ref, first_ref, slope_ref,
    turned_ref, weights, out, ups, downs, sems, *, head_dim,
):
    rows, width = features.shape
    half, own = rows // 2, rows // 4
    pair = 2 * head_dim

    def copy(source, target, at):
        return pltpu.make_async_copy(source, target, sems.at[at])

    to_weights = copy(qkv_hbm, weights, 0)
    to_out = copy(out_hbm, out, 1)
    to_mixer = [copy(up_hbm, ups, 2), copy(down_hbm, downs, 3)]
    to_weights.start()

    near, far = info_ref[NEAR], info_ref[FAR]

    def source_of(at):
        side = jnp.where(at < own, near, 1 - near)
        return group_row(info_ref, far, side, jnp.where(at < own, at, at - own), rows)

    row_source = source_of(lax.broadcasted_iota(jnp.int32, (half, 1), 0))
    lane_source = source_of(lax.broadcasted_iota(jnp.int32, (1, half), 1))
    pick = picked(row_source, rows)
    row_segment = jnp.zeros((half, 1), jnp.int32)
    lane_segment = jnp.zeros((1, half), jnp.int32)
    for bound in bounds_of(info_ref):
        row_segment += (row_source >= bound).astype(jnp.int32)
        lane_segment += (lane_source >= bound).astype(jnp.int32)
    valid = valid_ref[...].astype(F32).astype(BF16)
    usable = dot_last(jnp.broadcast_to(valid, (8, rows)), pick)[:1]
    same = lax.broadcasted_iota(jnp.int32, (half, half), 0) == lax.broadcasted_iota(
        jnp.int32, (half, half), 1
    )
    allowed = (row_segment == lane_segment) & ((usable > 0.5) | same)
    mask_ref[...] = jnp.where(allowed, 1.0, 0.0)
    features.wait()
    to_out.start()
    taken = dot(pick, features[...])
    own_ref[...] = taken[:own].astype(BF16)
    normed, _ = normal_parts(taken)
    normed_ref[...] = (normed * gain_ref[...]).astype(BF16)

    to_weights.wait()
    projected_ref[...] = dot(normed_ref[...], weights[...]).astype(BF16)
    projected_ref.send()
    normed_ref.send()
    mask_ref.send()
    own_ref.send()
    for one in to_mixer:
        one.start()

    @pl.loop(0, width // pair)
    def _(step):
        def columns(first):
            return pl.ds(pl.multiple_of(first + step * pair, pair), pair)

        queries = projected_ref[:own, columns(0)]
        keys = projected_ref[:, columns(width)]
        values = projected_ref[:, columns(2 * width)]
        open_ = mask_ref[:own, :] > 0
        mixed = []
        for head in range(2):
            here = slice(head * head_dim, (head + 1) * head_dim)
            shares = softmax_parts(queries[:, here], keys[:, here], open_, head_dim**-0.5)
            mixed.append(dot(shares.astype(BF16), values[:, here]).astype(BF16))
        shared_ref[own:, columns(0)] = jnp.concatenate(mixed, axis=1)

    to_out.wait()
    first = own_ref[...].astype(F32) + dot(shared_ref[own:, :], out[...])
    first_ref[...] = first.astype(BF16)
    total = first_ref[...].astype(F32)
    normed, _ = normal_parts(total)
    shared_ref[:own, :] = (normed * next_gain_ref[...]).astype(BF16)
    shared_ref.send()
    first_ref.send()

    for one in to_mixer:
        one.wait()
    hidden, slope = smooth_pair(dot(shared_ref[:own, :], ups[...]))
    slope_ref[...] = slope.astype(BF16)
    slope_ref.send()
    turned_ref[...] = (total + dot(hidden.astype(BF16), downs[...])).T.astype(BF16)


def attend(info, features, valid, gain, qkv, out, next_gain, up, down):
    rows, width = features.shape
    half, own = rows // 2, rows // 4
    wide, hidden = qkv.shape[1], up.shape[1]
    return call(
        functools.partial(attend_kernel, head_dim=width // HEADS),
        "attend",
        info,
        (features, valid, gain, qkv, out, next_gain, up, down),
        [
            shape_of((own, width), BF16),
            shape_of((half, width), BF16),
            shape_of((half, wide), BF16),
            shape_of((half, half), F32),
            shape_of((half, width), BF16),
            shape_of((own, width), BF16),
            shape_of((own, hidden), BF16),
            shape_of((width, own), BF16),
        ],
        raw=(3, 4, 6, 7),
        far_in=(0, 1, 2, 5),
        far_out=(0, 1, 2, 3, 5, 6, 7),
        scratch=[
            pltpu.VMEM((width, wide), BF16),
            pltpu.VMEM((width, width), BF16),
            pltpu.VMEM((width, hidden), BF16),
            pltpu.VMEM((hidden, width), BF16),
            pltpu.SemaphoreType.DMA((4,)),
        ],
        vmem=56,
        micros=20,
    )


def attend_back_kernel(
    info_ref, grad, projected, mask, out_hbm, qkv_hbm,
    kept_ref, sent_ref, e_own_ref, e_sent_ref, out, weights, grads, sems, *, head_dim,
):
    rows, width = grad.shape
    own, quarter = rows // 2, width // 4
    heads = HEADS // 2
    wide = heads * head_dim
    scale = head_dim**-0.5
    near = info_ref[NEAR]
    first = pl.multiple_of(near * wide, wide)
    to_out = pltpu.make_async_copy(out_hbm.at[pl.ds(first, wide), :], out, sems.at[0])
    to_weights = [
        pltpu.make_async_copy(
            qkv_hbm.at[:, pl.ds(pl.multiple_of(first + k * width, wide), wide)],
            weights.at[:, pl.ds(k * wide, wide)],
            sems.at[1 + k],
        )
        for k in range(3)
    ]
    to_out.start()
    for one in to_weights:
        one.start()

    projected.wait()
    mask.wait()
    to_out.wait()
    pulled = dot_last(grad[...], out[...]).astype(BF16)
    allowed = mask[...] > 0

    def columns(which):
        return projected.ref[:, pl.ds(pl.multiple_of(first + which * width, wide), wide)]

    all_queries, all_keys, all_values = columns(0), columns(1), columns(2)
    for head in range(heads):
        at = slice(head * head_dim, (head + 1) * head_dim)
        queries, keys, values = all_queries[:, at], all_keys[:, at], all_values[:, at]
        shares = softmax_parts(queries, keys, allowed, scale)
        share_grad = dot_last(pulled[:, at], values)
        centre = jnp.sum(share_grad * shares, axis=-1, keepdims=True)
        score_grad = (shares * (share_grad - centre)).astype(BF16)
        grads[:, at] = (dot(score_grad, keys) * scale).astype(BF16)
        at = slice(wide + head * head_dim, wide + (head + 1) * head_dim)
        grads[:, at] = (dot_rows(score_grad, queries) * scale).astype(BF16)
        at = slice(2 * wide + head * head_dim, 2 * wide + (head + 1) * head_dim)
        grads[:, at] = dot_rows(shares.astype(BF16), pulled[:, head * head_dim : (head + 1) * head_dim]).astype(BF16)
    core = info_ref[CORE]
    for target, side in ((sent_ref, 1 - core), (kept_ref, core)):
        for k in range(3):
            place = pl.multiple_of(k * wide + side * (wide // 2), wide // 2)
            target[:, k * quarter : (k + 1) * quarter] = grads[:, pl.ds(place, wide // 2)]
        place = pl.multiple_of((side * 2 + near) * quarter, quarter)
        target[:, 3 * quarter :] = grad.ref[:, pl.ds(place, quarter)]
        target.send()
    for one in to_weights:
        one.wait()
    summed = dot_last(grads[...], weights[...])
    e_own_ref[...] = summed[:own]
    e_sent_ref[...] = summed[own:].astype(BF16)


def attend_back(info, projected, mask, own_grad, near_grad, out, qkv):
    own, width = own_grad.shape
    rows = 2 * own
    wide = width // 2
    return call(
        functools.partial(attend_back_kernel, head_dim=width // HEADS),
        "attend_back",
        info,
        (Joined((own_grad, 0, own), (near_grad, 0, own)), projected, mask, out, qkv),
        [
            shape_of((rows, width), BF16),
            shape_of((rows, width), BF16),
            shape_of((own, width), F32),
            shape_of((own, width), BF16),
        ],
        raw=(3, 4),
        far_in=(1, 2),
        scratch=[
            pltpu.VMEM((wide, width), BF16),
            pltpu.VMEM((width, 3 * wide), BF16),
            pltpu.VMEM((rows, 3 * wide), BF16),
            pltpu.SemaphoreType.DMA((4,)),
        ],
        vmem=24,
        micros=11,
        far_out=(0,),
    )


def last_kernel(info_ref, e_own_ref, e_near_ref, grad_ref, x_ref, gain_ref, *refs):
    pieces, held = refs[:-1], refs[-1]
    upstream = e_own_ref[...] + e_near_ref[...].astype(F32)
    normed, rate = normal_parts(x_ref[...].astype(F32))
    back = normal_back(normed, rate, upstream * gain_ref[...])
    held[...] = grad_ref[...].astype(F32) + back
    own, quarter = held.shape[0], pieces[0].shape[1]
    for mask in range(4):
        at = pl.multiple_of((info_ref[SECTION] ^ mask) * quarter, quarter)
        value = held[:, pl.ds(at, quarter)].astype(BF16)
        pieces[min(mask, 2)][(mask // 3) * own : (mask // 3 + 1) * own, :] = value


def last_norm(info, e_own, e_near, grad, x, gain, sections):
    own, width = x.shape
    return call(
        last_kernel,
        "last_norm",
        info,
        (e_own, e_near, grad, x, gain),
        [
            shape_of((own, width // sections), BF16),
            shape_of((own, width // sections), BF16),
            shape_of((2 * own, width // sections), BF16),
        ],
        scratch=[pltpu.VMEM((own, width), F32)],
        plain=True,
        micros=20,
        vmem=8,
    )


def place_kernel(info_ref, *refs, turned):
    pieces, out_ref = refs[:-1], refs[-1]
    rows = out_ref.shape[0]
    own = rows // 4
    at = lax.broadcasted_iota(jnp.int32, (own, 1), 0)
    total = None
    for mask, piece in enumerate(pieces):
        section = info_ref[SECTION] ^ mask
        pick = picked(group_row(info_ref, section >> 1, section & 1, at, rows), rows)
        if turned:
            part = lax.dot_general(
                pick, piece[...], (((0,), (1,)), ((), ())), preferred_element_type=F32
            )
        else:
            part = dot_rows(pick, piece[...])
        total = part if total is None else total + part
    out_ref[...] = total.astype(out_ref.dtype)


def placed(info, pieces, dtype, turned, micros=0):
    own = pieces[0].shape[1 if turned else 0]
    quarter = pieces[0].shape[0 if turned else 1]
    rows = own * len(pieces)
    return call(
        functools.partial(place_kernel, turned=turned),
        "placed",
        info,
        pieces,
        [shape_of((rows, quarter), dtype)],
        plain=True,
        micros=micros,
        vmem=8,
    )[0]


def part_copies(info_ref, weight_hbm, held, sems, part, axis):
    quarter = held.shape[axis]
    copies = []
    width = part if part % 128 == 0 else quarter
    for k in range(quarter // width):
        first = hidden_block(k, info_ref) * part if width == part else 0
        source, target = pl.ds(pl.multiple_of(first, width), width), pl.ds(k * width, width)
        if axis == 1:
            pair = weight_hbm.at[:, source], held.at[:, target]
        else:
            pair = weight_hbm.at[source, :], held.at[target, :]
        copies.append(pltpu.make_async_copy(*pair, sems.at[k]))
    for copy in copies:
        copy.start()
    return copies, width


def mixer_back_kernel(info_ref, grad, slope, first, gain, ups, downs, out_ref):
    pulled = dot_last(grad[...], downs[...])
    lifted = (slope[...].astype(F32) * pulled).astype(BF16)
    total = dot_last(lifted, ups[...])
    normed, rate = normal_parts(first[...].astype(F32))
    back = normal_back(normed, rate, total * gain[...])
    out_ref[...] = (grad[...].astype(F32) + back).astype(BF16)


def mixer_back(info, grad, slope, first, gain, up, down):
    return call(
        mixer_back_kernel,
        "mixer_back",
        info,
        (grad, slope, first, gain, up, down),
        [shape_of(grad.shape, BF16)],
        vmem=24,
        far_in=(1, 2, 3),
        near_in=(4, 5),
        micros=60,
    )[0]


def pool_kernel(info_ref, pool, up_hbm, hidden_ref, slope_ref, held, sems, *, part):
    copies, _ = part_copies(info_ref, up_hbm, held, sems, part, 1)
    for copy in copies:
        copy.wait()
    hidden, slope = smooth_pair(dot(pool[...], held[...]))
    hidden_ref[...] = hidden.astype(BF16)
    hidden_ref.send()
    slope_ref[...] = slope.astype(BF16)


def pool_forward(info, shared, up, blocks):
    own, width = shared[0].shape[0] // 2, shared[0].shape[1]
    hidden = up.shape[1]
    quarter, part = hidden // 4, hidden // blocks
    pool = Joined(*[(array, 0, own) for array in shared])
    return call(
        functools.partial(pool_kernel, part=part),
        "pool_forward",
        info,
        (pool, own_quarter(info, up, blocks, 1)),
        [shape_of((pool.shape[0], quarter), BF16)] * 2,
        scratch=[pltpu.VMEM((width, quarter), BF16), pltpu.SemaphoreType.DMA((blocks // 4,))],
        vmem=24,
        raw=(1,),
        far_out=(0, 1),
        micros=60,
    )


def hidden_block(at, info):
    return (((at // 2) * 2 + info[CORE]) * 2 + at % 2) * 2 + info[NEAR]


def own_quarter(info, weight, blocks, axis):
    part = weight.shape[axis] // blocks
    if part % 128 == 0:
        return weight
    order = hidden_block(jnp.arange(blocks // 4), info)
    shape = weight.shape[:axis] + (blocks, part) + weight.shape[axis + 1 :]
    taken = jnp.take(weight.reshape(shape), order, axis=axis)
    return taken.reshape(weight.shape[:axis] + (-1,) + weight.shape[axis + 1 :])


def split_place(position, bit):
    chip, far = position >> 1, position & 1
    low = chip & ((1 << bit) - 1)
    rest = ((chip >> (bit + 1)) << bit) | low
    return (chip >> bit) & 1, rest * 2 + far


def halves_like(positions, rows, columns):
    return [shape_of((positions, rows, columns // 2), BF16)] * 2


def down_kernel(info_ref, grad, hidden, *refs, part, bits):
    outs, held = refs[:-1], refs[-1]
    grad.wait()
    held[...] = dot_rows(hidden[...], grad[...])
    store_positions(info_ref, outs, held, bits, (part, 1))


def down_gradient(info, hidden, grads, blocks, bits):
    pool, quarter = hidden.shape
    own, width = grads[0].shape
    part = quarter * 4 // blocks
    like = halves_like(blocks // 4, part, width)
    return call(
        functools.partial(down_kernel, part=part, bits=bits),
        "down_gradient",
        info,
        (Joined(*[(array, 0, own) for array in grads]), hidden),
        like,
        scratch=[pltpu.VMEM((quarter, width), F32)],
        vmem=20,
        micros=20,
        far_in=(1,),
    )


def store_positions(info_ref, outs, held, bits, layout):
    rest, quads = layout
    positions = held.shape[0] // (rest * quads)
    columns = held.shape[1] // 2
    own_place = info_ref[CHIP] * 2 + info_ref[FAR]
    for position in range(positions):
        source = position ^ own_place
        for quad in range(quads):
            if quads == 1:
                block = source
            else:
                block = (((source >> 1) * 2 + quad // 2) * 2 + (source & 1)) * 2 + quad % 2
            rows = pl.ds(pl.multiple_of(block * rest, rest), rest)
            for side, bit in enumerate((0, bits - 1)):
                goes, place = split_place(position, bit)
                place += side * positions // 2
                value = held[rows, side * columns : (side + 1) * columns]
                outs[goes][place, quad * rest : (quad + 1) * rest, :] = value.astype(BF16)


def up_kernel(info_ref, grad, slope, normed, down_hbm, *refs, part, bits):
    outs, (weight, lifted, total, sems) = refs[:2], refs[2:]
    copies, _ = part_copies(info_ref, down_hbm, weight, sems, part, 0)
    for copy in copies:
        copy.wait()
    pulled = dot_last(grad[...], weight[...])
    lifted[...] = (slope[...].astype(F32) * pulled).astype(BF16)
    total[...] = dot_rows(normed[...], lifted[...])
    store_positions(info_ref, outs, total, bits, (outs[0].shape[1] // 4, 4))


def up_gradient(info, slope, shared, grads, down, blocks, bits):
    pool, quarter = slope.shape
    hidden, width = down.shape
    own = grads[0].shape[0]
    like = halves_like(blocks // 4, width * 4 // blocks, quarter)
    return call(
        functools.partial(up_kernel, part=hidden // blocks, bits=bits),
        "up_gradient",
        info,
        (
            Joined(*[(array, 0, own) for array in grads]),
            slope,
            Joined(*[(array, 0, own) for array in shared]),
            own_quarter(info, down, blocks, 0),
        ),
        like,
        raw=(3,),
        scratch=[
            pltpu.VMEM((quarter, width), BF16),
            pltpu.VMEM((pool, quarter), BF16),
            pltpu.VMEM((width, quarter), F32),
            pltpu.SemaphoreType.DMA((blocks // 4,)),
        ],
        vmem=28,
        micros=8,
        far_in=(1, 2),
    )


def attend_grad_kernel(info_ref, normed, mixed, packs, *refs, bits):
    outs, total = refs[:-1], refs[-1]
    edge = total.shape[1] * 3 // 4
    total[:, :edge] = dot_rows(normed[...], packs[:, :edge])
    total[:, edge:] = dot_rows(mixed[...], packs[:, edge:])
    store_positions(info_ref, outs, total, bits, (outs[0].shape[1] // 4, 4))


def attend_gradient(info, normed, shared, packs, blocks, bits):
    half, width = normed[0].shape
    columns = packs[0].shape[1]
    own = half // 2
    like = halves_like(blocks // 4, width * 4 // blocks, columns)
    return call(
        functools.partial(attend_grad_kernel, bits=bits),
        "attend_gradient",
        info,
        (
            Joined(*[(array, 0, half) for array in normed]),
            Joined(*[(array, own, own) for array in shared]),
            Joined(*[(array, 0, half) for array in packs], far=(0,)),
        ),
        like,
        scratch=[pltpu.VMEM((width, columns), F32)],
        vmem=20,
        micros=0,
        far_in=(0, 1),
    )


def by_quad(info_ref, pieces):
    near, core = info_ref[NEAR] == 0, info_ref[CORE] == 0
    low = [jnp.where(near, pieces[k], pieces[k ^ 1]) for k in range(4)]
    return [jnp.where(core, low[k], low[k ^ 2]) for k in range(4)]


def gain_row(weight, grad, gain):
    total = jnp.sum(weight.astype(F32) * grad, axis=1, keepdims=True)
    eye = lax.broadcasted_iota(jnp.int32, (total.shape[0],) * 2, 0) == lax.broadcasted_iota(
        jnp.int32, (total.shape[0],) * 2, 1
    )
    return jnp.sum(jnp.where(eye, total, 0.0), axis=0, keepdims=True) / gain


def finish_kernel(info_ref, *refs, part, small, came):
    small_ref, came_ref, up_weight, qkv_weight, up_gain, qkv_gain = refs[4:10]
    up_ref, up_gain_ref, qkv_ref, out_ref, qkv_gain_ref = refs[10:15]
    pieces = by_quad(info_ref, [ref[...].astype(F32) for ref in refs[:4]])
    hidden = up_ref.shape[1] // 4
    quarter = out_ref.shape[1] // 4
    blocks = []
    for chip in range(hidden // (2 * part)):
        for core in range(2):
            for far in range(2):
                for near in range(2):
                    at = (chip * 2 + far) * part
                    blocks.append(pieces[core * 2 + near][:, at : at + part])
    up_ref[...] = jnp.concatenate(blocks, axis=1)
    for which in range(3):
        for near in range(2):
            for core in range(2):
                at = ((which * 2 + near) * 2 + core) * quarter
                source = hidden + which * quarter
                qkv_ref[:, at : at + quarter] = pieces[core * 2 + near][:, source : source + quarter]
    for k, piece in enumerate(pieces):
        out_ref[:, k * quarter : (k + 1) * quarter] = piece[:, hidden + 3 * quarter :]
    up_gain_ref[...] = gain_row(up_weight[...], up_ref[...], up_gain[...])
    qkv_gain_ref[...] = gain_row(qkv_weight[...], qkv_ref[...], qkv_gain[...])
    blocks = []
    for k in range(small[1]):
        blocks.append(small_ref[small[0] + k] + came_ref[came + k].astype(F32))
    column_finish(jnp.concatenate(blocks, axis=0), refs[15:])


def finish(info, pieces, sums, up, qkv, up_gain, qkv_gain, part, width, column_hidden):
    rest = pieces[0].shape[0]
    hidden, wide = up.shape[1], qkv.shape[1]
    own_blocks = None
    if up.shape[0] > rest:

        def own_rows(_, info_ref):
            block = (info_ref[CHIP] * 2 + info_ref[CORE]) * 4 + info_ref[SECTION]
            return (block, 0)

        own_blocks = {6: ((rest, hidden), own_rows), 7: ((rest, wide), own_rows)}
    shapes = [(rest, hidden), (1, rest), (rest, wide), (rest, wide // 3), (1, rest)]
    shapes += [(1, width), (width, 3 * width), (width, width), (1, width)]
    shapes += [(width, column_hidden)] * 2
    (small, small_at), count = sums.small
    handle, came_at = sums.small_sent
    results = call(
        functools.partial(finish_kernel, part=part, small=(small_at, count), came=came_at),
        "finish",
        info,
        (*pieces, small, sums.messages[handle], up, qkv, up_gain[None], qkv_gain[None]),
        [shape_of(dims, F32) for dims in shapes],
        plain=True,
        blocks=own_blocks,
        far_in=(6, 7),
        vmem=12,
    )
    up_grad, up_gain_grad, qkv_grad, out_grad, qkv_gain_grad, *columns = results
    columns[0], columns[3], columns[5] = columns[0][0], columns[3][0], columns[5].T
    return up_grad, up_gain_grad[0], qkv_grad, out_grad, qkv_gain_grad[0], columns


def ordered(arrays, *before):
    count = len(arrays)
    return lax.optimization_barrier((*arrays, *before))[:count]


def step_kernel(info_ref, *refs, inputs, adds, copies, ends, small):
    ins, outs = refs[:inputs], refs[inputs:]

    def value(kept, came, k):
        total = ins[kept[0]][kept[1] + k].astype(F32)
        if came is None:
            return total
        return total + ins[came[0]][came[1] + k].astype(F32)

    for kept, came, count, place, keep, sent in adds:
        for k in range(count):
            total = value(kept, came, k)
            to = ((k >> (place + 1)) << place) | (k & ((1 << place) - 1))
            if (k >> place) & 1:
                outs[sent[0]][sent[1] + to] = total.astype(BF16)
            else:
                outs[keep[0]][keep[1] + to] = total
    for source, count, target in copies:
        for k in range(count):
            outs[target[0]][target[1] + k] = ins[source[0]][source[1] + k]
    for end, sides in ends:
        columns = outs[end].shape[1] // 2
        for side, (kept, came) in enumerate(sides):
            outs[end][:, side * columns : (side + 1) * columns] = value(kept, came, 0)
    for kept, came, count, keep, sent in small:
        for k in range(count):
            if came is not None and len(came) == 4:
                far, first, half, size = came
                at = [pl.ds(first + side * half + k * size, size) for side in range(2)]
                other = jnp.concatenate([ins[far][rows, :] for rows in at], axis=1)
                total = ins[kept[0]][k * size : (k + 1) * size, :] + other.astype(F32)
            else:
                total = value(kept, came, k)
            outs[keep[0]][keep[1] + k] = total
            if sent is not None:
                outs[sent[0]][sent[1] + k] = total.astype(BF16)


class Sums:
    def __init__(self, info, bits, block):
        self.info, self.bits, self.block = info, bits, block
        self.gradients, self.messages, self.held = {}, [], {}
        self.small, self.small_sent, self.small_route = None, None, [*range(bits), "near", "core"]
        self.fresh = None

    def step(
        self, *advance, new=None, far_at=None, small=False, hold=(), before=(), micros=0
    ):
        with_small = small
        arrays, outs, adds, copies, ends = [], [], [], [], []
        sends, kept_count, kept_by, finished, small = {}, 0, [], [], []

        def given(array):
            for k, other in enumerate(arrays):
                if other is array:
                    return k
            arrays.append(array)
            return len(arrays) - 1

        def made(shape):
            outs.append(shape)
            return len(outs) - 1

        def to_send(key, count):
            at = sends.get(key, 0)
            sends[key] = at + count
            return key, at

        def to_keep(count):
            nonlocal kept_count
            kept_count += count
            return kept_count - count

        def there(kept):
            return given(kept[0]), kept[1]

        moving = [self.gradients[name] for name in advance]
        needed = {side["sent"][0] for one in moving for side in one}
        if with_small and self.small_sent is not None:
            needed.add(self.small_sent[0])
        needed = sorted(needed)
        came = ordered([self.messages[at] for at in needed], *before) if needed else ()
        came_at = {at: given(array) for at, array in zip(needed, came)}

        def arrived(sent):
            return None if sent is None else (came_at[sent[0]], sent[1])

        block = self.block
        for name, one in zip(advance, moving):
            if not one[0]["route"]:
                end = made(shape_of((block[0], 2 * block[1]), F32))
                ends.append((end, [(there(s["kept"]), arrived(s["sent"])) for s in one]))
                del self.gradients[name]
                continue
            for side in one:
                key = side["route"].pop(0)
                if key == "far":
                    place, side["below"] = 0, 0
                else:
                    place = len(side["left"]) - 1 - side["left"].index(key) + side["below"]
                    side["left"].remove(key)
                entry = [there(side["kept"]), arrived(side["sent"]), side["count"], place]
                side["count"] //= 2
                side["sent"] = to_send(key, side["count"])
                kept_by.append((side, entry, to_keep(side["count"])))
        sent_sides = [side for side, _, _ in kept_by]
        if new is not None:
            name, (kept, sent) = new
            one, count = [], kept.shape[0] // 2
            for number in range(2):
                order = tuple(range(self.bits))
                order = order if number == 0 else order[::-1]
                route = list(order[1:])
                route.insert(self.bits if far_at is None else far_at - 1, "far")
                side = {
                    "route": route,
                    "below": 1,
                    "left": [bit for bit in range(self.bits - 1, -1, -1) if bit != order[0]],
                    "kept": (kept, number * count),
                    "count": count,
                    "sent": to_send(order[0], count),
                }
                copies.append(((given(sent), number * count), count, side["sent"]))
                one.append(side)
            self.gradients[name] = one
            sent_sides += one
        if with_small:
            kept, count = self.small
            entry = [there(kept), arrived(self.small_sent), count, to_keep(count)]
            if self.fresh is not None:
                far, first = self.fresh
                entry[1] = (given(far), first, kept[0].shape[0], block[0])
                self.fresh = None
            self.small_sent = None
            if self.small_route:
                self.small_sent = to_send(self.small_route.pop(0), count)
            small.append((*entry, self.small_sent))
        keys = sorted(sends, key=str)
        sent_out = {key: made(shape_of((sends[key], *block), BF16)) for key in keys}
        if kept_count:
            kept_out = made(shape_of((kept_count, *block), F32))

        def target(sent):
            return None if sent is None else (sent_out[sent[0]], sent[1])

        adds = [(*entry, (kept_out, at), target(side["sent"])) for side, entry, at in kept_by]
        copies = [(source, count, target(sent)) for source, count, sent in copies]
        small = [(*entry[:3], (kept_out, entry[3]), target(entry[4])) for entry in small]
        results = call(
            functools.partial(
                step_kernel, inputs=len(arrays), adds=adds, copies=copies, ends=ends, small=small
            ),
            "sums_step",
            self.info,
            tuple(arrays),
            outs,
            vmem=12,
            plain=True,
            micros=micros,
        )
        for side, _, at in kept_by:
            side["kept"] = (results[kept_out], at)
        handles = {}
        for key in keys:
            handles[key] = len(self.messages)
            self.messages.append(None)
            self.held[handles[key]] = (key, results[sent_out[key]])
            if key not in hold:
                self.release(handles[key])
        for side in sent_sides:
            side["sent"] = (handles[side["sent"][0]], side["sent"][1])
        if with_small:
            self.small = ((results[kept_out], small[0][3][1]), self.small[1])
            if self.small_sent is not None:
                self.small_sent = (handles[self.small_sent[0]], self.small_sent[1])
        self.sent = [results[sent_out[key]] for key in keys]
        self.handles = handles
        return [results[end] for end, _ in ends]

    def release(self, handle, *before):
        key, array = self.held.pop(handle)
        (array,) = ordered((array,), *before)
        places = {"far": ("section", 2), "near": ("section", 1), "core": ("dp", 1)}
        axis, mask = places[key] if key in places else ("dp", 2 << key)
        self.messages[handle] = exchanged(array, axis, mask)


def quad_kernel(info_ref, *refs, inputs, sides, rest):
    ins, pieces, held = refs[:inputs], refs[inputs:-1], refs[-1]
    columns = held.shape[1] // len(sides)
    for k, (kept, came) in enumerate(sides):
        total = ins[kept[0]][kept[1]] + ins[came[0]][came[1]].astype(F32)
        held[:, k * columns : (k + 1) * columns] = total
    own = info_ref[CORE] * 2 + info_ref[NEAR]
    for mask, piece in enumerate(pieces):
        rows = pl.ds(pl.multiple_of((own ^ mask) * rest, rest), rest)
        piece[...] = held[rows, :].astype(BF16)


def quad_pieces(info, sums, names, rest):
    arrays = []

    def there(place):
        for k, other in enumerate(arrays):
            if other is place[0]:
                return k, place[1]
        arrays.append(place[0])
        return len(arrays) - 1, place[1]

    sides = [
        (there(side["kept"]), there((sums.messages[side["sent"][0]], side["sent"][1])))
        for name in names
        for side in sums.gradients[name]
    ]
    block, columns = sums.block
    return call(
        functools.partial(quad_kernel, inputs=len(arrays), sides=sides, rest=rest),
        "quad_pieces",
        info,
        tuple(arrays),
        [shape_of((rest, columns * len(sides)), BF16)] * 4,
        scratch=[pltpu.VMEM((block, columns * len(sides)), F32)],
        plain=True,
        vmem=8,
    )


TOGETHER = 4


def one_hot(rows, columns, row_of_column):
    row = lax.broadcasted_iota(jnp.int32, (rows, columns), 0)
    column = lax.broadcasted_iota(jnp.int32, (rows, columns), 1)
    return jnp.where(row == row_of_column(column), 1.0, 0.0).astype(BF16)


def head_order(count, small):
    heads, width = HEADS_ATTR, HEADS_ATTR * small

    def row_of(column):
        inside = column % width
        return column - inside + (inside % small) * heads + inside // small

    return one_hot(count, count, row_of)


def column_kernel(
    info_ref,
    cells_ref,
    cotangent,
    gain_ref,
    qkv_ref,
    out_ref,
    mix_gain_ref,
    up_ref,
    down_t_ref,
    mixer_up_hbm,
    mixer_down_hbm,
    *refs,
    width,
    small,
    sections,
):
    results = refs[:3]
    cells_grad_ref, sums_ref, mixer_up_ref, mixer_down_ref = refs[3:7]
    (
        projected,
        normed_low,
        shares_kept,
        score_grads,
        mixed,
        mixed_grad,
        sum_grad,
        turned_grad,
        upstream_all,
        gain_sum,
        mix_gain_sum,
        gain_wide,
        mix_gain_wide,
        qkv_group,
        out_group,
        out_group_t,
        up_group_t,
        down_group,
        qkv_heads,
        mixer_sems,
    ) = refs[7:]
    to_mixer = [
        pltpu.make_async_copy(mixer_up_hbm, mixer_up_ref, mixer_sems.at[0]),
        pltpu.make_async_copy(mixer_down_hbm, mixer_down_ref, mixer_sems.at[1]),
    ]
    lanes = cells_ref.shape[1]
    hidden_width = up_ref.shape[1]
    heads = HEADS_ATTR
    scale = small**-0.5
    lane_blocks = lanes // 128
    group = ATTR // sections
    wide = group * width
    up_at = (slice(0, width), slice(0, hidden_width))
    down_at = (slice(0, width), slice(hidden_width, 2 * hidden_width))
    qkv_at = (slice(width, 2 * width), slice(0, 3 * width))
    out_at = (slice(width, 2 * width), slice(3 * width, 4 * width))
    gain_at = (slice(width, 2 * width), slice(4 * width, 4 * width + 128))

    spread = one_hot(width, wide, lambda column: column % width)

    def diagonal(lanes_tiled):
        tiled = jnp.concatenate([lanes_tiled] * group, axis=0)
        row = lax.broadcasted_iota(jnp.int32, tiled.shape, 0) // lanes_tiled.shape[0]
        column = lax.broadcasted_iota(jnp.int32, tiled.shape, 1) // width
        return jnp.where(row == column, tiled, 0.0)

    triple = head_order(3 * width, small)
    qkv_heads[...] = dot_last(qkv_ref[...], triple).astype(BF16)
    qkv_group[...] = diagonal(dot(dot_last(triple, qkv_ref[...]).astype(BF16), spread)).astype(BF16)
    out_heads = dot(head_order(width, small), out_ref[...]).astype(BF16)
    out_wide = diagonal(dot(out_heads, spread))
    out_group[...] = out_wide.astype(BF16)
    out_group_t[...] = out_wide.T.astype(BF16)
    up_group_t[...] = diagonal(dot_rows(up_ref[...], spread)).astype(BF16)
    down_group[...] = diagonal(dot_rows(down_t_ref[...], spread)).astype(BF16)
    eye = lax.broadcasted_iota(jnp.int32, (width, width), 0) == lax.broadcasted_iota(
        jnp.int32, (width, width), 1
    )
    for ref, kept in ((gain_ref, gain_wide), (mix_gain_ref, mix_gain_wide)):
        column = jnp.sum(jnp.where(eye, ref[...], 0.0), axis=1, keepdims=True)
        kept[...] = jnp.broadcast_to(column, (width, lanes))

    sums_ref[...] = jnp.zeros(sums_ref.shape, F32)
    gain_sum[...] = jnp.zeros_like(gain_sum)
    mix_gain_sum[...] = jnp.zeros_like(mix_gain_sum)

    def at_group(g):
        if isinstance(g, int):
            return slice(g * wide, (g + 1) * wide)
        return pl.ds(pl.multiple_of(g * wide, wide), wide)

    def at_rows(a):
        return pl.ds(pl.multiple_of(a * width, width), width)

    def apart(value):
        return value.reshape(group, width, lanes)

    def each(value):
        size = value.shape[0] // group
        return [value[k * size : (k + 1) * size] for k in range(group)]

    def along(value):
        return jnp.concatenate(each(value), axis=1)

    cells_ref.wait()

    for g in range(sections):
        normed, _ = normal_parts(apart(cells_ref[at_group(g), :].astype(F32)), 1)
        low = (normed * gain_wide[...][None]).astype(BF16).reshape(wide, lanes)
        normed_low[at_group(g), :] = low
        part = dot(qkv_group[...], low).astype(BF16).astype(F32)
        projected[pl.ds(g * group, group)] = part.reshape(group, 3, small, heads, lanes)

    for block in range(lane_blocks):
        here = slice(block * 128, block * 128 + 128)

        @pl.loop(0, ATTR, step=TOGETHER)
        def _(first):
            several = range(TOGETHER)
            queries = [projected[first + k, 0, :, :, here] for k in several]
            scores = [[] for _ in several]
            for b in range(ATTR):
                key = projected[b, 1, :, :, here]
                for k in several:
                    scores[k].append(jnp.sum(queries[k] * key, axis=0) * scale)
            shares = []
            for k in several:
                peak = functools.reduce(jnp.maximum, scores[k])
                lifted = [jnp.exp(score - peak) for score in scores[k]]
                rate = 1.0 / functools.reduce(jnp.add, lifted)
                shares.append([each_one * rate for each_one in lifted])
                for b in range(ATTR):
                    shares_kept[first + k, b, :, here] = shares[k][b]
            totals = [None for _ in several]
            for b in range(ATTR):
                value = projected[b, 2, :, :, here]
                for k in several:
                    term = shares[k][b].astype(BF16).astype(F32)[None] * value
                    totals[k] = term if totals[k] is None else totals[k] + term
            for k in several:
                mixed[at_rows(first + k), here] = totals[k].reshape(width, 128).astype(BF16)

    cotangent.wait()
    for one in to_mixer:
        one.start()

    rows = cotangent.shape[0]
    source = group_row(
        info_ref,
        info_ref[FAR],
        info_ref[NEAR],
        lax.broadcasted_iota(jnp.int32, (1, lanes), 1),
        rows,
    )
    at = lax.broadcasted_iota(jnp.int32, (rows, lanes), 0)
    pick = jnp.where(at == source, 1.0, 0.0).astype(BF16)
    upstream_all[...] = dot_rows(cotangent[...], pick).astype(BF16)

    for piece in range(sections):
        g = info_ref[SECTION] ^ piece
        here = at_group(g)
        mixed_low = mixed[here, :]
        third = cells_ref[here, :].astype(F32) + dot(out_group_t[...], mixed_low)
        third = third.astype(BF16).astype(F32)
        normed, rate = normal_parts(apart(third), 1)
        low = (normed * mix_gain_wide[...][None]).astype(BF16).reshape(wide, lanes)
        hidden, slope = smooth_pair(dot(up_group_t[...], low))
        hidden = hidden.astype(BF16)
        change = jnp.concatenate([dot(down_t_ref[...], each_one) for each_one in each(hidden)], axis=0)
        result = (third + change).astype(BF16)
        results[min(piece, 2)][(piece // 3) * wide : (piece // 3 + 1) * wide, :] = result
        upstream = upstream_all[here, :]
        sums_ref[down_at] += dot_last(along(upstream), along(hidden))
        lifted_grad = (slope * dot(down_group[...], upstream)).astype(BF16)
        sums_ref[up_at] += dot_last(along(low), along(lifted_grad))
        normed_grad = apart(
            jnp.concatenate([dot(up_ref[...], each_one) for each_one in each(lifted_grad)], axis=0)
        )
        mix_gain_sum[...] += jnp.sum(normed_grad * normed, axis=0)
        back = normal_back(normed, rate, normed_grad * mix_gain_wide[...][None], 1)
        third_grad = (upstream.astype(F32) + back.reshape(wide, lanes)).astype(BF16)
        sum_grad[here, :] = third_grad
        sums_ref[out_at] += dot_last(along(third_grad), along(mixed_low))
        part = dot(out_group[...], third_grad).astype(BF16).astype(F32)
        mixed_grad[pl.ds(g * group, group)] = part.reshape(group, small, heads, lanes)

    for block in range(lane_blocks):
        here = slice(block * 128, block * 128 + 128)

        @pl.loop(0, ATTR, step=TOGETHER)
        def _(first):
            several = range(TOGETHER)
            pulled = [mixed_grad[first + k, :, :, here] for k in several]
            share_grads = [[] for _ in several]
            for b in range(ATTR):
                value = projected[b, 2, :, :, here]
                for k in several:
                    share_grads[k].append(jnp.sum(pulled[k] * value, axis=0))
            grads = []
            for k in several:
                shares = [shares_kept[first + k, b, :, here] for b in range(ATTR)]
                products = [s * g for s, g in zip(shares, share_grads[k])]
                centre = functools.reduce(jnp.add, products)
                grads.append([])
                for b in range(ATTR):
                    grad = (products[b] - shares[b] * centre).astype(BF16).astype(F32)
                    score_grads[first + k, b, :, here] = grad
                    shares_kept[first + k, b, :, here] = shares[b].astype(BF16).astype(F32)
                    grads[k].append(grad)
            totals = [None for _ in several]
            for b in range(ATTR):
                key = projected[b, 1, :, :, here]
                for k in several:
                    term = grads[k][b][None] * key
                    totals[k] = term if totals[k] is None else totals[k] + term
            for k in several:
                total = (totals[k] * scale).reshape(width, 128)
                mixed[at_rows(first + k), here] = total.astype(BF16)

        @pl.loop(0, ATTR, step=TOGETHER)
        def _(first):
            several = range(TOGETHER)
            key_grads = [None for _ in several]
            value_grads = [None for _ in several]
            for a in range(ATTR):
                query, pulled = projected[a, 0, :, :, here], mixed_grad[a, :, :, here]
                for k in several:
                    term = score_grads[a, first + k, :, here][None] * query
                    key_grads[k] = term if a == 0 else key_grads[k] + term
                    term = shares_kept[a, first + k, :, here][None] * pulled
                    value_grads[k] = term if a == 0 else value_grads[k] + term
            for k in several:
                projected[first + k, 1, :, :, here] = key_grads[k] * scale
                projected[first + k, 2, :, :, here] = value_grads[k]

    for g in range(sections):
        here = at_group(g)
        query_grads = each(mixed[here, :])
        grads = []
        for k in range(group):
            key_value = projected[g * group + k, 1:3].reshape(2 * width, lanes).astype(BF16)
            grads.append(jnp.concatenate([query_grads[k], key_value], axis=0))
        sums_ref[qkv_at] += dot_last(
            along(normed_low[here, :]), jnp.concatenate(grads, axis=1)
        )
        normed_grad = jnp.concatenate([dot(qkv_heads[...], grad) for grad in grads], axis=0)
        normed_grad = apart(normed_grad)
        normed, rate = normal_parts(apart(cells_ref[here, :].astype(F32)), 1)
        gain_sum[...] += jnp.sum(normed_grad * normed, axis=0)
        back = normal_back(normed, rate, normed_grad * gain_wide[...][None], 1)
        turned_grad[here, :] = sum_grad[here, :].astype(F32) + back.reshape(wide, lanes)

    cells_grad_ref[...] = turned_grad[...].T.astype(BF16)
    lane = lax.broadcasted_iota(jnp.int32, (width, 128), 1)
    first = jnp.sum(gain_sum[...], axis=1, keepdims=True)
    second = jnp.sum(mix_gain_sum[...], axis=1, keepdims=True)
    sums_ref[gain_at] = jnp.where(
        lane == 0, first, jnp.where(lane == 1, second, 0.0)
    )
    rows = sums_ref.shape[0]
    for half in range(2):
        at = 2 * wide + half * rows
        part = sums_ref[:, half * hidden_width : (half + 1) * hidden_width]
        results[2][at : at + rows, :] = part.astype(BF16)
    for one in to_mixer:
        one.wait()


def column_layers(
    info, cells, cotangent, gain, qkv, out, mix_gain, up, down, mixer_up, mixer_down, sections
):
    depth, lanes = cells.shape
    width = depth // ATTR
    small = width // HEADS_ATTR
    hidden = up.shape[1]
    wide = width * (ATTR // sections)
    piece = depth // sections
    out_shape = [
        shape_of((piece, lanes), BF16),
        shape_of((piece, lanes), BF16),
        shape_of((2 * piece + 4 * width, lanes), BF16),
        shape_of((lanes, depth), BF16),
        shape_of((2 * width, 2 * hidden), F32),
        shape_of(mixer_up.shape, BF16),
        shape_of(mixer_down.shape, BF16),
    ]
    arrays = (
        cells, cotangent, gain[None], qkv, out, mix_gain[None], up, down.T, mixer_up, mixer_down
    )
    results = call(
        functools.partial(column_kernel, width=width, small=small, sections=sections),
        "column_layers",
        info,
        arrays,
        out_shape,
        scratch=[
            pltpu.VMEM((ATTR, 3, small, HEADS_ATTR, lanes), F32),
            pltpu.VMEM((depth, lanes), BF16),
            pltpu.VMEM((ATTR, ATTR, HEADS_ATTR, lanes), F32),
            pltpu.VMEM((ATTR, ATTR, HEADS_ATTR, lanes), F32),
            pltpu.VMEM((depth, lanes), BF16),
            pltpu.VMEM((ATTR, small, HEADS_ATTR, lanes), F32),
            pltpu.VMEM((depth, lanes), BF16),
            pltpu.VMEM((depth, lanes), F32),
            pltpu.VMEM((depth, lanes), BF16),
            pltpu.VMEM((width, lanes), F32),
            pltpu.VMEM((width, lanes), F32),
            pltpu.VMEM((width, lanes), F32),
            pltpu.VMEM((width, lanes), F32),
            pltpu.VMEM((3 * wide, wide), BF16),
            pltpu.VMEM((wide, wide), BF16),
            pltpu.VMEM((wide, wide), BF16),
            pltpu.VMEM((hidden * wide // width, wide), BF16),
            pltpu.VMEM((hidden * wide // width, wide), BF16),
            pltpu.VMEM((width, 3 * width), BF16),
            pltpu.SemaphoreType.DMA((2,)),
        ],
        vmem=26,
        raw=(8, 9),
        near_out=(5, 6),
        far_in=(0, 1),
        micros=24,
    )
    return results[:3], *results[3:]


def column_finish(sums, refs):
    gain_ref, qkv_ref, out_ref, mix_gain_ref, up_ref, down_t_ref = refs
    width, hidden = up_ref.shape
    small = width // HEADS_ATTR
    up_ref[...] = sums[:width, :hidden]
    down_t_ref[...] = sums[:width, hidden : 2 * hidden]
    low = sums[width : 2 * width]
    qkv_ref[...] = jnp.dot(
        low[:, : 3 * width],
        head_order(3 * width, small).astype(F32),
        precision=lax.Precision.HIGHEST,
        preferred_element_type=F32,
    )
    out_ref[...] = lax.dot_general(
        head_order(width, small).astype(F32),
        low[:, 3 * width : 4 * width],
        (((0,), (1,)), ((), ())),
        precision=lax.Precision.HIGHEST,
        preferred_element_type=F32,
    )
    eye = lax.broadcasted_iota(jnp.int32, (width, width), 0) == lax.broadcasted_iota(
        jnp.int32, (width, width), 1
    )
    for k, ref in enumerate((gain_ref, mix_gain_ref)):
        at = 4 * width + k
        ref[...] = jnp.sum(jnp.where(eye, low[:, at : at + 1], 0.0), axis=0, keepdims=True)


def body(
    features,
    cotangent,
    row_counts,
    key_valid,
    attend_gain,
    attend_qkv,
    attend_out,
    mixer_gain,
    mixer_up,
    mixer_down,
    column_gain,
    column_qkv,
    column_out,
    column_mix_gain,
    column_up,
    column_down,
):
    dp_count, sections = lax.axis_size("dp"), lax.axis_size("section")
    dp_at, section_at = lax.axis_index("dp"), lax.axis_index("section")
    core, near, far = dp_at & 1, section_at & 1, section_at >> 1
    bits = (dp_count // 2).bit_length() - 1
    blocks = dp_count * sections
    group_rows, width = features.shape
    hidden = mixer_up.shape[1]
    entries = (core, near, far, dp_at >> 1, section_at)
    lane = lax.iota(jnp.int32, COUNTS)
    place = sum(jnp.where(lane == k, entry.astype(jnp.int32), 0) for k, entry in enumerate(entries))
    info = jnp.concatenate([place, row_counts[0]])

    def near_of(array):
        return exchanged(array, "section", 1)

    def core_of(array):
        return exchanged(array, "dp", 1)

    own_x, half_normed, projected, mask, shared, first, slope, second_t = attend(
        info, features, key_valid[None], attend_gain[None], attend_qkv, attend_out,
        mixer_gain[None], mixer_up, mixer_down,
    )
    shared_near, shared_core = near_of(shared), core_of(shared)
    half_core = core_of(half_normed)

    result_pieces, second_grad, column_sums, near_up, near_down = column_layers(
        info, second_t, cotangent, column_gain, column_qkv, column_out, column_mix_gain,
        column_up, column_down, mixer_up, mixer_down, sections,
    )
    shared_near, shared_core, half_core = ordered(
        (shared_near, shared_core, half_core), second_grad
    )
    grad_near, grad_core = near_of(second_grad), core_of(second_grad)
    shared_both = core_of(shared_near)

    first_grad = mixer_back(
        info, second_grad, slope, first, mixer_gain[None], near_up, near_down
    )
    first_near = near_of(first_grad)

    pool = ordered((shared, shared_near, shared_core, shared_both), first_grad)
    pool_hidden, pool_slope = pool_forward(info, pool, mixer_up, blocks)
    (grad_core,) = ordered((grad_core,), pool_hidden)
    (grad_near,) = ordered((grad_near,), pool_hidden)
    second_pool = (second_grad, grad_near, grad_core, core_of(grad_near))
    down_parts = down_gradient(info, pool_hidden, second_pool, blocks, bits)
    result_far = exchanged(result_pieces[2], "section", 2)
    sums = Sums(info, bits, down_parts[0].shape[1:])
    sums.step(new=("down", down_parts), far_at=1)
    (slope_later,) = ordered((pool_slope,), *sums.sent)
    up_parts = up_gradient(info, slope_later, pool, second_pool, mixer_down, blocks, bits)
    quarter = width // sections
    sums.small = (column_sums, 0), column_sums.shape[0] // sums.block[0]
    sums.fresh = result_far, 2 * quarter

    sums.step("down", new=("up", up_parts), small=True, hold=("far",))
    down_far = sums.handles["far"]
    first_near, own_grad = ordered((first_near, first_grad), *sums.sent)
    near_pieces = ordered((result_pieces[1], result_far[quarter : 2 * quarter]), *sums.sent)
    result_near = near_of(jnp.concatenate(near_pieces, axis=0))
    kept, sent, e_own, e_sent = attend_back(
        info, projected, mask, own_grad, first_near, attend_out, attend_qkv
    )
    sent_came = core_of(sent)
    sums.release(down_far, kept)
    sums.step("up", small=True, before=(result_near,), micros=40)
    settled = sums.sent
    (sent_came,) = ordered((sent_came,), *settled)
    attend_parts = attend_gradient(
        info, (half_normed, half_core), pool, (kept, sent_came), blocks, bits
    )
    (e_sent,) = ordered((e_sent,), *settled)
    e_near = near_of(e_sent)
    sums.step(new=("attend", attend_parts))
    for _ in range(bits - 1):
        sums.step("up", small=True, before=sums.sent)
    (e_near,) = ordered((e_near,), sums.messages[down_far], *sums.sent)
    input_pieces = last_norm(
        info, e_own, e_near, first_grad, own_x, attend_gain[None], sections
    )
    far_came = exchanged(input_pieces[2], "section", 2)
    for _ in range(bits - 1):
        sums.step("down", "attend", before=input_pieces[:1])
    up_far = sums.messages[sums.gradients["up"][0]["sent"][0]]
    (result_near,) = ordered((result_near,), *sums.sent)
    pieces = [result_pieces[0], result_near[:quarter], result_far[:quarter], result_near[quarter:]]
    result = placed(info, pieces, features.dtype, True, 20)
    (mixer_down_grad,) = sums.step("down", "attend", small=True, before=(result, up_far))
    (far_came,) = ordered((far_came,), *sums.sent)
    own = far_came.shape[0] // 2
    near_came = near_of(jnp.concatenate([input_pieces[1], far_came[own:]], axis=0))

    rest = width // blocks
    pieces = quad_pieces(info, sums, ("up", "attend"), rest)
    (near_came,) = ordered((near_came,), pieces[0])
    input_grad = placed(
        info,
        [input_pieces[0], near_came[:own], far_came[:own], near_came[own:]],
        F32,
        False,
        20,
    )
    moves = [(at, at ^ (sections + 1)) for at in range(blocks)]
    pieces = (
        pieces[0],
        exchanged(pieces[1], "section", 1),
        exchanged(pieces[2], "dp", 1),
        lax.ppermute(pieces[3], ("dp", "section"), moves),
    )

    own_block = dp_at * sections + section_at
    (own_block,) = ordered((own_block,), *sums.sent)

    def own_rows(array):
        return lax.dynamic_slice_in_dim(array, own_block * rest, rest, 0)

    (
        mixer_up_grad, mixer_gain_grad, attend_qkv_grad, attend_out_grad, attend_gain_grad,
        column_grads,
    ) = finish(
        info,
        pieces,
        sums,
        mixer_up if rest % 16 == 0 else own_rows(mixer_up),
        attend_qkv if rest % 16 == 0 else own_rows(attend_qkv),
        own_rows(mixer_gain),
        own_rows(attend_gain),
        hidden // blocks,
        column_gain.shape[0],
        column_up.shape[1],
    )

    return (
        result,
        input_grad,
        attend_gain_grad,
        attend_qkv_grad,
        attend_out_grad,
        mixer_gain_grad,
        mixer_up_grad,
        mixer_down_grad,
        *column_grads,
    )


def solution(mesh):
    split = P(("dp", "section"))
    return jax.shard_map(
        body,
        mesh=mesh,
        in_specs=(P("dp", None), P("dp", None), P("dp", None), P("dp")) + (P(),) * 12,
        out_specs=(P("dp", "section"),) * 2 + (split,) * 6 + (P(),) * 6,
        check_vma=False,
    )
```

```python
import functools

import jax
import jax.numpy as jnp
from jax import lax
from jax.experimental import pallas as pl
from jax.experimental.pallas import tpu as pltpu
from jax.sharding import PartitionSpec as P

ATTR = 16
HEADS = 8
HEADS_ATTR = 8

EPSILON = 1e-05
MASKED = -1e30
GELU_SCALE = 0.7978845608028654
GELU_CUBE = 0.044715
BF16 = jnp.bfloat16
F32 = jnp.float32

FLOPS, BYTES = 1.10e+09, 3.60e+06

CORE, NEAR, FAR, CHIP, SECTION, COUNTS = range(6)


def exchanged(value, axis, mask):
    count = lax.axis_size(axis)
    return lax.ppermute(value, axis, [(at, at ^ mask) for at in range(count)])


def normal_parts(vector, axis=-1):
    centred = vector - jnp.mean(vector, axis=axis, keepdims=True)
    rate = lax.rsqrt(jnp.mean(centred * centred, axis=axis, keepdims=True) + EPSILON)
    return centred * rate, rate


def normal_back(normed, rate, scaled, axis=-1):
    middle = jnp.mean(scaled, axis=axis, keepdims=True)
    along = jnp.mean(scaled * normed, axis=axis, keepdims=True)
    return rate * (scaled - middle - normed * along)


def smooth_pair(inputs):
    square = inputs * inputs
    bent = jnp.tanh(GELU_SCALE * inputs * (1.0 + GELU_CUBE * square))
    half = 0.5 * (1.0 + bent)
    slope = half + (0.5 * GELU_SCALE) * inputs * (1.0 - bent * bent) * (
        1.0 + (3.0 * GELU_CUBE) * square
    )
    return inputs * half, slope


def dot(left, right):
    return jnp.dot(left, right, preferred_element_type=F32)


def dot_rows(left, right):
    return lax.dot_general(left, right, (((0,), (0,)), ((), ())), preferred_element_type=F32)


def dot_last(left, right):
    return lax.dot_general(left, right, (((1,), (1,)), ((), ())), preferred_element_type=F32)


def shape_of(dims, dtype):
    return jax.ShapeDtypeStruct(dims, dtype)


class Joined:
    def __init__(self, *pieces, far=()):
        self.pieces, self.far = pieces, far
        self.shape = (sum(rows for _, _, rows in pieces), *pieces[0][0].shape[1:])
        self.dtype = pieces[0][0].dtype


class Arriving:
    def __init__(self, pieces, ref, sems):
        self.ref, self.shape, self.dtype = ref, ref.shape, ref.dtype
        self.copies, at = [], 0
        for k, (source, first, rows) in enumerate(pieces):
            target = ref
            if len(pieces) > 1:
                source, target = source.at[pl.ds(first, rows)], ref.at[pl.ds(at, rows)]
            self.copies.append(pltpu.make_async_copy(source, target, sems[k]))
            at += rows
        for copy in self.copies:
            copy.start()

    def wait(self):
        for copy in self.copies:
            copy.wait()
        self.copies = []

    def __getitem__(self, at):
        self.wait()
        return self.ref[at]


class Leaving:
    def __init__(self, target, ref, sem):
        self.ref, self.shape, self.dtype = ref, ref.shape, ref.dtype
        self.copy, self.started = pltpu.make_async_copy(ref, target, sem), False

    def __getitem__(self, at):
        return self.ref[at]

    def __setitem__(self, at, value):
        self.ref[at] = value

    def send(self):
        if not self.started:
            self.copy.start()
            self.started = True


def call(
    body, name, info, arrays, out_shape, scratch=(), vmem=16, raw=(), far_in=(), far_out=(), near_in=(),
    near_out=(), plain=False, micros=0,
    blocks=None,
):
    options = dict(
        compiler_params=pltpu.CompilerParams(vmem_limit_bytes=vmem * 2**20),
        cost_estimate=pl.CostEstimate(
            flops=int(micros * FLOPS), bytes_accessed=int(micros * BYTES), transcendentals=0
        ),
        name=name,
    )
    if plain:

        def whole(array, at=None):
            if blocks is not None and at in blocks:
                return pl.BlockSpec(*blocks[at])
            return pl.BlockSpec(array.shape, lambda *_: (0,) * len(array.shape))

        spec = pltpu.PrefetchScalarGridSpec(
            num_scalar_prefetch=1,
            grid=(1,),
            in_specs=[whole(array, at) for at, array in enumerate(arrays)],
            out_specs=[whole(shape) for shape in out_shape],
            scratch_shapes=scratch,
        )
        return pl.pallas_call(body, grid_spec=spec, out_shape=out_shape, **options)(info, *arrays)
    copied = [k for k in range(len(arrays)) if k not in raw and k not in near_in]
    flat, places, in_specs = [], [], []
    for k, array in enumerate(arrays):
        pieces = array.pieces if isinstance(array, Joined) else [(array, 0, array.shape[0])]
        places.append([(len(flat) + n, first, rows) for n, (_, first, rows) in enumerate(pieces)])
        for n, (piece, _, _) in enumerate(pieces):
            if k in raw or k in far_in or n in getattr(array, "far", ()):
                piece = pltpu.with_memory_space_constraint(piece, pltpu.HBM)
            if k in near_in:
                piece = pltpu.with_memory_space_constraint(piece, pltpu.VMEM)
            flat.append(piece)
            in_specs.append(
                pl.BlockSpec(memory_space=pltpu.VMEM if k in near_in else pl.ANY)
            )
    count, outs = len(flat), len(out_shape)
    leaving = [k for k in range(outs) if k not in near_out]

    def run(info_ref, *refs):
        given, made, rest = refs[:count], refs[count : count + outs], refs[count + outs :]
        held, rest = rest[: len(copied)], rest[len(copied) :]
        out_held, rest = rest[: len(leaving)], rest[len(leaving) :]
        in_sems, out_sems, *rest = rest
        inputs = []
        for k in range(len(arrays)):
            if k in raw or k in near_in:
                inputs.append(given[places[k][0][0]])
                continue
            pieces = [
                (given[at], first, rows)
                for at, first, rows in places[k]
            ]
            sems = [in_sems.at[at] for at, _, _ in places[k]]
            inputs.append(Arriving(pieces, held[copied.index(k)], sems))
        outputs = [
            Leaving(made[k], out_held[leaving.index(k)], out_sems.at[k]) if k in leaving else made[k]
            for k in range(outs)
        ]
        body(info_ref, *inputs, *outputs, *rest)
        outputs = [outputs[k] for k in leaving]
        for one in inputs:
            if isinstance(one, Arriving):
                one.wait()
        for one in outputs:
            one.send()
        for one in outputs:
            one.copy.wait()

    def in_vmem(array):
        return pltpu.VMEM(array.shape, array.dtype)

    plain_out = out_shape
    out_shape = list(out_shape)
    for k, shape in enumerate(plain_out):
        if k in far_out or k in near_out:
            space = pltpu.HBM if k in far_out else pltpu.VMEM
            out_shape[k] = space(shape.shape, shape.dtype)
    spec = pltpu.PrefetchScalarGridSpec(
        num_scalar_prefetch=1,
        grid=(),
        in_specs=in_specs,
        out_specs=[
            pl.BlockSpec(memory_space=pltpu.VMEM if k in near_out else pl.ANY) for k in range(outs)
        ],
        scratch_shapes=[in_vmem(arrays[k]) for k in copied]
        + [in_vmem(plain_out[k]) for k in leaving]
        + [pltpu.SemaphoreType.DMA((count,)), pltpu.SemaphoreType.DMA((outs,))]
        + list(scratch),
    )
    return pl.pallas_call(run, grid_spec=spec, out_shape=out_shape, **options)(info, *flat)


def picked(source, columns):
    at = lax.broadcasted_iota(jnp.int32, (source.shape[0], columns), 1)
    return jnp.where(at == source, 1.0, 0.0).astype(BF16)


def bounds_of(info_ref):
    bounds, bound = [], jnp.int32(0)
    for k in range(COUNTS, info_ref.shape[0]):
        bound = bound + info_ref[k]
        bounds.append(bound)
    return bounds


def group_row(info_ref, far, near, at, rows):
    start = jnp.int32(0)
    for k, bound in enumerate(bounds_of(info_ref)):
        start = jnp.where(info_ref[COUNTS + k] == rows // 2, bound - rows // 2, start)
    source = at + (start + far * (rows // 2) + near * (rows // 4))
    return jnp.where(source >= rows, source - rows, source)


def softmax_parts(queries, keys, allowed, scale):
    scores = jnp.where(allowed, dot_last(queries, keys) * scale, MASKED)
    lifted = jnp.exp(scores - jnp.max(scores, axis=-1, keepdims=True))
    return lifted * (1.0 / jnp.sum(lifted, axis=-1, keepdims=True))


def attend_kernel(
    info_ref, features, valid_ref, gain_ref, qkv_hbm, out_hbm, next_gain_ref, up_hbm, down_hbm,
    own_ref, normed_ref, projected_ref, mask_ref, shared_ref, first_ref, slope_ref,
    turned_ref, weights, out, ups, downs, sems, *, head_dim,
):
    rows, width = features.shape
    half, own = rows // 2, rows // 4
    pair = 2 * head_dim

    def copy(source, target, at):
        return pltpu.make_async_copy(source, target, sems.at[at])

    to_weights = copy(qkv_hbm, weights, 0)
    to_out = copy(out_hbm, out, 1)
    to_mixer = [copy(up_hbm, ups, 2), copy(down_hbm, downs, 3)]
    to_weights.start()

    near, far = info_ref[NEAR], info_ref[FAR]

    def source_of(at):
        side = jnp.where(at < own, near, 1 - near)
        return group_row(info_ref, far, side, jnp.where(at < own, at, at - own), rows)

    row_source = source_of(lax.broadcasted_iota(jnp.int32, (half, 1), 0))
    lane_source = source_of(lax.broadcasted_iota(jnp.int32, (1, half), 1))
    pick = picked(row_source, rows)
    row_segment = jnp.zeros((half, 1), jnp.int32)
    lane_segment = jnp.zeros((1, half), jnp.int32)
    for bound in bounds_of(info_ref):
        row_segment += (row_source >= bound).astype(jnp.int32)
        lane_segment += (lane_source >= bound).astype(jnp.int32)
    valid = valid_ref[...].astype(F32).astype(BF16)
    usable = dot_last(jnp.broadcast_to(valid, (8, rows)), pick)[:1]
    same = lax.broadcasted_iota(jnp.int32, (half, half), 0) == lax.broadcasted_iota(
        jnp.int32, (half, half), 1
    )
    allowed = (row_segment == lane_segment) & ((usable > 0.5) | same)
    mask_ref[...] = jnp.where(allowed, 1.0, 0.0)
    features.wait()
    to_out.start()
    taken = dot(pick, features[...])
    own_ref[...] = taken[:own].astype(BF16)
    normed, _ = normal_parts(taken)
    normed_ref[...] = (normed * gain_ref[...]).astype(BF16)

    to_weights.wait()
    projected_ref[...] = dot(normed_ref[...], weights[...]).astype(BF16)
    projected_ref.send()
    normed_ref.send()
    mask_ref.send()
    own_ref.send()
    for one in to_mixer:
        one.start()

    @pl.loop(0, width // pair)
    def _(step):
        def columns(first):
            return pl.ds(pl.multiple_of(first + step * pair, pair), pair)

        queries = projected_ref[:own, columns(0)]
        keys = projected_ref[:, columns(width)]
        values = projected_ref[:, columns(2 * width)]
        open_ = mask_ref[:own, :] > 0
        mixed = []
        for head in range(2):
            here = slice(head * head_dim, (head + 1) * head_dim)
            shares = softmax_parts(queries[:, here], keys[:, here], open_, head_dim**-0.5)
            mixed.append(dot(shares.astype(BF16), values[:, here]).astype(BF16))
        shared_ref[own:, columns(0)] = jnp.concatenate(mixed, axis=1)

    to_out.wait()
    first = own_ref[...].astype(F32) + dot(shared_ref[own:, :], out[...])
    first_ref[...] = first.astype(BF16)
    total = first_ref[...].astype(F32)
    normed, _ = normal_parts(total)
    shared_ref[:own, :] = (normed * next_gain_ref[...]).astype(BF16)
    shared_ref.send()
    first_ref.send()

    for one in to_mixer:
        one.wait()
    hidden, slope = smooth_pair(dot(shared_ref[:own, :], ups[...]))
    slope_ref[...] = slope.astype(BF16)
    slope_ref.send()
    turned_ref[...] = (total + dot(hidden.astype(BF16), downs[...])).T.astype(BF16)


def attend(info, features, valid, gain, qkv, out, next_gain, up, down):
    rows, width = features.shape
    half, own = rows // 2, rows // 4
    wide, hidden = qkv.shape[1], up.shape[1]
    return call(
        functools.partial(attend_kernel, head_dim=width // HEADS),
        "attend",
        info,
        (features, valid, gain, qkv, out, next_gain, up, down),
        [
            shape_of((own, width), BF16),
            shape_of((half, width), BF16),
            shape_of((half, wide), BF16),
            shape_of((half, half), F32),
            shape_of((half, width), BF16),
            shape_of((own, width), BF16),
            shape_of((own, hidden), BF16),
            shape_of((width, own), BF16),
        ],
        raw=(3, 4, 6, 7),
        far_in=(0, 1, 2, 5),
        far_out=(0, 1, 2, 3, 5, 6, 7),
        scratch=[
            pltpu.VMEM((width, wide), BF16),
            pltpu.VMEM((width, width), BF16),
            pltpu.VMEM((width, hidden), BF16),
            pltpu.VMEM((hidden, width), BF16),
            pltpu.SemaphoreType.DMA((4,)),
        ],
        vmem=56,
        micros=20,
    )


def attend_back_kernel(
    info_ref, grad, projected, mask, out_hbm, qkv_hbm,
    kept_ref, sent_ref, e_own_ref, e_sent_ref, out, weights, grads, sems, *, head_dim,
):
    rows, width = grad.shape
    own, quarter = rows // 2, width // 4
    heads = HEADS // 2
    wide = heads * head_dim
    scale = head_dim**-0.5
    near = info_ref[NEAR]
    first = pl.multiple_of(near * wide, wide)
    to_out = pltpu.make_async_copy(out_hbm.at[pl.ds(first, wide), :], out, sems.at[0])
    to_weights = [
        pltpu.make_async_copy(
            qkv_hbm.at[:, pl.ds(pl.multiple_of(first + k * width, wide), wide)],
            weights.at[:, pl.ds(k * wide, wide)],
            sems.at[1 + k],
        )
        for k in range(3)
    ]
    to_out.start()
    for one in to_weights:
        one.start()

    to_out.wait()
    pulled = dot_last(grad[...], out[...]).astype(BF16)
    projected.wait()
    mask.wait()
    allowed = mask[...] > 0

    def columns(which):
        return projected.ref[:, pl.ds(pl.multiple_of(first + which * width, wide), wide)]

    all_queries, all_keys, all_values = columns(0), columns(1), columns(2)
    for head in range(heads):
        at = slice(head * head_dim, (head + 1) * head_dim)
        queries, keys, values = all_queries[:, at], all_keys[:, at], all_values[:, at]
        shares = softmax_parts(queries, keys, allowed, scale)
        share_grad = dot_last(pulled[:, at], values)
        centre = jnp.sum(share_grad * shares, axis=-1, keepdims=True)
        score_grad = (shares * (share_grad - centre)).astype(BF16)
        grads[:, at] = (dot(score_grad, keys) * scale).astype(BF16)
        at = slice(wide + head * head_dim, wide + (head + 1) * head_dim)
        grads[:, at] = (dot_rows(score_grad, queries) * scale).astype(BF16)
        at = slice(2 * wide + head * head_dim, 2 * wide + (head + 1) * head_dim)
        grads[:, at] = dot_rows(shares.astype(BF16), pulled[:, head * head_dim : (head + 1) * head_dim]).astype(BF16)
    core = info_ref[CORE]
    for target, side in ((sent_ref, 1 - core), (kept_ref, core)):
        for k in range(3):
            place = pl.multiple_of(k * wide + side * (wide // 2), wide // 2)
            target[:, k * quarter : (k + 1) * quarter] = grads[:, pl.ds(place, wide // 2)]
        place = pl.multiple_of((side * 2 + near) * quarter, quarter)
        target[:, 3 * quarter :] = grad.ref[:, pl.ds(place, quarter)]
        target.send()
    for one in to_weights:
        one.wait()
    summed = dot_last(grads[...], weights[...])
    e_own_ref[...] = summed[:own]
    e_sent_ref[...] = summed[own:].astype(BF16)


def attend_back(info, projected, mask, own_grad, near_grad, out, qkv):
    own, width = own_grad.shape
    rows = 2 * own
    wide = width // 2
    return call(
        functools.partial(attend_back_kernel, head_dim=width // HEADS),
        "attend_back",
        info,
        (Joined((own_grad, 0, own), (near_grad, 0, own)), projected, mask, out, qkv),
        [
            shape_of((rows, width), BF16),
            shape_of((rows, width), BF16),
            shape_of((own, width), F32),
            shape_of((own, width), BF16),
        ],
        raw=(3, 4),
        far_in=(1, 2),
        scratch=[
            pltpu.VMEM((wide, width), BF16),
            pltpu.VMEM((width, 3 * wide), BF16),
            pltpu.VMEM((rows, 3 * wide), BF16),
            pltpu.SemaphoreType.DMA((4,)),
        ],
        vmem=24,
        micros=11,
        far_out=(0,),
    )


def last_kernel(info_ref, e_own_ref, e_near_ref, grad_ref, x_ref, gain_ref, *refs):
    pieces, held = refs[:-1], refs[-1]
    upstream = e_own_ref[...] + e_near_ref[...].astype(F32)
    normed, rate = normal_parts(x_ref[...].astype(F32))
    back = normal_back(normed, rate, upstream * gain_ref[...])
    held[...] = grad_ref[...].astype(F32) + back
    own, quarter = held.shape[0], pieces[0].shape[1]
    for mask in range(4):
        at = pl.multiple_of((info_ref[SECTION] ^ mask) * quarter, quarter)
        value = held[:, pl.ds(at, quarter)].astype(BF16)
        pieces[min(mask, 2)][(mask // 3) * own : (mask // 3 + 1) * own, :] = value


def last_norm(info, e_own, e_near, grad, x, gain, sections):
    own, width = x.shape
    return call(
        last_kernel,
        "last_norm",
        info,
        (e_own, e_near, grad, x, gain),
        [
            shape_of((own, width // sections), BF16),
            shape_of((own, width // sections), BF16),
            shape_of((2 * own, width // sections), BF16),
        ],
        scratch=[pltpu.VMEM((own, width), F32)],
        plain=True,
        micros=20,
        vmem=8,
    )


def place_kernel(info_ref, *refs, turned):
    pieces, out_ref = refs[:-1], refs[-1]
    rows = out_ref.shape[0]
    own = rows // 4
    at = lax.broadcasted_iota(jnp.int32, (own, 1), 0)
    total = None
    for mask, piece in enumerate(pieces):
        section = info_ref[SECTION] ^ mask
        pick = picked(group_row(info_ref, section >> 1, section & 1, at, rows), rows)
        if turned:
            part = lax.dot_general(
                pick, piece[...], (((0,), (1,)), ((), ())), preferred_element_type=F32
            )
        else:
            part = dot_rows(pick, piece[...])
        total = part if total is None else total + part
    out_ref[...] = total.astype(out_ref.dtype)


def placed(info, pieces, dtype, turned, micros=0):
    own = pieces[0].shape[1 if turned else 0]
    quarter = pieces[0].shape[0 if turned else 1]
    rows = own * len(pieces)
    return call(
        functools.partial(place_kernel, turned=turned),
        "placed",
        info,
        pieces,
        [shape_of((rows, quarter), dtype)],
        plain=True,
        micros=micros,
        vmem=8,
    )[0]


def part_copies(info_ref, weight_hbm, held, sems, part, axis):
    quarter = held.shape[axis]
    copies = []
    width = part if part % 128 == 0 else quarter
    for k in range(quarter // width):
        first = hidden_block(k, info_ref) * part if width == part else 0
        source, target = pl.ds(pl.multiple_of(first, width), width), pl.ds(k * width, width)
        if axis == 1:
            pair = weight_hbm.at[:, source], held.at[:, target]
        else:
            pair = weight_hbm.at[source, :], held.at[target, :]
        copies.append(pltpu.make_async_copy(*pair, sems.at[k]))
    for copy in copies:
        copy.start()
    return copies, width


def mixer_back_kernel(info_ref, grad, slope, first, gain, ups, downs, out_ref):
    pulled = dot_last(grad[...], downs[...])
    lifted = (slope[...].astype(F32) * pulled).astype(BF16)
    total = dot_last(lifted, ups[...])
    normed, rate = normal_parts(first[...].astype(F32))
    back = normal_back(normed, rate, total * gain[...])
    out_ref[...] = (grad[...].astype(F32) + back).astype(BF16)


def mixer_back(info, grad, slope, first, gain, up, down):
    return call(
        mixer_back_kernel,
        "mixer_back",
        info,
        (grad, slope, first, gain, up, down),
        [shape_of(grad.shape, BF16)],
        vmem=24,
        far_in=(1, 2, 3),
        near_in=(4, 5),
        micros=60,
    )[0]


def pool_kernel(info_ref, pool, up_hbm, hidden_ref, slope_ref, held, sems, *, part):
    copies, _ = part_copies(info_ref, up_hbm, held, sems, part, 1)
    for copy in copies:
        copy.wait()
    hidden, slope = smooth_pair(dot(pool[...], held[...]))
    hidden_ref[...] = hidden.astype(BF16)
    hidden_ref.send()
    slope_ref[...] = slope.astype(BF16)


def pool_forward(info, shared, up, blocks):
    own, width = shared[0].shape[0] // 2, shared[0].shape[1]
    hidden = up.shape[1]
    quarter, part = hidden // 4, hidden // blocks
    pool = Joined(*[(array, 0, own) for array in shared])
    return call(
        functools.partial(pool_kernel, part=part),
        "pool_forward",
        info,
        (pool, own_quarter(info, up, blocks, 1)),
        [shape_of((pool.shape[0], quarter), BF16)] * 2,
        scratch=[pltpu.VMEM((width, quarter), BF16), pltpu.SemaphoreType.DMA((blocks // 4,))],
        vmem=24,
        raw=(1,),
        far_out=(0, 1),
        micros=60,
    )


def hidden_block(at, info):
    return (((at // 2) * 2 + info[CORE]) * 2 + at % 2) * 2 + info[NEAR]


def own_quarter(info, weight, blocks, axis):
    part = weight.shape[axis] // blocks
    if part % 128 == 0:
        return weight
    order = hidden_block(jnp.arange(blocks // 4), info)
    shape = weight.shape[:axis] + (blocks, part) + weight.shape[axis + 1 :]
    taken = jnp.take(weight.reshape(shape), order, axis=axis)
    return taken.reshape(weight.shape[:axis] + (-1,) + weight.shape[axis + 1 :])


def split_place(position, bit):
    chip, far = position >> 1, position & 1
    low = chip & ((1 << bit) - 1)
    rest = ((chip >> (bit + 1)) << bit) | low
    return (chip >> bit) & 1, rest * 2 + far


def halves_like(positions, rows, columns):
    return [shape_of((positions, rows, columns // 2), BF16)] * 2


def down_kernel(info_ref, grad, hidden, *refs, part, bits):
    outs, held = refs[:-1], refs[-1]
    grad.wait()
    held[...] = dot_rows(hidden[...], grad[...])
    store_positions(info_ref, outs, held, bits, (part, 1))


def down_gradient(info, hidden, grads, blocks, bits):
    pool, quarter = hidden.shape
    own, width = grads[0].shape
    part = quarter * 4 // blocks
    like = halves_like(blocks // 4, part, width)
    return call(
        functools.partial(down_kernel, part=part, bits=bits),
        "down_gradient",
        info,
        (Joined(*[(array, 0, own) for array in grads]), hidden),
        like,
        scratch=[pltpu.VMEM((quarter, width), F32)],
        vmem=20,
        micros=20,
        far_in=(1,),
    )


def store_positions(info_ref, outs, held, bits, layout):
    rest, quads = layout
    positions = held.shape[0] // (rest * quads)
    columns = held.shape[1] // 2
    own_place = info_ref[CHIP] * 2 + info_ref[FAR]
    for position in range(positions):
        source = position ^ own_place
        for quad in range(quads):
            if quads == 1:
                block = source
            else:
                block = (((source >> 1) * 2 + quad // 2) * 2 + (source & 1)) * 2 + quad % 2
            rows = pl.ds(pl.multiple_of(block * rest, rest), rest)
            for side, bit in enumerate((0, bits - 1)):
                goes, place = split_place(position, bit)
                place += side * positions // 2
                value = held[rows, side * columns : (side + 1) * columns]
                outs[goes][place, quad * rest : (quad + 1) * rest, :] = value.astype(BF16)


def up_kernel(info_ref, grad, slope, normed, down_hbm, *refs, part, bits):
    outs, (weight, lifted, total, sems) = refs[:2], refs[2:]
    copies, _ = part_copies(info_ref, down_hbm, weight, sems, part, 0)
    for copy in copies:
        copy.wait()
    pulled = dot_last(grad[...], weight[...])
    lifted[...] = (slope[...].astype(F32) * pulled).astype(BF16)
    total[...] = dot_rows(normed[...], lifted[...])
    store_positions(info_ref, outs, total, bits, (outs[0].shape[1] // 4, 4))


def up_gradient(info, slope, shared, grads, down, blocks, bits):
    pool, quarter = slope.shape
    hidden, width = down.shape
    own = grads[0].shape[0]
    like = halves_like(blocks // 4, width * 4 // blocks, quarter)
    return call(
        functools.partial(up_kernel, part=hidden // blocks, bits=bits),
        "up_gradient",
        info,
        (
            Joined(*[(array, 0, own) for array in grads]),
            slope,
            Joined(*[(array, 0, own) for array in shared]),
            own_quarter(info, down, blocks, 0),
        ),
        like,
        raw=(3,),
        scratch=[
            pltpu.VMEM((quarter, width), BF16),
            pltpu.VMEM((pool, quarter), BF16),
            pltpu.VMEM((width, quarter), F32),
            pltpu.SemaphoreType.DMA((blocks // 4,)),
        ],
        vmem=28,
        micros=8,
        far_in=(1, 2),
    )


def attend_grad_kernel(info_ref, normed, packs, mixed, *refs, bits):
    outs, total = refs[:-1], refs[-1]
    edge = total.shape[1] * 3 // 4
    total[:, :edge] = dot_rows(normed[...], packs[:, :edge])
    total[:, edge:] = dot_rows(mixed[...], packs[:, edge:])
    store_positions(info_ref, outs, total, bits, (outs[0].shape[1] // 4, 4))


def attend_gradient(info, normed, shared, packs, blocks, bits):
    half, width = normed[0].shape
    columns = packs[0].shape[1]
    own = half // 2
    like = halves_like(blocks // 4, width * 4 // blocks, columns)
    return call(
        functools.partial(attend_grad_kernel, bits=bits),
        "attend_gradient",
        info,
        (
            Joined(*[(array, 0, half) for array in normed]),
            Joined(*[(array, 0, half) for array in packs], far=(0,)),
            Joined(*[(array, own, own) for array in shared]),
        ),
        like,
        scratch=[pltpu.VMEM((width, columns), F32)],
        vmem=20,
        micros=0,
        far_in=(0, 2),
    )


def by_quad(info_ref, pieces):
    near, core = info_ref[NEAR] == 0, info_ref[CORE] == 0
    low = [jnp.where(near, pieces[k], pieces[k ^ 1]) for k in range(4)]
    return [jnp.where(core, low[k], low[k ^ 2]) for k in range(4)]


def gain_row(weight, grad, gain):
    total = jnp.sum(weight.astype(F32) * grad, axis=1, keepdims=True)
    eye = lax.broadcasted_iota(jnp.int32, (total.shape[0],) * 2, 0) == lax.broadcasted_iota(
        jnp.int32, (total.shape[0],) * 2, 1
    )
    return jnp.sum(jnp.where(eye, total, 0.0), axis=0, keepdims=True) / gain


def finish_kernel(info_ref, *refs, part, small, came):
    small_ref, came_ref, up_weight, qkv_weight, up_gain, qkv_gain = refs[4:10]
    up_ref, up_gain_ref, qkv_ref, out_ref, qkv_gain_ref = refs[10:15]
    pieces = by_quad(info_ref, [ref[...].astype(F32) for ref in refs[:4]])
    hidden = up_ref.shape[1] // 4
    quarter = out_ref.shape[1] // 4
    blocks = []
    for chip in range(hidden // (2 * part)):
        for core in range(2):
            for far in range(2):
                for near in range(2):
                    at = (chip * 2 + far) * part
                    blocks.append(pieces[core * 2 + near][:, at : at + part])
    up_ref[...] = jnp.concatenate(blocks, axis=1)
    for which in range(3):
        for near in range(2):
            for core in range(2):
                at = ((which * 2 + near) * 2 + core) * quarter
                source = hidden + which * quarter
                qkv_ref[:, at : at + quarter] = pieces[core * 2 + near][:, source : source + quarter]
    for k, piece in enumerate(pieces):
        out_ref[:, k * quarter : (k + 1) * quarter] = piece[:, hidden + 3 * quarter :]
    up_gain_ref[...] = gain_row(up_weight[...], up_ref[...], up_gain[...])
    qkv_gain_ref[...] = gain_row(qkv_weight[...], qkv_ref[...], qkv_gain[...])
    blocks = []
    for k in range(small[1]):
        blocks.append(small_ref[small[0] + k] + came_ref[came + k].astype(F32))
    column_finish(jnp.concatenate(blocks, axis=0), refs[15:])


def finish(info, pieces, sums, up, qkv, up_gain, qkv_gain, part, width, column_hidden):
    rest = pieces[0].shape[0]
    hidden, wide = up.shape[1], qkv.shape[1]
    own_blocks = None
    if up.shape[0] > rest:

        def own_rows(_, info_ref):
            block = (info_ref[CHIP] * 2 + info_ref[CORE]) * 4 + info_ref[SECTION]
            return (block, 0)

        own_blocks = {6: ((rest, hidden), own_rows), 7: ((rest, wide), own_rows)}
    shapes = [(rest, hidden), (1, rest), (rest, wide), (rest, wide // 3), (1, rest)]
    shapes += [(1, width), (width, 3 * width), (width, width), (1, width)]
    shapes += [(width, column_hidden)] * 2
    (small, small_at), count = sums.small
    handle, came_at = sums.small_sent
    results = call(
        functools.partial(finish_kernel, part=part, small=(small_at, count), came=came_at),
        "finish",
        info,
        (*pieces, small, sums.messages[handle], up, qkv, up_gain[None], qkv_gain[None]),
        [shape_of(dims, F32) for dims in shapes],
        plain=True,
        blocks=own_blocks,
        far_in=(6, 7),
        vmem=12,
    )
    up_grad, up_gain_grad, qkv_grad, out_grad, qkv_gain_grad, *columns = results
    columns[0], columns[3], columns[5] = columns[0][0], columns[3][0], columns[5].T
    return up_grad, up_gain_grad[0], qkv_grad, out_grad, qkv_gain_grad[0], columns


def ordered(arrays, *before):
    count = len(arrays)
    return lax.optimization_barrier((*arrays, *before))[:count]


def step_kernel(info_ref, *refs, inputs, adds, copies, ends, small):
    ins, outs = refs[:inputs], refs[inputs:]

    def value(kept, came, k):
        total = ins[kept[0]][kept[1] + k].astype(F32)
        if came is None:
            return total
        return total + ins[came[0]][came[1] + k].astype(F32)

    for kept, came, count, place, keep, sent in adds:
        for k in range(count):
            total = value(kept, came, k)
            to = ((k >> (place + 1)) << place) | (k & ((1 << place) - 1))
            if (k >> place) & 1:
                outs[sent[0]][sent[1] + to] = total.astype(BF16)
            else:
                outs[keep[0]][keep[1] + to] = total
    for source, count, target in copies:
        for k in range(count):
            outs[target[0]][target[1] + k] = ins[source[0]][source[1] + k]
    for end, sides in ends:
        columns = outs[end].shape[1] // 2
        for side, (kept, came) in enumerate(sides):
            outs[end][:, side * columns : (side + 1) * columns] = value(kept, came, 0)
    for kept, came, count, keep, sent in small:
        for k in range(count):
            if came is not None and len(came) == 4:
                far, first, half, size = came
                at = [pl.ds(first + side * half + k * size, size) for side in range(2)]
                other = jnp.concatenate([ins[far][rows, :] for rows in at], axis=1)
                total = ins[kept[0]][k * size : (k + 1) * size, :] + other.astype(F32)
            else:
                total = value(kept, came, k)
            outs[keep[0]][keep[1] + k] = total
            if sent is not None:
                outs[sent[0]][sent[1] + k] = total.astype(BF16)


class Sums:
    def __init__(self, info, bits, block):
        self.info, self.bits, self.block = info, bits, block
        self.gradients, self.messages, self.held = {}, [], {}
        self.small, self.small_sent, self.small_route = None, None, [*range(bits), "near", "core"]
        self.fresh = None

    def step(
        self, *advance, new=None, far_at=None, small=False, hold=(), before=(), micros=0
    ):
        with_small = small
        arrays, outs, adds, copies, ends = [], [], [], [], []
        sends, kept_count, kept_by, finished, small = {}, 0, [], [], []

        def given(array):
            for k, other in enumerate(arrays):
                if other is array:
                    return k
            arrays.append(array)
            return len(arrays) - 1

        def made(shape):
            outs.append(shape)
            return len(outs) - 1

        def to_send(key, count):
            at = sends.get(key, 0)
            sends[key] = at + count
            return key, at

        def to_keep(count):
            nonlocal kept_count
            kept_count += count
            return kept_count - count

        def there(kept):
            return given(kept[0]), kept[1]

        moving = [self.gradients[name] for name in advance]
        needed = {side["sent"][0] for one in moving for side in one}
        if with_small and self.small_sent is not None:
            needed.add(self.small_sent[0])
        needed = sorted(needed)
        came = ordered([self.messages[at] for at in needed], *before) if needed else ()
        came_at = {at: given(array) for at, array in zip(needed, came)}

        def arrived(sent):
            return None if sent is None else (came_at[sent[0]], sent[1])

        block = self.block
        for name, one in zip(advance, moving):
            if not one[0]["route"]:
                end = made(shape_of((block[0], 2 * block[1]), F32))
                ends.append((end, [(there(s["kept"]), arrived(s["sent"])) for s in one]))
                del self.gradients[name]
                continue
            for side in one:
                key = side["route"].pop(0)
                if key == "far":
                    place, side["below"] = 0, 0
                else:
                    place = len(side["left"]) - 1 - side["left"].index(key) + side["below"]
                    side["left"].remove(key)
                entry = [there(side["kept"]), arrived(side["sent"]), side["count"], place]
                side["count"] //= 2
                side["sent"] = to_send(key, side["count"])
                kept_by.append((side, entry, to_keep(side["count"])))
        sent_sides = [side for side, _, _ in kept_by]
        if new is not None:
            name, (kept, sent) = new
            one, count = [], kept.shape[0] // 2
            for number in range(2):
                order = tuple(range(self.bits))
                order = order if number == 0 else order[::-1]
                route = list(order[1:])
                route.insert(self.bits if far_at is None else far_at - 1, "far")
                side = {
                    "route": route,
                    "below": 1,
                    "left": [bit for bit in range(self.bits - 1, -1, -1) if bit != order[0]],
                    "kept": (kept, number * count),
                    "count": count,
                    "sent": to_send(order[0], count),
                }
                copies.append(((given(sent), number * count), count, side["sent"]))
                one.append(side)
            self.gradients[name] = one
            sent_sides += one
        if with_small:
            kept, count = self.small
            entry = [there(kept), arrived(self.small_sent), count, to_keep(count)]
            if self.fresh is not None:
                far, first = self.fresh
                entry[1] = (given(far), first, kept[0].shape[0], block[0])
                self.fresh = None
            self.small_sent = None
            if self.small_route:
                self.small_sent = to_send(self.small_route.pop(0), count)
            small.append((*entry, self.small_sent))
        keys = sorted(sends, key=str)
        sent_out = {key: made(shape_of((sends[key], *block), BF16)) for key in keys}
        if kept_count:
            kept_out = made(shape_of((kept_count, *block), F32))

        def target(sent):
            return None if sent is None else (sent_out[sent[0]], sent[1])

        adds = [(*entry, (kept_out, at), target(side["sent"])) for side, entry, at in kept_by]
        copies = [(source, count, target(sent)) for source, count, sent in copies]
        small = [(*entry[:3], (kept_out, entry[3]), target(entry[4])) for entry in small]
        results = call(
            functools.partial(
                step_kernel, inputs=len(arrays), adds=adds, copies=copies, ends=ends, small=small
            ),
            "sums_step",
            self.info,
            tuple(arrays),
            outs,
            vmem=12,
            plain=True,
            micros=micros,
        )
        for side, _, at in kept_by:
            side["kept"] = (results[kept_out], at)
        handles = {}
        for key in keys:
            handles[key] = len(self.messages)
            self.messages.append(None)
            self.held[handles[key]] = (key, results[sent_out[key]])
            if key not in hold:
                self.release(handles[key])
        for side in sent_sides:
            side["sent"] = (handles[side["sent"][0]], side["sent"][1])
        if with_small:
            self.small = ((results[kept_out], small[0][3][1]), self.small[1])
            if self.small_sent is not None:
                self.small_sent = (handles[self.small_sent[0]], self.small_sent[1])
        self.sent = [results[sent_out[key]] for key in keys]
        self.handles = handles
        return [results[end] for end, _ in ends]

    def release(self, handle, *before):
        key, array = self.held.pop(handle)
        (array,) = ordered((array,), *before)
        places = {"far": ("section", 2), "near": ("section", 1), "core": ("dp", 1)}
        axis, mask = places[key] if key in places else ("dp", 2 << key)
        self.messages[handle] = exchanged(array, axis, mask)


def quad_kernel(info_ref, *refs, inputs, sides, rest):
    ins, pieces, held = refs[:inputs], refs[inputs:-1], refs[-1]
    columns = held.shape[1] // len(sides)
    for k, (kept, came) in enumerate(sides):
        total = ins[kept[0]][kept[1]] + ins[came[0]][came[1]].astype(F32)
        held[:, k * columns : (k + 1) * columns] = total
    own = info_ref[CORE] * 2 + info_ref[NEAR]
    for mask, piece in enumerate(pieces):
        rows = pl.ds(pl.multiple_of((own ^ mask) * rest, rest), rest)
        piece[...] = held[rows, :].astype(BF16)


def quad_pieces(info, sums, names, rest):
    arrays = []

    def there(place):
        for k, other in enumerate(arrays):
            if other is place[0]:
                return k, place[1]
        arrays.append(place[0])
        return len(arrays) - 1, place[1]

    sides = [
        (there(side["kept"]), there((sums.messages[side["sent"][0]], side["sent"][1])))
        for name in names
        for side in sums.gradients[name]
    ]
    block, columns = sums.block
    return call(
        functools.partial(quad_kernel, inputs=len(arrays), sides=sides, rest=rest),
        "quad_pieces",
        info,
        tuple(arrays),
        [shape_of((rest, columns * len(sides)), BF16)] * 4,
        scratch=[pltpu.VMEM((block, columns * len(sides)), F32)],
        plain=True,
        vmem=8,
    )


TOGETHER = 4


def one_hot(rows, columns, row_of_column):
    row = lax.broadcasted_iota(jnp.int32, (rows, columns), 0)
    column = lax.broadcasted_iota(jnp.int32, (rows, columns), 1)
    return jnp.where(row == row_of_column(column), 1.0, 0.0).astype(BF16)


def head_order(count, small):
    heads, width = HEADS_ATTR, HEADS_ATTR * small

    def row_of(column):
        inside = column % width
        return column - inside + (inside % small) * heads + inside // small

    return one_hot(count, count, row_of)


def column_kernel(
    info_ref,
    cells_ref,
    cotangent,
    gain_ref,
    qkv_ref,
    out_ref,
    mix_gain_ref,
    up_ref,
    down_t_ref,
    mixer_up_hbm,
    mixer_down_hbm,
    *refs,
    width,
    small,
    sections,
):
    results = refs[:3]
    cells_grad_ref, sums_ref, mixer_up_ref, mixer_down_ref = refs[3:7]
    (
        projected,
        normed_low,
        shares_kept,
        score_grads,
        mixed,
        mixed_grad,
        sum_grad,
        turned_grad,
        upstream_all,
        gain_sum,
        mix_gain_sum,
        gain_wide,
        mix_gain_wide,
        qkv_group,
        out_group,
        out_group_t,
        up_group_t,
        down_group,
        qkv_heads,
        mixer_sems,
    ) = refs[7:]
    to_mixer = [
        pltpu.make_async_copy(mixer_up_hbm, mixer_up_ref, mixer_sems.at[0]),
        pltpu.make_async_copy(mixer_down_hbm, mixer_down_ref, mixer_sems.at[1]),
    ]
    lanes = cells_ref.shape[1]
    hidden_width = up_ref.shape[1]
    heads = HEADS_ATTR
    scale = small**-0.5
    lane_blocks = lanes // 128
    group = ATTR // sections
    wide = group * width
    up_at = (slice(0, width), slice(0, hidden_width))
    down_at = (slice(0, width), slice(hidden_width, 2 * hidden_width))
    qkv_at = (slice(width, 2 * width), slice(0, 3 * width))
    out_at = (slice(width, 2 * width), slice(3 * width, 4 * width))
    gain_at = (slice(width, 2 * width), slice(4 * width, 4 * width + 128))

    spread = one_hot(width, wide, lambda column: column % width)

    def diagonal(lanes_tiled):
        tiled = jnp.concatenate([lanes_tiled] * group, axis=0)
        row = lax.broadcasted_iota(jnp.int32, tiled.shape, 0) // lanes_tiled.shape[0]
        column = lax.broadcasted_iota(jnp.int32, tiled.shape, 1) // width
        return jnp.where(row == column, tiled, 0.0)

    triple = head_order(3 * width, small)
    qkv_heads[...] = dot_last(qkv_ref[...], triple).astype(BF16)
    qkv_group[...] = diagonal(dot(dot_last(triple, qkv_ref[...]).astype(BF16), spread)).astype(BF16)
    out_heads = dot(head_order(width, small), out_ref[...]).astype(BF16)
    out_wide = diagonal(dot(out_heads, spread))
    out_group[...] = out_wide.astype(BF16)
    out_group_t[...] = out_wide.T.astype(BF16)
    up_group_t[...] = diagonal(dot_rows(up_ref[...], spread)).astype(BF16)
    down_group[...] = diagonal(dot_rows(down_t_ref[...], spread)).astype(BF16)
    eye = lax.broadcasted_iota(jnp.int32, (width, width), 0) == lax.broadcasted_iota(
        jnp.int32, (width, width), 1
    )
    for ref, kept in ((gain_ref, gain_wide), (mix_gain_ref, mix_gain_wide)):
        column = jnp.sum(jnp.where(eye, ref[...], 0.0), axis=1, keepdims=True)
        kept[...] = jnp.broadcast_to(column, (width, lanes))

    sums_ref[...] = jnp.zeros(sums_ref.shape, F32)
    gain_sum[...] = jnp.zeros_like(gain_sum)
    mix_gain_sum[...] = jnp.zeros_like(mix_gain_sum)

    def at_group(g):
        if isinstance(g, int):
            return slice(g * wide, (g + 1) * wide)
        return pl.ds(pl.multiple_of(g * wide, wide), wide)

    def at_rows(a):
        return pl.ds(pl.multiple_of(a * width, width), width)

    def apart(value):
        return value.reshape(group, width, lanes)

    def each(value):
        size = value.shape[0] // group
        return [value[k * size : (k + 1) * size] for k in range(group)]

    def along(value):
        return jnp.concatenate(each(value), axis=1)

    cells_ref.wait()

    for g in range(sections):
        normed, _ = normal_parts(apart(cells_ref[at_group(g), :].astype(F32)), 1)
        low = (normed * gain_wide[...][None]).astype(BF16).reshape(wide, lanes)
        normed_low[at_group(g), :] = low
        part = dot(qkv_group[...], low).astype(BF16).astype(F32)
        projected[pl.ds(g * group, group)] = part.reshape(group, 3, small, heads, lanes)

    for block in range(lane_blocks):
        here = slice(block * 128, block * 128 + 128)

        @pl.loop(0, ATTR, step=TOGETHER)
        def _(first):
            several = range(TOGETHER)
            queries = [projected[first + k, 0, :, :, here] for k in several]
            scores = [[] for _ in several]
            for b in range(ATTR):
                key = projected[b, 1, :, :, here]
                for k in several:
                    scores[k].append(jnp.sum(queries[k] * key, axis=0) * scale)
            shares = []
            for k in several:
                peak = functools.reduce(jnp.maximum, scores[k])
                lifted = [jnp.exp(score - peak) for score in scores[k]]
                rate = 1.0 / functools.reduce(jnp.add, lifted)
                shares.append([each_one * rate for each_one in lifted])
                for b in range(ATTR):
                    shares_kept[first + k, b, :, here] = shares[k][b]
            totals = [None for _ in several]
            for b in range(ATTR):
                value = projected[b, 2, :, :, here]
                for k in several:
                    term = shares[k][b].astype(BF16).astype(F32)[None] * value
                    totals[k] = term if totals[k] is None else totals[k] + term
            for k in several:
                mixed[at_rows(first + k), here] = totals[k].reshape(width, 128).astype(BF16)

    cotangent.wait()
    for one in to_mixer:
        one.start()

    rows = cotangent.shape[0]
    source = group_row(
        info_ref,
        info_ref[FAR],
        info_ref[NEAR],
        lax.broadcasted_iota(jnp.int32, (1, lanes), 1),
        rows,
    )
    at = lax.broadcasted_iota(jnp.int32, (rows, lanes), 0)
    pick = jnp.where(at == source, 1.0, 0.0).astype(BF16)
    upstream_all[...] = dot_rows(cotangent[...], pick).astype(BF16)

    for piece in range(sections):
        g = info_ref[SECTION] ^ piece
        here = at_group(g)
        mixed_low = mixed[here, :]
        third = cells_ref[here, :].astype(F32) + dot(out_group_t[...], mixed_low)
        third = third.astype(BF16).astype(F32)
        normed, rate = normal_parts(apart(third), 1)
        low = (normed * mix_gain_wide[...][None]).astype(BF16).reshape(wide, lanes)
        hidden, slope = smooth_pair(dot(up_group_t[...], low))
        hidden = hidden.astype(BF16)
        change = jnp.concatenate([dot(down_t_ref[...], each_one) for each_one in each(hidden)], axis=0)
        result = (third + change).astype(BF16)
        results[min(piece, 2)][(piece // 3) * wide : (piece // 3 + 1) * wide, :] = result
        upstream = upstream_all[here, :]
        sums_ref[down_at] += dot_last(along(upstream), along(hidden))
        lifted_grad = (slope * dot(down_group[...], upstream)).astype(BF16)
        sums_ref[up_at] += dot_last(along(low), along(lifted_grad))
        normed_grad = apart(
            jnp.concatenate([dot(up_ref[...], each_one) for each_one in each(lifted_grad)], axis=0)
        )
        mix_gain_sum[...] += jnp.sum(normed_grad * normed, axis=0)
        back = normal_back(normed, rate, normed_grad * mix_gain_wide[...][None], 1)
        third_grad = (upstream.astype(F32) + back.reshape(wide, lanes)).astype(BF16)
        sum_grad[here, :] = third_grad
        sums_ref[out_at] += dot_last(along(third_grad), along(mixed_low))
        part = dot(out_group[...], third_grad).astype(BF16).astype(F32)
        mixed_grad[pl.ds(g * group, group)] = part.reshape(group, small, heads, lanes)

    for block in range(lane_blocks):
        here = slice(block * 128, block * 128 + 128)

        @pl.loop(0, ATTR, step=TOGETHER)
        def _(first):
            several = range(TOGETHER)
            pulled = [mixed_grad[first + k, :, :, here] for k in several]
            share_grads = [[] for _ in several]
            for b in range(ATTR):
                value = projected[b, 2, :, :, here]
                for k in several:
                    share_grads[k].append(jnp.sum(pulled[k] * value, axis=0))
            grads = []
            for k in several:
                shares = [shares_kept[first + k, b, :, here] for b in range(ATTR)]
                products = [s * g for s, g in zip(shares, share_grads[k])]
                centre = functools.reduce(jnp.add, products)
                grads.append([])
                for b in range(ATTR):
                    grad = (products[b] - shares[b] * centre).astype(BF16).astype(F32)
                    score_grads[first + k, b, :, here] = grad
                    shares_kept[first + k, b, :, here] = shares[b].astype(BF16).astype(F32)
                    grads[k].append(grad)
            totals = [None for _ in several]
            for b in range(ATTR):
                key = projected[b, 1, :, :, here]
                for k in several:
                    term = grads[k][b][None] * key
                    totals[k] = term if totals[k] is None else totals[k] + term
            for k in several:
                total = (totals[k] * scale).reshape(width, 128)
                mixed[at_rows(first + k), here] = total.astype(BF16)

        @pl.loop(0, ATTR, step=TOGETHER)
        def _(first):
            several = range(TOGETHER)
            key_grads = [None for _ in several]
            value_grads = [None for _ in several]
            for a in range(ATTR):
                query, pulled = projected[a, 0, :, :, here], mixed_grad[a, :, :, here]
                for k in several:
                    term = score_grads[a, first + k, :, here][None] * query
                    key_grads[k] = term if a == 0 else key_grads[k] + term
                    term = shares_kept[a, first + k, :, here][None] * pulled
                    value_grads[k] = term if a == 0 else value_grads[k] + term
            for k in several:
                projected[first + k, 1, :, :, here] = key_grads[k] * scale
                projected[first + k, 2, :, :, here] = value_grads[k]

    for g in range(sections):
        here = at_group(g)
        query_grads = each(mixed[here, :])
        grads = []
        for k in range(group):
            key_value = projected[g * group + k, 1:3].reshape(2 * width, lanes).astype(BF16)
            grads.append(jnp.concatenate([query_grads[k], key_value], axis=0))
        sums_ref[qkv_at] += dot_last(
            along(normed_low[here, :]), jnp.concatenate(grads, axis=1)
        )
        normed_grad = jnp.concatenate([dot(qkv_heads[...], grad) for grad in grads], axis=0)
        normed_grad = apart(normed_grad)
        normed, rate = normal_parts(apart(cells_ref[here, :].astype(F32)), 1)
        gain_sum[...] += jnp.sum(normed_grad * normed, axis=0)
        back = normal_back(normed, rate, normed_grad * gain_wide[...][None], 1)
        turned_grad[here, :] = sum_grad[here, :].astype(F32) + back.reshape(wide, lanes)

    cells_grad_ref[...] = turned_grad[...].T.astype(BF16)
    lane = lax.broadcasted_iota(jnp.int32, (width, 128), 1)
    first = jnp.sum(gain_sum[...], axis=1, keepdims=True)
    second = jnp.sum(mix_gain_sum[...], axis=1, keepdims=True)
    sums_ref[gain_at] = jnp.where(
        lane == 0, first, jnp.where(lane == 1, second, 0.0)
    )
    rows = sums_ref.shape[0]
    for half in range(2):
        at = 2 * wide + half * rows
        part = sums_ref[:, half * hidden_width : (half + 1) * hidden_width]
        results[2][at : at + rows, :] = part.astype(BF16)
    for one in to_mixer:
        one.wait()


def column_layers(
    info, cells, cotangent, gain, qkv, out, mix_gain, up, down, mixer_up, mixer_down, sections
):
    depth, lanes = cells.shape
    width = depth // ATTR
    small = width // HEADS_ATTR
    hidden = up.shape[1]
    wide = width * (ATTR // sections)
    piece = depth // sections
    out_shape = [
        shape_of((piece, lanes), BF16),
        shape_of((piece, lanes), BF16),
        shape_of((2 * piece + 4 * width, lanes), BF16),
        shape_of((lanes, depth), BF16),
        shape_of((2 * width, 2 * hidden), F32),
        shape_of(mixer_up.shape, BF16),
        shape_of(mixer_down.shape, BF16),
    ]
    arrays = (
        cells, cotangent, gain[None], qkv, out, mix_gain[None], up, down.T, mixer_up, mixer_down
    )
    results = call(
        functools.partial(column_kernel, width=width, small=small, sections=sections),
        "column_layers",
        info,
        arrays,
        out_shape,
        scratch=[
            pltpu.VMEM((ATTR, 3, small, HEADS_ATTR, lanes), F32),
            pltpu.VMEM((depth, lanes), BF16),
            pltpu.VMEM((ATTR, ATTR, HEADS_ATTR, lanes), F32),
            pltpu.VMEM((ATTR, ATTR, HEADS_ATTR, lanes), F32),
            pltpu.VMEM((depth, lanes), BF16),
            pltpu.VMEM((ATTR, small, HEADS_ATTR, lanes), F32),
            pltpu.VMEM((depth, lanes), BF16),
            pltpu.VMEM((depth, lanes), F32),
            pltpu.VMEM((depth, lanes), BF16),
            pltpu.VMEM((width, lanes), F32),
            pltpu.VMEM((width, lanes), F32),
            pltpu.VMEM((width, lanes), F32),
            pltpu.VMEM((width, lanes), F32),
            pltpu.VMEM((3 * wide, wide), BF16),
            pltpu.VMEM((wide, wide), BF16),
            pltpu.VMEM((wide, wide), BF16),
            pltpu.VMEM((hidden * wide // width, wide), BF16),
            pltpu.VMEM((hidden * wide // width, wide), BF16),
            pltpu.VMEM((width, 3 * width), BF16),
            pltpu.SemaphoreType.DMA((2,)),
        ],
        vmem=26,
        raw=(8, 9),
        near_out=(5, 6),
        far_in=(0, 1),
        micros=24,
    )
    return results[:3], *results[3:]


def column_finish(sums, refs):
    gain_ref, qkv_ref, out_ref, mix_gain_ref, up_ref, down_t_ref = refs
    width, hidden = up_ref.shape
    small = width // HEADS_ATTR
    up_ref[...] = sums[:width, :hidden]
    down_t_ref[...] = sums[:width, hidden : 2 * hidden]
    low = sums[width : 2 * width]
    qkv_ref[...] = jnp.dot(
        low[:, : 3 * width],
        head_order(3 * width, small).astype(F32),
        precision=lax.Precision.HIGHEST,
        preferred_element_type=F32,
    )
    out_ref[...] = lax.dot_general(
        head_order(width, small).astype(F32),
        low[:, 3 * width : 4 * width],
        (((0,), (1,)), ((), ())),
        precision=lax.Precision.HIGHEST,
        preferred_element_type=F32,
    )
    eye = lax.broadcasted_iota(jnp.int32, (width, width), 0) == lax.broadcasted_iota(
        jnp.int32, (width, width), 1
    )
    for k, ref in enumerate((gain_ref, mix_gain_ref)):
        at = 4 * width + k
        ref[...] = jnp.sum(jnp.where(eye, low[:, at : at + 1], 0.0), axis=0, keepdims=True)


def body(
    features,
    cotangent,
    row_counts,
    key_valid,
    attend_gain,
    attend_qkv,
    attend_out,
    mixer_gain,
    mixer_up,
    mixer_down,
    column_gain,
    column_qkv,
    column_out,
    column_mix_gain,
    column_up,
    column_down,
):
    dp_count, sections = lax.axis_size("dp"), lax.axis_size("section")
    dp_at, section_at = lax.axis_index("dp"), lax.axis_index("section")
    core, near, far = dp_at & 1, section_at & 1, section_at >> 1
    bits = (dp_count // 2).bit_length() - 1
    blocks = dp_count * sections
    group_rows, width = features.shape
    hidden = mixer_up.shape[1]
    entries = (core, near, far, dp_at >> 1, section_at)
    lane = lax.iota(jnp.int32, COUNTS)
    place = sum(jnp.where(lane == k, entry.astype(jnp.int32), 0) for k, entry in enumerate(entries))
    info = jnp.concatenate([place, row_counts[0]])

    def near_of(array):
        return exchanged(array, "section", 1)

    def core_of(array):
        return exchanged(array, "dp", 1)

    own_x, half_normed, projected, mask, shared, first, slope, second_t = attend(
        info, features, key_valid[None], attend_gain[None], attend_qkv, attend_out,
        mixer_gain[None], mixer_up, mixer_down,
    )
    shared_near, shared_core = near_of(shared), core_of(shared)
    half_core = core_of(half_normed)

    result_pieces, second_grad, column_sums, near_up, near_down = column_layers(
        info, second_t, cotangent, column_gain, column_qkv, column_out, column_mix_gain,
        column_up, column_down, mixer_up, mixer_down, sections,
    )
    shared_near, shared_core, half_core = ordered(
        (shared_near, shared_core, half_core), second_grad
    )
    grad_near, grad_core = near_of(second_grad), core_of(second_grad)
    shared_both = core_of(shared_near)

    first_grad = mixer_back(
        info, second_grad, slope, first, mixer_gain[None], near_up, near_down
    )
    first_near = near_of(first_grad)

    pool = ordered((shared, shared_near, shared_core, shared_both), first_grad)
    pool_hidden, pool_slope = pool_forward(info, pool, mixer_up, blocks)
    (grad_core,) = ordered((grad_core,), pool_hidden)
    (grad_near,) = ordered((grad_near,), pool_hidden)
    second_pool = (second_grad, grad_near, grad_core, core_of(grad_near))
    down_parts = down_gradient(info, pool_hidden, second_pool, blocks, bits)
    result_far = exchanged(result_pieces[2], "section", 2)
    sums = Sums(info, bits, down_parts[0].shape[1:])
    sums.step(new=("down", down_parts), far_at=1)
    (slope_later,) = ordered((pool_slope,), *sums.sent)
    up_parts = up_gradient(info, slope_later, pool, second_pool, mixer_down, blocks, bits)
    quarter = width // sections
    sums.small = (column_sums, 0), column_sums.shape[0] // sums.block[0]
    sums.fresh = result_far, 2 * quarter

    sums.step("down", new=("up", up_parts), small=True, hold=("far",))
    down_far = sums.handles["far"]
    first_near, own_grad = ordered((first_near, first_grad), *sums.sent)
    near_pieces = ordered((result_pieces[1], result_far[quarter : 2 * quarter]), *sums.sent)
    result_near = near_of(jnp.concatenate(near_pieces, axis=0))
    kept, sent, e_own, e_sent = attend_back(
        info, projected, mask, own_grad, first_near, attend_out, attend_qkv
    )
    sent_came = core_of(sent)
    sums.release(down_far, kept)
    sums.step("up", small=True, before=(result_near,), micros=40)
    settled = sums.sent
    (sent_came,) = ordered((sent_came,), *settled)
    attend_parts = attend_gradient(
        info, (half_normed, half_core), pool, (kept, sent_came), blocks, bits
    )
    (e_sent,) = ordered((e_sent,), *settled)
    e_near = near_of(e_sent)
    sums.step(new=("attend", attend_parts))
    for _ in range(bits - 1):
        sums.step("up", small=True, before=sums.sent)
    (e_near,) = ordered((e_near,), sums.messages[down_far], *sums.sent)
    input_pieces = last_norm(
        info, e_own, e_near, first_grad, own_x, attend_gain[None], sections
    )
    far_came = exchanged(input_pieces[2], "section", 2)
    for _ in range(bits - 1):
        sums.step("down", "attend", before=input_pieces[:1])
    up_far = sums.messages[sums.gradients["up"][0]["sent"][0]]
    (result_near,) = ordered((result_near,), *sums.sent)
    pieces = [result_pieces[0], result_near[:quarter], result_far[:quarter], result_near[quarter:]]
    result = placed(info, pieces, features.dtype, True, 20)
    (mixer_down_grad,) = sums.step("down", "attend", small=True, before=(result, up_far))
    (far_came,) = ordered((far_came,), *sums.sent)
    own = far_came.shape[0] // 2
    near_came = near_of(jnp.concatenate([input_pieces[1], far_came[own:]], axis=0))

    rest = width // blocks
    pieces = quad_pieces(info, sums, ("up", "attend"), rest)
    (near_came,) = ordered((near_came,), pieces[0])
    input_grad = placed(
        info,
        [input_pieces[0], near_came[:own], far_came[:own], near_came[own:]],
        F32,
        False,
        20,
    )
    moves = [(at, at ^ (sections + 1)) for at in range(blocks)]
    pieces = (
        pieces[0],
        exchanged(pieces[1], "section", 1),
        exchanged(pieces[2], "dp", 1),
        lax.ppermute(pieces[3], ("dp", "section"), moves),
    )

    own_block = dp_at * sections + section_at
    (own_block,) = ordered((own_block,), *sums.sent)

    def own_rows(array):
        return lax.dynamic_slice_in_dim(array, own_block * rest, rest, 0)

    (
        mixer_up_grad, mixer_gain_grad, attend_qkv_grad, attend_out_grad, attend_gain_grad,
        column_grads,
    ) = finish(
        info,
        pieces,
        sums,
        mixer_up if rest % 16 == 0 else own_rows(mixer_up),
        attend_qkv if rest % 16 == 0 else own_rows(attend_qkv),
        own_rows(mixer_gain),
        own_rows(attend_gain),
        hidden // blocks,
        column_gain.shape[0],
        column_up.shape[1],
    )

    return (
        result,
        input_grad,
        attend_gain_grad,
        attend_qkv_grad,
        attend_out_grad,
        mixer_gain_grad,
        mixer_up_grad,
        mixer_down_grad,
        *column_grads,
    )


def solution(mesh):
    split = P(("dp", "section"))
    return jax.shard_map(
        body,
        mesh=mesh,
        in_specs=(P("dp", None), P("dp", None), P("dp", None), P("dp")) + (P(),) * 12,
        out_specs=(P("dp", "section"),) * 2 + (split,) * 6 + (P(),) * 6,
        check_vma=False,
    )
```
